32 devices in a mesh: node: 4 (over z), dev: 8 (over y, x, core).
Axes of the slice: x: 2, y: 2, z: 4, core: 2. Of those that a mesh axis runs over, the one named last changes fastest.
Arguments:
- image: bfloat16 [128, 14, 14, 512], P(('node', 'dev')), may hold values from -30 to 30
- crop_sides: int32 [128], P(('node', 'dev')), may hold values from 6 to 14, as said below
- proj_in: bfloat16 [512, 512], replicated, may hold values from -0.25 to 0.25
- kernel_large: bfloat16 [31, 31, 512], replicated, may hold values from -0.1875 to 0.1875
- kernel_small: bfloat16 [5, 5, 512], replicated, may hold values from -1.25 to 1.25
- proj_out: bfloat16 [512, 512], replicated, may hold values from -0.25 to 0.25
- proj_up: bfloat16 [512, 2048], replicated, may hold values from -0.25 to 0.25
- proj_down: bfloat16 [2048, 512], replicated, may hold values from -0.125 to 0.125
- norm_gain: float32 [7, 512], replicated, may hold values from 0.5 to 1.5
- norm_shift: float32 [7, 512], replicated, may hold values from -2 to 2
- wide_gain: float32 [2048], replicated, may hold values from 0.5 to 1.5
- wide_shift: float32 [2048], replicated, may hold values from -2 to 2
- cotangent: bfloat16 [128, 14, 14, 512], P(('node', 'dev')), may hold values from -6 to 6
Outputs:
- block_out: bfloat16 [128, 14, 14, 512], P(('node', 'dev'))
- grad_image: float32 [128, 14, 14, 512], P(('node', 'dev'))
- grad_proj_in: float32 [512, 512], replicated
- grad_kernel_large: float32 [31, 31, 512], replicated
- grad_kernel_small: float32 [5, 5, 512], replicated
- grad_proj_out: float32 [512, 512], replicated
- grad_proj_up: float32 [512, 2048], replicated
- grad_proj_down: float32 [2048, 512], replicated
- grad_norm_gain: float32 [7, 512], replicated
- grad_norm_shift: float32 [7, 512], replicated
- grad_wide_gain: float32 [2048], replicated
- grad_wide_shift: float32 [2048], replicated
The draws below stay inside these ranges and needn't reach their ends.
Inputs may be any that keep to these rules, and one draw needn't show every extreme that they name: `crop_sides`: each crop's side is 6 or 14 cells; its map fills the top left corner of its 14 x 14 canvas, the other cells are padding.
All inputs are finite; a program needn't handle non-finite values.
Results may differ from the reference program's by a relative error of at most 0.012.
Values sent between devices are 32-bit elements; how exact they have to be, the bound alone decides.
No kernel may reach another device: no remote copies, remote signals or barrier semaphores. Data moves between devices by JAX's collectives and lax.ppermute only.
A program may use at most 192 MiB of HBM per device.

```python
import math
import jax
import jax.numpy as jnp
import numpy as np
from jax import lax

C = 512
FF = 2048
K_LARGE = 31
K_SMALL = 5
CANVAS = 14
CROPS = 128


def draw_crop_sides(key, part):
    key = jax.random.fold_in(key, 11)
    pick_draw = jax.random.randint(key, (CROPS,), 0, 4)
    side_cells = jnp.where(pick_draw == 0, CANVAS, 6).astype(jnp.int32)
    side_cells = side_cells.at[0].set(CANVAS)
    side_cells = side_cells.at[1].set(6)
    return side_cells


def draw_image(key, part):
    key = jax.random.fold_in(key, 23)
    subkeys = jax.random.split(key, 3)
    crop_ramp = 1.0 + 0.75 * jnp.arange(CROPS, dtype=jnp.float32) / (CROPS - 1)
    crop_ramp = crop_ramp[:, None, None, None]
    channel = jnp.exp(jax.random.uniform(subkeys[1], (C,), jnp.float32, -math.log(2.0), math.log(2.0)))
    offset = 0.5 * jax.random.normal(subkeys[2], (C,), jnp.float32)
    noise = jax.random.normal(subkeys[0], (CROPS, CANVAS, CANVAS, C), jnp.float32)
    return (crop_ramp * (noise * channel + offset)).astype(jnp.bfloat16)


def block_scale(key, dims, shards, low, high):
    factor_of = 1.0
    for axis_at, blocks in shards:
        heights = jax.random.uniform(jax.random.fold_in(jax.random.fold_in(key, 6), axis_at), (blocks,), jnp.float32, low / len(shards), high / len(shards))
        factor_of = factor_of * jnp.repeat(jnp.exp(heights), dims[axis_at] // blocks).reshape((-1,) + (1,) * (len(dims) - 1 - axis_at))
    return factor_of


def normal_values(rng, shape, deviation, most, cuts=(), kind=jnp.bfloat16):
    level = block_scale(rng, shape, cuts, -0.22, 0.18) if cuts else 1.0
    array = jax.random.normal(rng, shape, jnp.float32) * deviation * level
    return jnp.minimum(jnp.maximum(array, -most), most).astype(kind)


def setup_inputs(seed: int = 0) -> dict:
    seeds = jax.random.split(jax.random.key(seed), 14)
    image = draw_image(jax.random.fold_in(seeds[13], 71), 0)
    crop_sides = draw_crop_sides(jax.random.fold_in(seeds[13], 71), 0)
    proj_in = normal_values(seeds[2], (C, C), C ** -0.5, 0.25)
    kernel_large = normal_values(seeds[3], (K_LARGE, K_LARGE, C), (K_LARGE * K_LARGE) ** -0.5, 0.1875)
    kernel_small = normal_values(seeds[4], (K_SMALL, K_SMALL, C), (K_SMALL * K_SMALL) ** -0.5, 1.25)
    proj_out = normal_values(seeds[5], (C, C), C ** -0.5, 0.25)
    proj_up = normal_values(seeds[6], (C, FF), C ** -0.5, 0.25)
    proj_down = normal_values(seeds[7], (FF, C), FF ** -0.5, 0.125)
    norm_gain = jnp.clip(1.0 + 0.1 * jax.random.normal(seeds[8], (7, C), jnp.float32), 0.5, 1.5)
    norm_shift = normal_values(seeds[9], (7, C), 0.3, 2.0, (), jnp.float32)
    wide_gain = jnp.clip(1.0 + 0.1 * jax.random.normal(seeds[10], (FF,), jnp.float32), 0.5, 1.5)
    wide_shift = normal_values(seeds[11], (FF,), 0.3, 2.0, (), jnp.float32)
    cotangent = normal_values(seeds[12], (CROPS, CANVAS, CANVAS, C), 1.0, 6.0, ((0, 32),))
    return dict(image=image, crop_sides=crop_sides, proj_in=proj_in, kernel_large=kernel_large, kernel_small=kernel_small, proj_out=proj_out, proj_up=proj_up, proj_down=proj_down, norm_gain=norm_gain, norm_shift=norm_shift, wide_gain=wide_gain, wide_shift=wide_shift, cotangent=cotangent)


EPSILON = 1e-05

@jax.custom_vjp
def low(v):
    return lax.optimization_barrier(v.astype(jnp.bfloat16)).astype(jnp.float32)

@jax.custom_vjp
def low_back(v):
    return v

def low_keep(v):
    return (low(v), None)

def low_pass(kept, grad):
    return (grad,)

def back_keep(v):
    return (v, None)

def back_low(kept, grad):
    return (low(grad),)
low.defvjp(low_keep, low_pass)
low_back.defvjp(back_keep, back_low)

def canvas_mask(crop_sides):
    places = jnp.arange(CANVAS, dtype=jnp.int32)
    inside_rows = places[None, :, None] < crop_sides[:, None, None]
    inside_cols = places[None, None, :] < crop_sides[:, None, None]
    return jnp.logical_and(inside_rows, inside_cols).astype(jnp.float32)[..., None]

def batch_norm(values, valid_mask, pixel_count, scaling, offsets):
    column_mean = lax.optimization_barrier(jnp.sum(valid_mask * values, axis=(0, 1, 2))) / pixel_count
    spread = lax.optimization_barrier(jnp.sum(valid_mask * values * values, axis=(0, 1, 2))) / pixel_count - column_mean * column_mean
    return ((values - column_mean) * lax.rsqrt(spread + EPSILON) * scaling + offsets) * valid_mask

def pointwise(values, weight):
    flattened = values.reshape(-1, values.shape[-1])
    result = jnp.dot(flattened, weight, precision=lax.Precision.HIGHEST, preferred_element_type=jnp.float32)
    return result.reshape(values.shape[:-1] + (weight.shape[1],))

def banded(kernel):
    side = kernel.shape[0]
    half = (side - 1) // 2
    places = np.arange(CANVAS)
    offsets = places[:, None] - places[None, :]
    inside = (np.abs(offsets) <= half).astype(np.float32)
    taps = np.clip(offsets + half, 0, side - 1).astype(np.int32)
    entries = kernel[taps[:, :, None, None], taps[None, None, :, :]]
    weights = jnp.asarray(inside[:, :, None, None] * inside[None, None, :, :], dtype=kernel.dtype)
    entries = entries * weights[..., None]
    entries = jnp.transpose(entries, (0, 2, 1, 3, 4))
    return entries.reshape(CANVAS * CANVAS, CANVAS * CANVAS, kernel.shape[-1])

def depthwise(values, kernel):
    matrix = banded(kernel)
    flattened = values.reshape(values.shape[0], CANVAS * CANVAS, values.shape[-1])
    result = jnp.einsum('nic,ioc->noc', flattened, matrix, precision=lax.Precision.HIGHEST)
    return result.reshape(values.shape)

def reference(image, crop_sides, proj_in, kernel_large, kernel_small, proj_out, proj_up, proj_down, norm_gain, norm_shift, wide_gain, wide_shift, cotangent):
    valid_mask = canvas_mask(crop_sides)
    pixel_count = jnp.sum(valid_mask)

    def forward(picture, inward, larger, smaller, outward, upward, downward, gains, shifts, wide_gains, wide_shifts):

        def normalize(values, index):
            return batch_norm(values, valid_mask, pixel_count, gains[index], shifts[index])
        resid_in = picture * valid_mask
        pre_out = normalize(resid_in, 0)
        proj_pre = low_back(pointwise(low(pre_out), inward))
        mixer_in = low(jax.nn.gelu(normalize(proj_pre, 1)))
        large_conv = low_back(depthwise(mixer_in, larger))
        small_conv = low_back(depthwise(mixer_in, smaller))
        merged = jax.nn.gelu(normalize(large_conv, 2) + normalize(small_conv, 3))
        proj_back = low_back(pointwise(low(merged), outward))
        resid_mid = resid_in + normalize(proj_back, 4)
        hidden_pre = low_back(pointwise(low(normalize(resid_mid, 5)), upward))
        hidden_act = jax.nn.gelu(batch_norm(hidden_pre, valid_mask, pixel_count, wide_gains, wide_shifts))
        ffn_proj = low_back(pointwise(low(hidden_act), downward))
        return resid_mid + normalize(ffn_proj, 6)
    block_out, pullback = jax.vjp(forward, image.astype(jnp.float32), proj_in.astype(jnp.float32), kernel_large.astype(jnp.float32), kernel_small.astype(jnp.float32), proj_out.astype(jnp.float32), proj_up.astype(jnp.float32), proj_down.astype(jnp.float32), norm_gain, norm_shift, wide_gain, wide_shift)
    gradients = pullback(cotangent.astype(jnp.float32))
    return (block_out.astype(jnp.bfloat16), gradients[0], gradients[1], gradients[2], gradients[3], gradients[4], gradients[5], gradients[6], gradients[7], gradients[8], gradients[9], gradients[10])
```

```python
import jax
import jax.numpy as jnp
import numpy as np
from jax import lax
from jax.sharding import PartitionSpec as P

EPSILON = 1e-05


def canvas_mask(crop_sides, canvas):
    places = jnp.arange(canvas, dtype=jnp.int32)
    inside_rows = places[None, :, None] < crop_sides[:, None, None]
    inside_cols = places[None, None, :] < crop_sides[:, None, None]
    return jnp.logical_and(inside_rows, inside_cols).astype(jnp.float32)[..., None]


def pointwise(values, weight):
    flattened = values.reshape(-1, values.shape[-1])
    result = jnp.dot(flattened, weight, preferred_element_type=jnp.float32)
    return result.reshape(values.shape[:-1] + (weight.shape[1],))


def transposed(gradient, weight):
    flattened = gradient.reshape(-1, gradient.shape[-1])
    result = lax.dot_general(
        flattened, weight, (((1,), (1,)), ((), ())), preferred_element_type=jnp.float32
    )
    return result.reshape(gradient.shape[:-1] + (weight.shape[0],))


def weight_grad(inputs, gradient):
    flat_inputs = inputs.reshape(-1, inputs.shape[-1])
    flat_grads = gradient.reshape(-1, gradient.shape[-1])
    return lax.dot_general(
        flat_inputs, flat_grads, (((0,), (0,)), ((), ())), preferred_element_type=jnp.float32
    )


def wave_tables(canvas):
    period = 2 * canvas - 1
    pairs = [(0, v) for v in range(canvas)]
    pairs += [(u, v) for u in range(1, canvas) for v in range(period)]
    waves = np.array(pairs)

    def tables(places):
        grid = np.stack(np.meshgrid(places, places, indexing="ij"), -1).reshape(-1, 2)
        angle = 2 * np.pi * ((waves @ grid.T) % period) / period
        return np.cos(angle).astype(np.float32), np.sin(angle).astype(np.float32)

    share = np.full((len(pairs), 1), 2.0 / period**2, np.float32)
    share[0] = 1.0 / period**2
    return tables, share


def spread(table, values):
    return lax.dot_general(
        table, values, (((1,), (0,)), ((), ())), precision=lax.Precision.HIGH, preferred_element_type=jnp.float32
    )


def gather_back(table, values):
    return lax.dot_general(
        table, values, (((0,), (0,)), ((), ())), precision=lax.Precision.HIGH, preferred_element_type=jnp.float32
    )


def to_waves(values):
    count, canvas, _, channels = values.shape
    tables, _ = wave_tables(canvas)
    cosines, sines = tables(np.arange(canvas))
    flat = values.astype(jnp.float32).reshape(count, canvas * canvas, channels)
    flat = flat.transpose(1, 0, 2).reshape(canvas * canvas, count * channels)
    real = spread(cosines, flat).reshape(-1, count, channels)
    imag = -spread(sines, flat).reshape(-1, count, channels)
    return real, imag


def from_waves(real, imag, canvas):
    waves, count, channels = real.shape
    tables, share = wave_tables(canvas)
    cosines, sines = tables(np.arange(canvas))
    flat = gather_back(cosines * share, real.reshape(waves, -1))
    flat = flat - gather_back(sines * share, imag.reshape(waves, -1))
    return flat.reshape(canvas, canvas, count, channels).transpose(2, 0, 1, 3)


def kernel_waves(kernel, canvas):
    side = kernel.shape[0]
    reach = min((side - 1) // 2, canvas - 1)
    middle = (side - 1) // 2
    tables, _ = wave_tables(canvas)
    cosines, sines = tables(np.arange(-reach, reach + 1))
    used = kernel[middle - reach : middle + reach + 1, middle - reach : middle + reach + 1]
    flat = used.astype(jnp.float32).reshape(-1, kernel.shape[2])
    return spread(cosines, flat)[:, None], spread(sines, flat)[:, None]


def kernel_grad(value_waves, grad_waves, side, canvas):
    reach = min((side - 1) // 2, canvas - 1)
    tables, share = wave_tables(canvas)
    cosines, sines = tables(np.arange(-reach, reach + 1))
    real = jnp.sum(value_waves[0] * grad_waves[0] + value_waves[1] * grad_waves[1], axis=1)
    imag = jnp.sum(value_waves[1] * grad_waves[0] - value_waves[0] * grad_waves[1], axis=1)
    flat = gather_back(cosines * share, real) - gather_back(sines * share, imag)
    taps = 2 * reach + 1
    rim = (side - taps) // 2
    return jnp.pad(flat.reshape(taps, taps, -1), ((rim, rim), (rim, rim), (0, 0)))


def times(left, right):
    return (left[0] * right[0] - left[1] * right[1], left[0] * right[1] + left[1] * right[0])


def times_conj(left, right):
    return (left[0] * right[0] + left[1] * right[1], left[0] * right[1] - left[1] * right[0])


AXES = ("node", "dev")


def total(parts):
    sizes = [part.size for part in parts]
    flat = jnp.concatenate([part.reshape(-1) for part in parts])
    flat = jnp.pad(flat, (0, -flat.shape[0] % 1024)).reshape(-1, 128)
    devices = lax.axis_size(AXES)
    copies = jnp.broadcast_to(flat[None], (devices,) + flat.shape)
    flat = jnp.sum(lax.all_to_all(copies, AXES, 0, 0, tiled=True), axis=0).reshape(-1)
    results = []
    offset = 0
    for part, size in zip(parts, sizes):
        results.append(flat[offset : offset + size].reshape(part.shape))
        offset += size
    return results


def moments(values, valid_mask):
    masked = valid_mask * values
    return (
        jnp.sum(valid_mask),
        jnp.sum(masked, axis=(0, 1, 2)),
        jnp.sum(masked * values, axis=(0, 1, 2)),
    )


def finish(values, valid_mask, pixel_count, column_sum, square, scaling, offsets):
    column_mean = column_sum / pixel_count
    spread = square / pixel_count - column_mean * column_mean
    reciprocal = lax.rsqrt(spread + EPSILON)
    normed = (values - column_mean) * reciprocal
    return ((normed * scaling + offsets) * valid_mask, (normed, reciprocal, pixel_count))


def norm_forward(values, valid_mask, scaling, offsets):
    pixel_count, column_sum, square = moments(values, valid_mask)
    pixel_count, column_sum, square = total((pixel_count, column_sum, square))
    return finish(values, valid_mask, pixel_count, column_sum, square, scaling, offsets)


def grad_moments(gradient, valid_mask, saved):
    masked = gradient * valid_mask
    return (masked, jnp.sum(masked, axis=(0, 1, 2)), jnp.sum(masked * saved[0], axis=(0, 1, 2)))


def grad_finish(masked, valid_mask, saved, scaling, shift_sum, gain_sum):
    normed, reciprocal, pixel_count = saved
    return (
        valid_mask
        * scaling
        * reciprocal
        * (masked - shift_sum / pixel_count - normed * gain_sum / pixel_count)
    )


def norm_backward(gradient, valid_mask, saved, scaling):
    masked, shift_sum, gain_sum = grad_moments(gradient, valid_mask, saved)
    shift_sum, gain_sum = total((shift_sum, gain_sum))
    return (
        grad_finish(masked, valid_mask, saved, scaling, shift_sum, gain_sum),
        gain_sum,
        shift_sum,
    )


def settle_joined(gradients):
    return lax.psum(gradients, AXES)


def gelu_back(values, gradient):
    unused, gelu_pull = jax.vjp(jax.nn.gelu, values)
    return gelu_pull(gradient)[0]


def local(
    image,
    crop_sides,
    proj_in,
    kernel_large,
    kernel_small,
    proj_out,
    proj_up,
    proj_down,
    norm_gain,
    norm_shift,
    wide_gain,
    wide_shift,
    cotangent,
):
    valid_mask = canvas_mask(crop_sides, image.shape[1])
    resid_in = image.astype(jnp.float32) * valid_mask
    pre_out, pre_saved = norm_forward(resid_in, valid_mask, norm_gain[0], norm_shift[0])
    pre_low = pre_out.astype(jnp.bfloat16)
    proj_pre = pointwise(pre_low, proj_in)
    mid_norm, mid_saved = norm_forward(proj_pre, valid_mask, norm_gain[1], norm_shift[1])
    mixer_low = jax.nn.gelu(mid_norm).astype(jnp.bfloat16)
    canvas = image.shape[1]
    mixer_waves = to_waves(mixer_low)
    large_waves = kernel_waves(kernel_large, canvas)
    small_waves = kernel_waves(kernel_small, canvas)
    large_conv = from_waves(*times(large_waves, mixer_waves), canvas)
    small_conv = from_waves(*times(small_waves, mixer_waves), canvas)
    large_norm, large_saved = norm_forward(large_conv, valid_mask, norm_gain[2], norm_shift[2])
    small_norm, small_saved = norm_forward(small_conv, valid_mask, norm_gain[3], norm_shift[3])
    merged = large_norm + small_norm
    merged_low = jax.nn.gelu(merged).astype(jnp.bfloat16)
    proj_back = pointwise(merged_low, proj_out)
    back_norm, back_saved = norm_forward(proj_back, valid_mask, norm_gain[4], norm_shift[4])
    resid_mid = resid_in + back_norm
    ffn_norm, ffn_saved = norm_forward(resid_mid, valid_mask, norm_gain[5], norm_shift[5])
    ffn_low = ffn_norm.astype(jnp.bfloat16)
    hidden_pre = pointwise(ffn_low, proj_up)
    hidden_norm, hidden_saved = norm_forward(hidden_pre, valid_mask, wide_gain, wide_shift)
    hidden_low = jax.nn.gelu(hidden_norm).astype(jnp.bfloat16)
    ffn_proj = pointwise(hidden_low, proj_down)
    ffn_out, out_saved = norm_forward(ffn_proj, valid_mask, norm_gain[6], norm_shift[6])
    block_out = (resid_mid + ffn_out).astype(jnp.bfloat16)
    upstream = cotangent.astype(jnp.float32)
    down_grad, gain_last, shift_last = norm_backward(upstream, valid_mask, out_saved, norm_gain[6])
    down_low = down_grad.astype(jnp.bfloat16)
    grad_down = weight_grad(hidden_low, down_low)
    hidden_grad = gelu_back(hidden_norm, transposed(down_low, proj_down))
    up_grad, gain_wide, shift_wide = norm_backward(hidden_grad, valid_mask, hidden_saved, wide_gain)
    up_low = up_grad.astype(jnp.bfloat16)
    grad_up = weight_grad(ffn_low, up_low)
    ffn_grad, gain_ffn, shift_ffn = norm_backward(
        transposed(up_low, proj_up), valid_mask, ffn_saved, norm_gain[5]
    )
    resid_grad = upstream + ffn_grad
    back_grad, gain_back, shift_back = norm_backward(
        resid_grad, valid_mask, back_saved, norm_gain[4]
    )
    back_low = back_grad.astype(jnp.bfloat16)
    grad_out = weight_grad(merged_low, back_low)
    merged_grad = gelu_back(merged, transposed(back_low, proj_out))
    large_grad, gain_large, shift_large = norm_backward(
        merged_grad, valid_mask, large_saved, norm_gain[2]
    )
    small_grad, gain_small, shift_small = norm_backward(
        merged_grad, valid_mask, small_saved, norm_gain[3]
    )
    large_low = large_grad.astype(jnp.bfloat16)
    small_low = small_grad.astype(jnp.bfloat16)
    large_grad_waves = to_waves(large_low)
    small_grad_waves = to_waves(small_low)
    grad_large = kernel_grad(mixer_waves, large_grad_waves, kernel_large.shape[0], canvas)
    grad_small = kernel_grad(mixer_waves, small_grad_waves, kernel_small.shape[0], canvas)
    back_large = times_conj(large_waves, large_grad_waves)
    back_small = times_conj(small_waves, small_grad_waves)
    mixer_back = from_waves(back_large[0] + back_small[0], back_large[1] + back_small[1], canvas)
    mid_grad = gelu_back(mid_norm, mixer_back)
    pre_grad, gain_mid, shift_mid = norm_backward(mid_grad, valid_mask, mid_saved, norm_gain[1])
    pre_round = pre_grad.astype(jnp.bfloat16)
    grad_in = weight_grad(pre_low, pre_round)
    first_grad, gain_first, shift_first = norm_backward(
        transposed(pre_round, proj_in), valid_mask, pre_saved, norm_gain[0]
    )
    grad_image = (resid_grad + first_grad) * valid_mask
    grad_in, grad_large, grad_small, grad_out, grad_up, grad_down = settle_joined(
        [grad_in, grad_large, grad_small, grad_out, grad_up, grad_down]
    )
    gain_grads = jnp.stack(
        [gain_first, gain_mid, gain_large, gain_small, gain_back, gain_ffn, gain_last]
    )
    shift_grads = jnp.stack(
        [shift_first, shift_mid, shift_large, shift_small, shift_back, shift_ffn, shift_last]
    )
    return (
        block_out,
        grad_image,
        grad_in,
        grad_large,
        grad_small,
        grad_out,
        grad_up,
        grad_down,
        gain_grads,
        shift_grads,
        gain_wide,
        shift_wide,
    )


def solution(mesh):
    return jax.shard_map(
        local,
        mesh=mesh,
        in_specs=(
            P(("node", "dev"), None, None, None),
            P(("node", "dev")),
            P(),
            P(),
            P(),
            P(),
            P(),
            P(),
            P(),
            P(),
            P(),
            P(),
            P(("node", "dev"), None, None, None),
        ),
        out_specs=(
            P(("node", "dev"), None, None, None),
            P(("node", "dev"), None, None, None),
            P(),
            P(),
            P(),
            P(),
            P(),
            P(),
            P(),
            P(),
            P(),
            P(),
        ),
        check_vma=False,
    )
```

```python
import functools
import math

import jax
import jax.numpy as jnp
import ml_dtypes
import numpy as np
from jax import lax
from jax.experimental import pallas as pl
from jax.experimental.pallas import tpu as pltpu
from jax.sharding import PartitionSpec as P

EPSILON = 1e-05
ROOT = 0.7978845608028654
CUBIC = 0.044715
AXES = ("node", "chip", "core")
ROW = 16
F32 = jnp.float32
BF16 = jnp.bfloat16


def split(table):
    high = table.astype(ml_dtypes.bfloat16)
    low = (table - high.astype(np.float64)).astype(ml_dtypes.bfloat16)
    return high, low


@functools.lru_cache(maxsize=None)
def wave_tables(canvas, side_large, side_small):
    period = 2 * canvas - 1
    pairs = [(0, v) for v in range(canvas)]
    pairs += [(u, v) for u in range(1, canvas) for v in range(period)]
    waves = np.array(pairs)
    half = -(-len(pairs) // 16) * 16

    def table(places_h, places_w, keep, sign):
        grid = np.stack(np.meshgrid(places_h, places_w, indexing="ij"), -1).reshape(-1, 2)
        angle = 2 * np.pi * ((waves @ grid.T) % period) / period
        out = np.zeros((2 * half, grid.shape[0]))
        out[: len(pairs)] = np.cos(angle) * keep
        out[half : half + len(pairs)] = sign * np.sin(angle) * keep
        return out

    share = np.zeros((2 * half, 1))
    share[: len(pairs)] = 2.0 / period**2
    share[half : half + len(pairs)] = 2.0 / period**2
    share[0] = 1.0 / period**2

    inside = (np.arange(ROW) < canvas).astype(np.float64)
    cells = table(np.arange(canvas), np.arange(ROW), np.tile(inside, canvas), -1.0)

    def taps(side, row):
        middle = (side - 1) // 2
        offsets_h = np.arange(side) - middle
        offsets_w = np.arange(row) - middle
        keep = (np.abs(offsets_h) < canvas)[:, None] & (np.abs(offsets_w) < canvas)[None, :]
        keep = keep & (np.arange(row) < side)[None, :]
        return table(offsets_h, offsets_w, keep.reshape(-1).astype(np.float64), 1.0)

    def taps_back(side, row):
        first, count = used_rows(side, canvas)
        return taps(side, row)[:, first * row : (first + count) * row]

    def tap_row(side):
        return -(-side // 16) * 16

    large = taps(side_large, tap_row(side_large))
    small = taps(side_small, tap_row(side_small))
    turn = np.ones((2 * half, 1))
    turn[half:] = -1.0
    return dict(
        half=half,
        ahead=split(cells),
        back=split((cells * share).T),
        large=split(large),
        small=split(small),
        large_back=split((taps_back(side_large, 32) * turn * share).T),
        small_back=split((taps_back(side_small, 8) * turn * share).T),
    )


def used_rows(side, canvas):
    first = max(0, (side - 1) // 2 - (canvas - 1))
    return first, side - 2 * first


def dot(left, right):
    return jnp.dot(left, right, preferred_element_type=F32)


def dot_nt(left, right):
    return lax.dot_general(left, right, (((1,), (1,)), ((), ())), preferred_element_type=F32)


def dot_tn(left, right):
    return lax.dot_general(left, right, (((0,), (0,)), ((), ())), preferred_element_type=F32)


def halves(values):
    high = values.astype(BF16)
    return high, (values - high.astype(F32)).astype(BF16)


def gelu(values):
    inner = values * (ROOT + (ROOT * CUBIC) * (values * values))
    return values * (0.5 + 0.5 * jnp.tanh(inner))


def gelu_slope(values):
    square = values * values
    bend = jnp.tanh(values * (ROOT + (ROOT * CUBIC) * square))
    slope = ROOT + (3.0 * ROOT * CUBIC) * square
    return 0.5 + 0.5 * bend + values * slope * (0.5 - 0.5 * bend * bend)


def rows(at):
    return pl.ds(pl.multiple_of(at * ROW, ROW), ROW)


def fold(values):
    return values[:8] + values[8:]


def twice(values):
    return jnp.concatenate([values, values], axis=0)


def columns_inside(side, channels):
    places = lax.broadcasted_iota(jnp.int32, (ROW, 128), 0)
    inside = (places < side).astype(F32)
    return jnp.concatenate([inside] * (channels // 128), axis=1)


def first_step():
    return pl.program_id(0) == 0


def last_step():
    return pl.program_id(0) == pl.num_programs(0) - 1


def received(sent, width):
    summed = jnp.sum(sent[...], axis=0, keepdims=True)
    return [summed[:, at : at + width] for at in range(0, summed.shape[1], width)]


def keep(coefs, values):
    for at, value in enumerate(values):
        coefs[at] = jnp.broadcast_to(value, coefs.shape[1:])


def note(out, values):
    values = list(values)
    values += [jnp.zeros_like(values[0])] * (out.shape[0] - len(values))
    out[...] = jnp.concatenate(values, axis=0)


def add_sums(sums, parts):
    @pl.when(first_step())
    def _():
        sums[...] = jnp.zeros_like(sums)

    for at, part in enumerate(parts):
        sums[at] += part


def publish(sums, out, extra=()):
    @pl.when(last_step())
    def _():
        parts = [jnp.sum(sums[at], axis=0, keepdims=True) for at in range(sums.shape[0])]
        parts += list(extra)
        out[...] = jnp.broadcast_to(jnp.concatenate(parts, axis=1), out.shape)


def norm_coefs(column_sum, square, count, scaling, offsets):
    mean = column_sum / count
    reciprocal = lax.rsqrt(square / count - mean * mean + EPSILON)
    factor = scaling * reciprocal
    return mean, reciprocal, factor, offsets - mean * factor


def back_coefs(shift_sum, gain_sum, count, mean, reciprocal, scaling):
    factor = scaling * reciprocal
    slope = factor * reciprocal * gain_sum / count
    return factor, factor * shift_sum / count - slope * mean, slope


def zeros(count, channels):
    return tuple(jnp.zeros((8, channels), F32) for _ in range(count))


def enter_stage(sides, image, cotangent, x_out, u_out, sent, padded, sums):
    at_crop = pl.program_id(0)
    side = sides[at_crop]
    canvas, channels = image.shape[1], image.shape[3]
    inside = columns_inside(side, channels)

    @pl.when(first_step())
    def _():
        padded[...] = jnp.zeros_like(padded)

    def step(at, carry):
        mask = jnp.where(at < side, inside, 0.0)
        start = pl.multiple_of(at * ROW, ROW)
        padded[0, pl.ds(start, canvas), :] = image[0, at].astype(F32)
        padded[1, pl.ds(start, canvas), :] = cotangent[0, at].astype(F32)
        x = padded[0, rows(at), :] * mask
        u = padded[1, rows(at), :] * mask
        x_out[rows(at), :] = x.astype(BF16)
        u_out[rows(at), :] = u.astype(BF16)
        return carry[0] + fold(x), carry[1] + fold(x * x)

    add_sums(sums, lax.fori_loop(0, canvas, step, zeros(2, channels), unroll=7))
    count = jnp.int32(0)
    for at in range(sides.shape[0]):
        count += sides[at] * sides[at]
    publish(sums, sent, [jnp.full((1, 128), count.astype(F32))])


def first_stage(sides, came, scale, offset, x_in, weight, low_out, pre_out, sent, seen, coefs, sums):
    channels = x_in.shape[1]
    canvas = x_in.shape[0] // ROW
    side = sides[pl.program_id(0)]

    @pl.when(first_step())
    def _():
        parts = received(came, 128)
        tiles = channels // 128
        column_sum = jnp.concatenate(parts[:tiles], axis=1)
        square = jnp.concatenate(parts[tiles : 2 * tiles], axis=1)
        count = jnp.concatenate([parts[2 * tiles]] * tiles, axis=1)
        mean, reciprocal, factor, constant = norm_coefs(column_sum, square, count, scale[0:1], offset[0:1])
        keep(coefs, [factor, constant])
        note(seen, [count, mean, reciprocal, column_sum, square])

    inside = columns_inside(side, channels)
    factor, constant = twice(coefs[0]), twice(coefs[1])

    def step(at, carry):
        mask = jnp.where(at < side, inside, 0.0)
        low_out[rows(at), :] = (mask * (factor * x_in[rows(at), :].astype(F32) + constant)).astype(BF16)
        return carry

    lax.fori_loop(0, canvas, step, 0, unroll=7)
    pre_out[...] = dot(low_out[...], weight[...])

    def measure(at, carry):
        pre = pre_out[rows(at), :]
        return carry[0] + fold(pre), carry[1] + fold(pre * pre)

    add_sums(sums, lax.fori_loop(0, canvas, measure, zeros(2, channels), unroll=7))
    publish(sums, sent)


def times(spectrum, kernel, half, at, conj):
    real, imag = pl.ds(pl.multiple_of(at * 16, 16), 16), pl.ds(pl.multiple_of(half + at * 16, 16), 16)
    a, b = spectrum[real, :], spectrum[imag, :]
    c, d = kernel[real, :], kernel[imag, :]
    if conj:
        return real, imag, a * c + b * d, b * c - a * d
    return real, imag, a * c - b * d, a * d + b * c


def ahead(tables, values):
    return dot(tables[0][...], values) + dot(tables[1][...], values)


def back(tables, high, low):
    return dot(tables[0][...], high) + dot(tables[0][...], low) + dot(tables[1][...], high)


def mixer_stage(
    sides, came, seen, scale, offset, pre_in, ahead_t, back_t, large_w, small_w,
    low_out, large_out, small_out, sent, noted, coefs, sums, spectrum, high, low,
):
    channels = pre_in.shape[1]
    canvas = pre_in.shape[0] // ROW
    half = spectrum.shape[0] // 2
    side = sides[pl.program_id(0)]

    @pl.when(first_step())
    def _():
        mean, reciprocal, factor, constant = norm_coefs(
            *received(came, channels), seen[0:1], scale[1:2], offset[1:2]
        )
        keep(coefs, [factor, constant])
        note(noted, [mean, reciprocal])

    inside = columns_inside(side, channels)
    factor, constant = twice(coefs[0]), twice(coefs[1])

    def step(at, carry):
        mask = jnp.where(at < side, inside, 0.0)
        low_out[rows(at), :] = gelu(mask * (factor * pre_in[rows(at), :] + constant)).astype(BF16)
        return carry

    lax.fori_loop(0, canvas, step, 0, unroll=7)
    spectrum[...] = ahead(ahead_t, low_out[...])
    parts = ()
    for kernel, out in ((large_w, large_out), (small_w, small_out)):

        def product(at, carry):
            real, imag, new_real, new_imag = times(spectrum, kernel, half, at, False)
            high[real, :], low[real, :] = halves(new_real)
            high[imag, :], low[imag, :] = halves(new_imag)
            return carry

        lax.fori_loop(0, half // 16, product, 0, unroll=4)
        out[...] = back(back_t, high[...], low[...])

        def measure(at, carry):
            conv = jnp.where(at < side, inside, 0.0) * out[rows(at), :]
            out[rows(at), :] = conv
            return carry[0] + fold(conv), carry[1] + fold(conv * conv)

        parts += lax.fori_loop(0, canvas, measure, zeros(2, channels), unroll=7)
    add_sums(sums, parts)
    publish(sums, sent)


def merge_stage(
    sides, came, seen, scale, offset, large_in, small_in, x_in, u_in, weight,
    low_out, proj_out, sent, noted, coefs, sums,
):
    channels = x_in.shape[1]
    canvas = x_in.shape[0] // ROW
    side = sides[pl.program_id(0)]

    @pl.when(first_step())
    def _():
        large_sum, large_square, small_sum, small_square = received(came, channels)
        large = norm_coefs(large_sum, large_square, seen[0:1], scale[2:3], offset[2:3])
        small = norm_coefs(small_sum, small_square, seen[0:1], scale[3:4], offset[3:4])
        keep(coefs, [large[2], small[2], large[3] + small[3]])
        note(noted, [large[0], large[1], small[0], small[1], large[2], small[2], large[3] + small[3]])

    inside = columns_inside(side, channels)
    large, small, constant = twice(coefs[0]), twice(coefs[1]), twice(coefs[2])

    def step(at, carry):
        mask = jnp.where(at < side, inside, 0.0)
        merged = mask * (large * large_in[rows(at), :] + small * small_in[rows(at), :] + constant)
        low_out[rows(at), :] = gelu(merged).astype(BF16)
        return carry

    lax.fori_loop(0, canvas, step, 0, unroll=7)
    proj_out[...] = dot(low_out[...], weight[...])

    def measure(at, carry):
        proj = proj_out[rows(at), :]
        x, u = x_in[rows(at), :].astype(F32), u_in[rows(at), :].astype(F32)
        parts = (proj, proj * proj, proj * x, proj * u)
        return tuple(old + fold(part) for old, part in zip(carry, parts))

    add_sums(sums, lax.fori_loop(0, canvas, measure, zeros(4, channels), unroll=2))
    publish(sums, sent)


def widen_stage(
    sides, came, seen, scale, offset, x_in, proj_in, weight, low_out, hidden_out, sent, noted, coefs, sums
):
    channels = x_in.shape[1]
    canvas = x_in.shape[0] // ROW
    side = sides[pl.program_id(0)]

    @pl.when(first_step())
    def _():
        proj_sum, proj_square, cross, _ = parts = received(came, channels)
        count, x_mean, x_sum, x_square = seen[0:1], seen[1:2], seen[3:4], seen[4:5]
        mean, reciprocal, factor, constant = norm_coefs(
            proj_sum, proj_square, count, scale[4:5], offset[4:5]
        )
        mid_mean = x_mean + factor * mean + constant
        x_var = x_square / count - x_mean * x_mean
        proj_var = proj_square / count - mean * mean
        both = cross / count - x_mean * mean
        mid_var = x_var + factor * factor * proj_var + 2.0 * factor * both
        mid_reciprocal = lax.rsqrt(mid_var + EPSILON)
        mid_factor = scale[5:6] * mid_reciprocal
        keep(coefs, [mid_factor, mid_factor * factor, mid_factor * (constant - mid_mean) + offset[5:6]])
        note(noted, [mean, reciprocal, mid_mean, mid_reciprocal] + parts)

    inside = columns_inside(side, channels)
    from_x, from_proj, constant = twice(coefs[0]), twice(coefs[1]), twice(coefs[2])

    def step(at, carry):
        mask = jnp.where(at < side, inside, 0.0)
        x = x_in[rows(at), :].astype(F32)
        low_out[rows(at), :] = (mask * (from_x * x + from_proj * proj_in[rows(at), :] + constant)).astype(BF16)
        return carry

    lax.fori_loop(0, canvas, step, 0, unroll=7)
    parts = [[], []]
    for at_block in range(hidden_out.shape[1] // channels):
        block = slice(at_block * channels, (at_block + 1) * channels)
        hidden_out[:, block] = dot(low_out[...], weight[:, block])

        def measure(at, carry):
            hidden = hidden_out[rows(at), block]
            return carry[0] + fold(hidden), carry[1] + fold(hidden * hidden)

        found = lax.fori_loop(0, canvas, measure, zeros(2, channels), unroll=7)
        parts[0].append(found[0])
        parts[1].append(found[1])
    add_sums(sums, [jnp.concatenate(part, axis=1) for part in parts])
    hand_over(sums, sent)


def hand_over(sums, out):
    @pl.when(last_step())
    def _():
        out[...] = jnp.concatenate([jnp.sum(sums[at], axis=0, keepdims=True) for at in range(2)], axis=0)


def narrow_stage(
    sides, came, seen, wide_scale, wide_offset, hidden_in, u_in, weight, low_out, proj_out, sent, noted, coefs, sums
):
    channels = u_in.shape[1]
    canvas = u_in.shape[0] // ROW
    wide = hidden_in.shape[1]
    side = sides[pl.program_id(0)]

    @pl.when(first_step())
    def _():
        count = jnp.concatenate([seen[0:1]] * (wide // channels), axis=1)
        mean, reciprocal, factor, constant = norm_coefs(
            came[0:1], came[1:2], count, wide_scale[...], wide_offset[...]
        )
        keep(coefs, [factor, constant])
        note(noted, [mean, reciprocal, factor, constant, count])

    for at_block in range(wide // channels):
        block = slice(at_block * channels, (at_block + 1) * channels)
        factor, constant = twice(coefs[0, :, block]), twice(coefs[1, :, block])

        def step(at, carry):
            low_out[rows(at), block] = gelu(factor * hidden_in[rows(at), block] + constant).astype(BF16)
            return carry

        lax.fori_loop(0, canvas, step, 0, unroll=7)
    proj_out[...] = dot(low_out[...], weight[...])
    inside = columns_inside(side, channels)

    def measure(at, carry):
        proj = jnp.where(at < side, inside, 0.0) * proj_out[rows(at), :]
        proj_out[rows(at), :] = proj
        u = u_in[rows(at), :].astype(F32)
        parts = (proj, proj * proj, proj * u, u)
        return tuple(old + fold(part) for old, part in zip(carry, parts))

    add_sums(sums, lax.fori_loop(0, canvas, measure, zeros(4, channels), unroll=2))
    publish(sums, sent)


def wide_back_stage(
    sides, came, seen, wide_seen, scale, offset, proj_in, u_in, hidden_in, weight,
    down_out, grad_out, sent, noted, coefs, sums,
):
    channels = u_in.shape[1]
    canvas = u_in.shape[0] // ROW
    wide = hidden_in.shape[1]
    side = sides[pl.program_id(0)]

    @pl.when(first_step())
    def _():
        proj_sum, proj_square, cross, u_sum = received(came, channels)
        count = seen[0:1]
        mean, reciprocal, factor, constant = norm_coefs(
            proj_sum, proj_square, count, scale[6:7], offset[6:7]
        )
        gain_sum = reciprocal * (cross - mean * u_sum)
        keep(coefs, back_coefs(u_sum, gain_sum, count, mean, reciprocal, scale[6:7]))
        note(noted, [mean, reciprocal, u_sum, gain_sum, factor, constant])

    inside = columns_inside(side, channels)
    factor, constant, slope = twice(coefs[0]), twice(coefs[1]), twice(coefs[2])

    def step(at, carry):
        mask = jnp.where(at < side, inside, 0.0)
        u = u_in[rows(at), :].astype(F32)
        down_out[rows(at), :] = (mask * (factor * u - constant - slope * proj_in[rows(at), :])).astype(BF16)
        return carry

    lax.fori_loop(0, canvas, step, 0, unroll=7)
    parts = [[], []]
    for at_block in range(wide // channels):
        block = slice(at_block * channels, (at_block + 1) * channels)
        grad_out[:, block] = dot(down_out[...], weight[:, block])
        wide_factor = jnp.broadcast_to(wide_seen[2:3, block], (ROW, channels))
        wide_constant = jnp.broadcast_to(wide_seen[3:4, block], (ROW, channels))

        def measure(at, carry):
            hidden = hidden_in[rows(at), block]
            grad = grad_out[rows(at), block] * gelu_slope(wide_factor * hidden + wide_constant)
            grad_out[rows(at), block] = grad
            return carry[0] + fold(grad), carry[1] + fold(grad * hidden)

        found = lax.fori_loop(0, canvas, measure, zeros(2, channels))
        parts[0].append(found[0])
        parts[1].append(found[1])
    add_sums(sums, [jnp.concatenate(part, axis=1) for part in parts])
    hand_over(sums, sent)


def narrow_back_stage(
    sides, came, wide_seen, wide_scale, grad_in, hidden_in, x_in, proj_in, weight,
    up_out, ffn_out, sent, noted, coefs, sums,
):
    channels = x_in.shape[1]
    canvas = x_in.shape[0] // ROW
    wide = hidden_in.shape[1]
    side = sides[pl.program_id(0)]

    @pl.when(first_step())
    def _():
        mean, reciprocal, count = wide_seen[0:1], wide_seen[1:2], wide_seen[4:5]
        shift_sum = came[0:1]
        gain_sum = reciprocal * (came[1:2] - mean * shift_sum)
        keep(coefs, back_coefs(shift_sum, gain_sum, count, mean, reciprocal, wide_scale[...]))
        note(noted, [gain_sum, shift_sum])

    for at_block in range(wide // channels):
        block = slice(at_block * channels, (at_block + 1) * channels)
        factor, constant, slope = (twice(coefs[at, :, block]) for at in range(3))

        def step(at, carry):
            grad = factor * grad_in[rows(at), block] - constant - slope * hidden_in[rows(at), block]
            up_out[rows(at), block] = grad.astype(BF16)
            return carry

        lax.fori_loop(0, canvas, step, 0, unroll=7)
    ffn_out[...] = dot(up_out[...], weight[...])
    inside = columns_inside(side, channels)

    def measure(at, carry):
        grad = jnp.where(at < side, inside, 0.0) * ffn_out[rows(at), :]
        ffn_out[rows(at), :] = grad
        parts = (grad, grad * x_in[rows(at), :].astype(F32), grad * proj_in[rows(at), :])
        return tuple(old + fold(part) for old, part in zip(carry, parts))

    add_sums(sums, lax.fori_loop(0, canvas, measure, zeros(3, channels), unroll=2))
    publish(sums, sent)


def mid_back_stage(
    sides, came, seen, merge_seen, mid_seen, last_seen, scale, offset,
    x_in, u_in, proj_in, ffn_in, large_in, small_in, weight,
    resid_out, back_out, grad_out, sent, noted, coefs, sums,
):
    channels = x_in.shape[1]
    canvas = x_in.shape[0] // ROW
    side = sides[pl.program_id(0)]

    @pl.when(first_step())
    def _():
        ffn_sum, ffn_x, ffn_proj = received(came, channels)
        count, u_sum = seen[0:1], last_seen[2:3]
        mean, reciprocal, mid_mean, mid_reciprocal = (mid_seen[at : at + 1] for at in range(4))
        proj_sum, proj_square, cross, proj_u = (mid_seen[at : at + 1] for at in range(4, 8))
        proj_factor = scale[4:5] * reciprocal
        proj_constant = offset[4:5] - mean * proj_factor
        ffn_mid = ffn_x + proj_factor * ffn_proj + proj_constant * ffn_sum
        mid_gain = mid_reciprocal * (ffn_mid - mid_mean * ffn_sum)
        factor, constant, slope = back_coefs(ffn_sum, mid_gain, count, mid_mean, mid_reciprocal, scale[5:6])
        mid_proj = cross + proj_factor * proj_square + proj_constant * proj_sum
        resid_sum = u_sum
        resid_proj = proj_u + factor * ffn_proj - constant * proj_sum - slope * mid_proj
        gain = reciprocal * (resid_proj - mean * resid_sum)
        second = back_coefs(resid_sum, gain, count, mean, reciprocal, scale[4:5])
        keep(coefs, [factor, constant + slope * proj_constant, slope, slope * proj_factor, *second])
        note(noted, [mid_gain, ffn_sum, gain, resid_sum])

    inside = columns_inside(side, channels)

    def step(at, carry):
        mask = jnp.where(at < side, inside, 0.0)
        x, u = x_in[rows(at), :].astype(F32), u_in[rows(at), :].astype(F32)
        proj = proj_in[rows(at), :]
        resid = twice(coefs[0]) * ffn_in[rows(at), :] - twice(coefs[1]) - twice(coefs[2]) * x
        resid = u + mask * (resid - twice(coefs[3]) * proj)
        resid_out[rows(at), :] = resid
        down = twice(coefs[4]) * resid - twice(coefs[5]) - twice(coefs[6]) * proj
        back_out[rows(at), :] = (mask * down).astype(BF16)
        return carry

    lax.fori_loop(0, canvas, step, 0)
    grad_out[...] = dot(back_out[...], weight[...])
    large = jnp.broadcast_to(merge_seen[4:5], (ROW, channels))
    small = jnp.broadcast_to(merge_seen[5:6], (ROW, channels))
    constant = jnp.broadcast_to(merge_seen[6:7], (ROW, channels))

    def measure(at, carry):
        large_conv, small_conv = large_in[rows(at), :], small_in[rows(at), :]
        grad = grad_out[rows(at), :] * gelu_slope(large * large_conv + small * small_conv + constant)
        grad_out[rows(at), :] = grad
        parts = (grad, grad * large_conv, grad * small_conv)
        return tuple(old + fold(part) for old, part in zip(carry, parts))

    add_sums(sums, lax.fori_loop(0, canvas, measure, zeros(3, channels), unroll=2))
    publish(sums, sent)


def mixer_back_stage(
    sides, came, seen, merge_seen, first_seen, scale, offset, large_in, small_in, grad_in, pre_in,
    ahead_t, back_t, large_w, small_w,
    large_out, small_out, grad_out, sent, noted, coefs, sums, large_s, small_s, high, low,
):
    channels = pre_in.shape[1]
    canvas = pre_in.shape[0] // ROW
    half = large_s.shape[0] // 2
    side = sides[pl.program_id(0)]

    @pl.when(first_step())
    def _():
        shift_sum, with_large, with_small = received(came, channels)
        count = seen[0:1]
        large_mean, large_r, small_mean, small_r = (merge_seen[at : at + 1] for at in range(4))
        large_gain = large_r * (with_large - large_mean * shift_sum)
        small_gain = small_r * (with_small - small_mean * shift_sum)
        keep(
            coefs,
            [
                *back_coefs(shift_sum, large_gain, count, large_mean, large_r, scale[2:3]),
                *back_coefs(shift_sum, small_gain, count, small_mean, small_r, scale[3:4]),
            ],
        )
        note(noted, [large_gain, small_gain, shift_sum])

    inside = columns_inside(side, channels)

    def step(at, carry):
        mask = jnp.where(at < side, inside, 0.0)
        grad = grad_in[rows(at), :]
        large = twice(coefs[0]) * grad - twice(coefs[1]) - twice(coefs[2]) * large_in[rows(at), :]
        small = twice(coefs[3]) * grad - twice(coefs[4]) - twice(coefs[5]) * small_in[rows(at), :]
        large_out[rows(at), :] = (mask * large).astype(BF16)
        small_out[rows(at), :] = (mask * small).astype(BF16)
        return carry

    lax.fori_loop(0, canvas, step, 0)
    large_s[...] = ahead(ahead_t, large_out[...])
    small_s[...] = ahead(ahead_t, small_out[...])

    def product(at, carry):
        real, imag, one_real, one_imag = times(large_s, large_w, half, at, True)
        _, _, two_real, two_imag = times(small_s, small_w, half, at, True)
        high[real, :], low[real, :] = halves(one_real + two_real)
        high[imag, :], low[imag, :] = halves(one_imag + two_imag)
        return carry

    lax.fori_loop(0, half // 16, product, 0, unroll=4)
    grad_out[...] = back(back_t, high[...], low[...])
    reciprocal = first_seen[1:2]
    factor = scale[1:2] * reciprocal
    constant = jnp.broadcast_to(offset[1:2] - first_seen[0:1] * factor, (ROW, channels))
    factor = jnp.broadcast_to(factor, (ROW, channels))

    def measure(at, carry):
        mask = jnp.where(at < side, inside, 0.0)
        pre = pre_in[rows(at), :]
        grad = mask * grad_out[rows(at), :] * gelu_slope(factor * pre + constant)
        grad_out[rows(at), :] = grad
        return carry[0] + fold(grad), carry[1] + fold(grad * pre)

    add_sums(sums, lax.fori_loop(0, canvas, measure, zeros(2, channels)))
    publish(sums, sent)


def first_back_stage(
    sides, came, seen, first_seen, scale, grad_in, pre_in, x_in, weight,
    low_out, grad_out, sent, noted, coefs, sums,
):
    channels = pre_in.shape[1]
    canvas = pre_in.shape[0] // ROW
    side = sides[pl.program_id(0)]

    @pl.when(first_step())
    def _():
        shift_sum, with_pre = received(came, channels)
        mean, reciprocal = first_seen[0:1], first_seen[1:2]
        gain_sum = reciprocal * (with_pre - mean * shift_sum)
        keep(coefs, back_coefs(shift_sum, gain_sum, seen[0:1], mean, reciprocal, scale[1:2]))
        note(noted, [gain_sum, shift_sum])

    inside = columns_inside(side, channels)
    factor, constant, slope = twice(coefs[0]), twice(coefs[1]), twice(coefs[2])

    def step(at, carry):
        mask = jnp.where(at < side, inside, 0.0)
        grad = factor * grad_in[rows(at), :] - constant - slope * pre_in[rows(at), :]
        low_out[rows(at), :] = (mask * grad).astype(BF16)
        return carry

    lax.fori_loop(0, canvas, step, 0, unroll=7)
    grad_out[...] = dot(low_out[...], weight[...])

    def measure(at, carry):
        grad = grad_out[rows(at), :]
        return carry[0] + fold(grad), carry[1] + fold(grad * x_in[rows(at), :].astype(F32))

    add_sums(sums, lax.fori_loop(0, canvas, measure, zeros(2, channels), unroll=7))
    publish(sums, sent)


def leave_stage(sides, came, seen, scale, resid_in, grad_in, x_in, image_out, noted, coefs):
    channels = x_in.shape[1]
    canvas = x_in.shape[0] // ROW
    side = sides[pl.program_id(0)]

    @pl.when(first_step())
    def _():
        shift_sum, with_x = received(came, channels)
        count, mean, reciprocal = (seen[at : at + 1] for at in range(3))
        gain_sum = reciprocal * (with_x - mean * shift_sum)
        keep(coefs, back_coefs(shift_sum, gain_sum, count, mean, reciprocal, scale[0:1]))
        note(noted, [gain_sum, shift_sum])

    inside = columns_inside(side, channels)
    factor, constant, slope = twice(coefs[0]), twice(coefs[1]), twice(coefs[2])

    def step(at, carry):
        mask = jnp.where(at < side, inside, 0.0)
        grad = factor * grad_in[rows(at), :] - constant - slope * x_in[rows(at), :].astype(F32)
        image_out[0, at] = (mask * (resid_in[rows(at), :] + grad))[:canvas]
        return carry

    lax.fori_loop(0, canvas, step, 0, unroll=7)


def block_out_stage(sides, mid_seen, last_seen, scale, offset, x_in, mid_in, last_in, out):
    channels = x_in.shape[1]
    canvas = x_in.shape[0] // ROW
    side = sides[pl.program_id(0)]
    inside = columns_inside(side, channels)
    factor = scale[4:5] * mid_seen[1:2]
    constant = offset[4:5] - mid_seen[0:1] * factor + last_seen[5:6]
    constant = jnp.broadcast_to(constant, (ROW, channels))
    factor = jnp.broadcast_to(factor, (ROW, channels))
    last = jnp.broadcast_to(last_seen[4:5], (ROW, channels))

    def step(at, carry):
        mask = jnp.where(at < side, inside, 0.0)
        added = factor * mid_in[rows(at), :] + last * last_in[rows(at), :] + constant
        out[0, at] = (x_in[rows(at), :].astype(F32) + mask * added)[:canvas].astype(BF16)
        return carry

    lax.fori_loop(0, canvas, step, 0, unroll=7)


def kernel_waves_stage(large, small, large_t, small_t, large_out, small_out, large_rows, small_rows):
    for kernel, table, out, flat in (
        (large, large_t, large_out, large_rows),
        (small, small_t, small_out, small_rows),
    ):
        side = kernel.shape[0]
        row = flat.shape[0] // side
        flat[...] = jnp.zeros_like(flat)
        for at in range(side):
            flat[at * row : at * row + side, :] = kernel[at]
        out[...] = ahead(table, flat[...])


def kernel_grad_stage(
    place, mixer, large, small, merged, merged_grad, ahead_t, large_t, small_t, other_out, mine_out,
    mixer_s, grad_s, large_sum, small_sum, flat, proj_sum,
):
    half = mixer_s.shape[0] // 2
    at_crop = pl.program_id(0)
    proj = dot_tn(merged[...], merged_grad[...])

    @pl.when(at_crop == 0)
    def _():
        proj_sum[...] = proj

    @pl.when(at_crop != 0)
    def _():
        proj_sum[...] += proj

    mixer_s[...] = ahead(ahead_t, mixer[...])
    for grad, total in ((large, large_sum), (small, small_sum)):
        grad_s[...] = ahead(ahead_t, grad[...])

        def product(at, carry):
            real, imag, new_real, new_imag = times(mixer_s, grad_s, half, at, True)

            @pl.when(at_crop == 0)
            def _():
                total[real, :] = new_real
                total[imag, :] = new_imag

            @pl.when(at_crop != 0)
            def _():
                total[real, :] += new_real
                total[imag, :] += new_imag

            return carry

        lax.fori_loop(0, half // 16, product, 0, unroll=4)

    @pl.when(last_step())
    def _():
        start = 0
        for total, table in ((large_sum, large_t), (small_sum, small_t)):
            size = table[0].shape[0]
            flat[start : start + size, :] = back(table, *halves(total[...]))
            start += size
        flat[start:, :] = jnp.zeros((flat.shape[0] - start, flat.shape[1]), F32)
        size, rest = flat.shape[0] // 2, proj_sum.shape[0] // 2
        for out, core in ((mine_out, place[0]), (other_out, 1 - place[0])):
            out[:size, :] = flat[pl.ds(pl.multiple_of(core * size, 8), size), :]
            out[size:, :] = proj_sum[pl.ds(pl.multiple_of(core * rest, 8), rest), :]


def kernel_grad_out_stage(settled, large_out, small_out, proj_out, flat, *, canvas):
    rest = proj_out.shape[0] // 2
    size = settled.shape[0] // 2 - rest
    for core in range(2):
        start = core * (size + rest)
        flat[core * size : (core + 1) * size, :] = settled[start : start + size, :]
        proj_out[core * rest : (core + 1) * rest, :] = settled[start + size : start + size + rest, :]
    start = 0
    for out, row in ((large_out, 32), (small_out, 8)):
        side = out.shape[0]
        first, count = used_rows(side, canvas)
        for at in range(side):
            if first <= at < first + count:
                out[at] = flat[start : start + side, :]
                start += row
            else:
                out[at] = jnp.zeros(out.shape[1:], F32)


def weight_grad_stage(place, inputs, gradient, out):
    out[...] = dot_tn(inputs[...], gradient[...])


SMEM = pl.BlockSpec(memory_space=pltpu.SMEM)


def whole(shape):
    return pl.BlockSpec(shape, lambda at: (0,) * len(shape))


VMEM = 62 * 1024 * 1024


def call(kernel, crops, ins, outs, scratch):
    def spec(shape, kind):
        if kind == "smem":
            return SMEM
        if kind == "rows":
            return pl.BlockSpec((shape[0] // crops, shape[1]), lambda at: (at, 0))
        if kind == "map":
            return pl.BlockSpec((1,) + tuple(shape[1:]), lambda at: (at, 0, 0, 0))
        return whole(tuple(shape))

    flat, specs, places = [], [], []
    for value, kind in ins:
        group = value if isinstance(value, tuple) else (value,)
        places.append((len(flat), len(group) if isinstance(value, tuple) else 0))
        for part in group:
            flat.append(part)
            specs.append(spec(part.shape, kind))

    def body(*refs):
        given = [refs[at : at + size] if size else refs[at] for at, size in places]
        kernel(*given, *refs[len(flat) :])

    return pl.pallas_call(
        body,
        grid=(crops,),
        in_specs=specs,
        out_specs=[spec(shape, kind) for shape, _, kind in outs],
        out_shape=[jax.ShapeDtypeStruct(shape, dtype) for shape, dtype, _ in outs],
        scratch_shapes=[pltpu.VMEM(shape, dtype) for shape, dtype in scratch],
        compiler_params=pltpu.CompilerParams(
            dimension_semantics=("arbitrary",), vmem_limit_bytes=VMEM
        ),
        cost_estimate=pl.CostEstimate(
            flops=0,
            bytes_accessed=sum(part.size * part.dtype.itemsize for part in flat)
            + sum(math.prod(shape) * jnp.dtype(dtype).itemsize for shape, dtype, _ in outs),
            transcendentals=0,
        ),
        name=getattr(kernel, "func", kernel).__name__,
    )(*flat)


def weight_grad(inputs, gradient, place=None):
    deep, high = inputs.shape
    wide = gradient.shape[1]
    if place is None:
        place = jnp.zeros((1,), jnp.int32)
    else:
        high = high // 2
    block, across = min(high, 512), min(wide, 512)
    return pl.pallas_call(
        weight_grad_stage,
        grid_spec=pltpu.PrefetchScalarGridSpec(
            num_scalar_prefetch=1,
            grid=(high // block, wide // across),
            in_specs=[
                pl.BlockSpec((deep, block), lambda i, j, place: (0, place[0] * (high // block) + i)),
                pl.BlockSpec((deep, across), lambda i, j, place: (0, j)),
            ],
            out_specs=pl.BlockSpec((block, across), lambda i, j, place: (i, j)),
        ),
        out_shape=jax.ShapeDtypeStruct((high, wide), F32),
        compiler_params=pltpu.CompilerParams(
            dimension_semantics=("arbitrary", "arbitrary"), vmem_limit_bytes=VMEM
        ),
        cost_estimate=pl.CostEstimate(
            flops=2 * deep * high * wide,
            bytes_accessed=2 * deep * (high + wide) + 4 * high * wide,
            transcendentals=0,
        ),
        name="weight_grad_stage",
    )(place, inputs, gradient)


def exchange(sent):
    return lax.all_to_all(sent, AXES, 0, 0, tiled=True)


SWAP = [(0, 1), (1, 0)]


def wide_exchange(sums):
    core = lax.axis_index("core")
    mine = lax.dynamic_index_in_dim(sums, core, 0, False)
    other = lax.dynamic_index_in_dim(sums, 1 - core, 0, False)
    mine = mine + lax.ppermute(other, "core", SWAP)
    chips = lax.axis_size(("node", "chip"))
    copies = jnp.broadcast_to(mine[None], (chips,) + mine.shape)
    mine = jnp.sum(lax.all_to_all(copies, ("node", "chip"), 0, 0, tiled=True), axis=0)
    other = lax.ppermute(mine, "core", SWAP)
    return jnp.where(core == 0, jnp.stack([mine, other]), jnp.stack([other, mine]))


def sum_and_cut(arrays, place, ways):
    count, wide = arrays[0].shape
    part = count // ways

    def body(place, *refs):
        total = refs[0][...]
        for ref in refs[1 : len(arrays)]:
            total = total + ref[...]
        for at, out in enumerate(refs[len(arrays) :]):

            @pl.when(pl.program_id(0) == at)
            def _():
                out[...] = total

    return pl.pallas_call(
        body,
        grid_spec=pltpu.PrefetchScalarGridSpec(
            num_scalar_prefetch=1,
            grid=(ways,),
            in_specs=[pl.BlockSpec((part, wide), lambda at, place: (place[0] ^ at, 0))] * len(arrays),
            out_specs=[pl.BlockSpec((part, wide), lambda at, place: (0, 0))] * ways,
        ),
        out_shape=[jax.ShapeDtypeStruct((part, wide), F32)] * ways,
        compiler_params=pltpu.CompilerParams(dimension_semantics=("arbitrary",), vmem_limit_bytes=VMEM),
        cost_estimate=pl.CostEstimate(
            flops=0, bytes_accessed=4 * count * wide * (len(arrays) + 1), transcendentals=0
        ),
        name="sum_and_cut",
    )(place, *arrays)


def join(parts, place):
    part, wide = parts[0].shape
    ways = len(parts)

    def body(place, *refs):
        for at, ref in enumerate(refs[:ways]):

            @pl.when(pl.program_id(0) == at)
            def _():
                refs[ways][...] = ref[...]

    return pl.pallas_call(
        body,
        grid_spec=pltpu.PrefetchScalarGridSpec(
            num_scalar_prefetch=1,
            grid=(ways,),
            in_specs=[pl.BlockSpec((part, wide), lambda at, place: (0, 0))] * ways,
            out_specs=pl.BlockSpec((part, wide), lambda at, place: (place[0] ^ at, 0)),
        ),
        out_shape=jax.ShapeDtypeStruct((ways * part, wide), F32),
        compiler_params=pltpu.CompilerParams(dimension_semantics=("arbitrary",), vmem_limit_bytes=VMEM),
        cost_estimate=pl.CostEstimate(flops=0, bytes_accessed=8 * ways * part * wide, transcendentals=0),
        name="join",
    )(place, *parts)


def place_on(axis):
    return lax.axis_index(axis)[None]


def across(parts, axis):
    size = lax.axis_size(axis)
    return [
        lax.ppermute(part, axis, [(at, at ^ k) for at in range(size)]) if k else part
        for k, part in enumerate(parts)
    ]


class Settle:
    def __init__(self, other, mine, steps):
        half = mine.shape[0]
        self.first = mine
        if half % (8 * lax.axis_size(("node", "chip"))):
            first = lax.axis_index("core") == 0
            both = jnp.where(first, jnp.concatenate([mine, other]), jnp.concatenate([other, mine]))
            self.value = lax.psum(both, AXES)
            self.steps = []
        else:
            self.parts = [mine, lax.ppermute(other, "core", SWAP)]
            self.steps = list(steps)

    def chip(self):
        self.cut("chip")

    def node(self):
        self.cut("node")

    def cut(self, axis):
        self.parts = sum_and_cut(self.parts, place_on(axis), lax.axis_size(axis))
        self.mark = self.parts[0]
        self.parts = across(self.parts, axis)

    def piece(self):
        (self.mark,) = sum_and_cut(self.parts, place_on("node") * 0, 1)
        self.parts = across([self.mark] * lax.axis_size("node"), "node")

    def gather(self):
        (self.mark,) = sum_and_cut(self.parts, place_on("node") * 0, 1)
        self.value = lax.all_gather(self.mark, ("core", "chip", "node"), axis=0, tiled=True)

    def to_chip(self):
        self.join("node", "chip")

    def to_core(self):
        self.join("chip", "core")

    def end(self):
        self.value = self.mark = join(self.parts, place_on("core"))

    def join(self, axis, onward):
        self.mark = join(self.parts, place_on(axis))
        self.parts = across([self.mark] * lax.axis_size(onward), onward)

    def step(self, token):
        if not self.steps:
            return token
        self.parts, token = lax.optimization_barrier((self.parts, token))
        getattr(self, self.steps.pop(0))()
        return self.mark


BY_PERMUTES = ("chip", "node", "piece", "to_chip", "to_core", "end")
BY_GATHER = ("chip", "node", "gather")


def settle_weight_grad(inputs, gradient, steps):
    core = place_on("core")
    other = weight_grad(inputs, gradient, 1 - core)
    gradient, other = lax.optimization_barrier((gradient, other))
    mine = weight_grad(inputs, gradient, core)
    return Settle(other, mine, steps)


def together(value, *tokens):
    return lax.optimization_barrier((value, tokens))[0]


def local(
    image, crop_sides, proj_in, kernel_large, kernel_small, proj_out, proj_up, proj_down,
    norm_gain, norm_shift, wide_gain, wide_shift, cotangent,
):
    crops, canvas, _, channels = image.shape
    wide = proj_up.shape[1]
    devices = lax.axis_size(AXES)
    cells = crops * canvas * ROW
    tables = wave_tables(canvas, kernel_large.shape[0], kernel_small.shape[0])
    half = tables["half"]

    def const(name):
        return tuple(jnp.asarray(part) for part in tables[name])

    ahead_t, back_t = const("ahead"), const("back")
    sides = (crop_sides, "smem")
    scale, offset = (norm_gain, "whole"), (norm_shift, "whole")
    wide_scale, wide_offset = (wide_gain[None], "whole"), (wide_shift[None], "whole")
    full, full_low = ((cells, channels), F32, "rows"), ((cells, channels), BF16, "rows")
    wide_full, wide_low = ((cells, wide), F32, "rows"), ((cells, wide), BF16, "rows")
    seen_out, wide_seen_out = ((8, channels), F32, "whole"), ((8, wide), F32, "whole")

    def send(count):
        return ((devices, count), F32, "whole")

    def coefs(count, width=channels):
        return ((count, 8, width), F32)

    def run(kernel, ins, outs, scratch):
        return call(kernel, crops, ins, outs, scratch)

    def r(value):
        return (value, "rows")

    def w(value):
        return (value, "whole")

    x, u, sent = run(
        enter_stage,
        [sides, (image, "map"), (cotangent, "map")],
        [full_low, full_low, send(2 * channels + 128)],
        [((2, canvas * ROW, channels), F32), coefs(2)],
    )
    came = exchange(sent)
    spectrum_out = ((2 * half, channels), F32, "whole")
    large_w, small_w = call(
        kernel_waves_stage,
        1,
        [w(kernel_large), w(kernel_small), w(const("large")), w(const("small"))],
        [spectrum_out, spectrum_out],
        [
            ((tables["large"][0].shape[1], channels), BF16),
            ((tables["small"][0].shape[1], channels), BF16),
        ],
    )
    pre_low, pre, sent, seen = run(
        first_stage,
        [sides, w(came), scale, offset, r(x), w(proj_in)],
        [full_low, full, send(2 * channels), seen_out],
        [coefs(2), coefs(2)],
    )
    spectrum = ((2 * half, channels), F32)
    spectrum_low = ((2 * half, channels), BF16)
    mixer_low, large, small, sent, first_seen = run(
        mixer_stage,
        [sides, w(exchange(sent)), w(seen), scale, offset, r(pre), w(ahead_t), w(back_t), w(large_w), w(small_w)],
        [full_low, full, full, send(4 * channels), seen_out],
        [coefs(2), coefs(4), spectrum, spectrum_low, spectrum_low],
    )
    merged_low, proj, sent, merge_seen = run(
        merge_stage,
        [sides, w(exchange(sent)), w(seen), scale, offset, r(large), r(small), r(x), r(u), w(proj_out)],
        [full_low, full, send(4 * channels), seen_out],
        [coefs(3), coefs(4)],
    )
    ffn_low, hidden, sent, mid_seen = run(
        widen_stage,
        [sides, w(exchange(sent)), w(seen), scale, offset, r(x), r(proj), w(proj_up)],
        [full_low, wide_full, ((2, wide), F32, "whole"), seen_out],
        [coefs(3), coefs(2, wide)],
    )
    hidden_low, last, sent, wide_seen = run(
        narrow_stage,
        [sides, w(wide_exchange(sent)), w(seen), wide_scale, wide_offset, r(hidden), r(u), w(proj_down)],
        [wide_low, full, send(4 * channels), wide_seen_out],
        [coefs(2, wide), coefs(4)],
    )
    down_low, hidden_grad, sent, last_seen = run(
        wide_back_stage,
        [sides, w(exchange(sent)), w(seen), w(wide_seen), scale, offset, r(last), r(u), r(hidden), w(proj_down.T)],
        [full_low, wide_full, ((2, wide), F32, "whole"), seen_out],
        [coefs(3), coefs(2, wide)],
    )
    came = wide_exchange(sent)
    grad_down = weight_grad(hidden_low, down_low)
    came = together(came, grad_down)
    up_low, ffn_grad, sent, wide_noted = run(
        narrow_back_stage,
        [sides, w(came), w(wide_seen), wide_scale, r(hidden_grad), r(hidden), r(x), r(proj), w(proj_up.T)],
        [wide_low, full, send(3 * channels), wide_seen_out],
        [coefs(3, wide), coefs(3)],
    )
    came = exchange(sent)
    grad_up = weight_grad(ffn_low, up_low)
    came = together(came, grad_up)
    grad_down, grad_up = lax.psum((grad_down, grad_up), AXES)
    resid_grad, back_low, merged_grad, sent, mid_noted = run(
        mid_back_stage,
        [
            sides, w(came), w(seen), w(merge_seen), w(mid_seen), w(last_seen), scale, offset,
            r(x), r(u), r(proj), r(ffn_grad), r(large), r(small), w(proj_out.T),
        ],
        [full, full_low, full, send(3 * channels), seen_out],
        [coefs(7), coefs(3)],
    )
    came = exchange(sent)
    large_low, small_low, mixer_grad, sent, mixer_noted = run(
        mixer_back_stage,
        [
            sides, w(came), w(seen), w(merge_seen), w(first_seen), scale, offset,
            r(large), r(small), r(merged_grad), r(pre), w(ahead_t), w(back_t), w(large_w), w(small_w),
        ],
        [full_low, full_low, full, send(2 * channels), seen_out],
        [coefs(6), coefs(2), spectrum, spectrum, spectrum_low, spectrum_low],
    )
    came = exchange(sent)
    taps_t = (const("large_back"), const("small_back"))
    tap_rows = sum(table[0].shape[0] for table in taps_t)
    tap_rows = -(-tap_rows // (16 * devices)) * 16 * devices
    half_taps = (((tap_rows + channels) // 2, channels), F32, "whole")
    other, mine = run(
        kernel_grad_stage,
        [
            (place_on("core"), "smem"), r(mixer_low), r(large_low), r(small_low), r(merged_low), r(back_low),
            w(ahead_t), w(taps_t[0]), w(taps_t[1]),
        ],
        [half_taps, half_taps],
        [spectrum, spectrum, spectrum, spectrum, ((tap_rows, channels), F32), ((channels, channels), F32)],
    )
    settle_taps = Settle(other, mine, BY_PERMUTES)
    came = together(came, settle_taps.step(sent))
    pre_round, first_grad, sent, first_noted = run(
        first_back_stage,
        [sides, w(came), w(seen), w(first_seen), scale, r(mixer_grad), r(pre), r(x), w(proj_in.T)],
        [full_low, full, send(2 * channels), seen_out],
        [coefs(3), coefs(2)],
    )
    settle_in = settle_weight_grad(pre_low, pre_round, BY_PERMUTES)
    came = exchange(together(sent, settle_in.first))
    token = settle_in.step(settle_taps.step(settle_in.first))
    (block_out,) = run(
        block_out_stage,
        [sides, w(mid_seen), w(last_seen), scale, offset, r(x), r(proj), r(together(last, token))],
        [(image.shape, BF16, "map")],
        [],
    )
    token = settle_in.step(settle_taps.step(block_out))
    came = together(came, token)
    grad_image, enter_noted = run(
        leave_stage,
        [sides, w(came), w(seen), scale, r(resid_grad), r(first_grad), r(x)],
        [(image.shape, F32, "map"), seen_out],
        [coefs(3)],
    )
    token = grad_image
    while settle_in.steps or settle_taps.steps:
        token = settle_in.step(settle_taps.step(token))
    grad_in = settle_in.value
    grad_large, grad_small, grad_out = call(
        functools.partial(kernel_grad_out_stage, canvas=canvas),
        1,
        [w(settle_taps.value)],
        [(kernel_large.shape, F32, "whole"), (kernel_small.shape, F32, "whole"), (proj_out.shape, F32, "whole")],
        [((tap_rows, channels), F32)],
    )
    gain_grads = jnp.stack(
        [enter_noted[0], first_noted[0], mixer_noted[0], mixer_noted[1], mid_noted[2], mid_noted[0], last_seen[3]]
    )
    shift_grads = jnp.stack(
        [enter_noted[1], first_noted[1], mixer_noted[2], mixer_noted[2], mid_noted[3], mid_noted[1], last_seen[2]]
    )
    return (
        block_out, grad_image, grad_in, grad_large, grad_small, grad_out, grad_up, grad_down,
        gain_grads, shift_grads, wide_noted[0], wide_noted[1],
    )


def solution(mesh):
    nodes, devices = mesh.devices.shape
    chips = jax.sharding.Mesh(mesh.devices.reshape(nodes, devices // 2, 2), AXES)
    maps = P(AXES, None, None, None)
    return jax.shard_map(
        local,
        mesh=chips,
        in_specs=(maps, P(AXES)) + (P(),) * 10 + (maps,),
        out_specs=(maps, maps) + (P(),) * 10,
        check_vma=False,
    )
```

```python
import functools
import math

import jax
import jax.numpy as jnp
import ml_dtypes
import numpy as np
from jax import lax
from jax.experimental import pallas as pl
from jax.experimental.pallas import tpu as pltpu
from jax.sharding import PartitionSpec as P

EPSILON = 1e-05
ROOT = 0.7978845608028654
CUBIC = 0.044715
AXES = ("node", "chip", "core")
ROW = 16
F32 = jnp.float32
BF16 = jnp.bfloat16


def split(table):
    high = table.astype(ml_dtypes.bfloat16)
    low = (table - high.astype(np.float64)).astype(ml_dtypes.bfloat16)
    return high, low


@functools.lru_cache(maxsize=None)
def wave_tables(canvas, side_large, side_small):
    period = 2 * canvas - 1
    pairs = [(0, v) for v in range(canvas)]
    pairs += [(u, v) for u in range(1, canvas) for v in range(period)]
    waves = np.array(pairs)
    half = -(-len(pairs) // 16) * 16

    def table(places_h, places_w, keep, sign):
        grid = np.stack(np.meshgrid(places_h, places_w, indexing="ij"), -1).reshape(-1, 2)
        angle = 2 * np.pi * ((waves @ grid.T) % period) / period
        out = np.zeros((2 * half, grid.shape[0]))
        out[: len(pairs)] = np.cos(angle) * keep
        out[half : half + len(pairs)] = sign * np.sin(angle) * keep
        return out

    share = np.zeros((2 * half, 1))
    share[: len(pairs)] = 2.0 / period**2
    share[half : half + len(pairs)] = 2.0 / period**2
    share[0] = 1.0 / period**2

    inside = (np.arange(ROW) < canvas).astype(np.float64)
    cells = table(np.arange(canvas), np.arange(ROW), np.tile(inside, canvas), -1.0)

    def taps(side, row):
        middle = (side - 1) // 2
        offsets_h = np.arange(side) - middle
        offsets_w = np.arange(row) - middle
        keep = (np.abs(offsets_h) < canvas)[:, None] & (np.abs(offsets_w) < canvas)[None, :]
        keep = keep & (np.arange(row) < side)[None, :]
        return table(offsets_h, offsets_w, keep.reshape(-1).astype(np.float64), 1.0)

    def taps_back(side):
        first, count = used_rows(side, canvas)
        every = taps(side, side).reshape(2 * half, side, side)
        used = every[:, first : first + count, first : first + count].reshape(2 * half, -1)
        return np.pad(used, ((0, 0), (0, -used.shape[1] % 8)))

    def tap_row(side):
        return -(-side // 16) * 16

    large = taps(side_large, tap_row(side_large))
    small = taps(side_small, tap_row(side_small))
    turn = np.ones((2 * half, 1))
    turn[half:] = -1.0
    return dict(
        half=half,
        ahead=split(cells),
        back=split((cells * share).T),
        large=split(large),
        small=split(small),
        large_back=split((taps_back(side_large) * turn * share).T),
        small_back=split((taps_back(side_small) * turn * share).T),
    )


def used_rows(side, canvas):
    first = max(0, (side - 1) // 2 - (canvas - 1))
    return first, side - 2 * first


def dot(left, right):
    return jnp.dot(left, right, preferred_element_type=F32)


def dot_nt(left, right):
    return lax.dot_general(left, right, (((1,), (1,)), ((), ())), preferred_element_type=F32)


def dot_tn(left, right):
    return lax.dot_general(left, right, (((0,), (0,)), ((), ())), preferred_element_type=F32)


def halves(values):
    high = values.astype(BF16)
    return high, (values - high.astype(F32)).astype(BF16)


def gelu(values):
    inner = values * (ROOT + (ROOT * CUBIC) * (values * values))
    return values * (0.5 + 0.5 * jnp.tanh(inner))


def gelu_slope(values):
    square = values * values
    bend = jnp.tanh(values * (ROOT + (ROOT * CUBIC) * square))
    slope = ROOT + (3.0 * ROOT * CUBIC) * square
    return 0.5 + 0.5 * bend + values * slope * (0.5 - 0.5 * bend * bend)


def rows(at):
    return pl.ds(pl.multiple_of(at * ROW, ROW), ROW)


def fold(values):
    return values[:8] + values[8:]


def twice(values):
    return jnp.concatenate([values, values], axis=0)


def columns_inside(side, channels):
    places = lax.broadcasted_iota(jnp.int32, (ROW, 128), 0)
    inside = (places < side).astype(F32)
    return jnp.concatenate([inside] * (channels // 128), axis=1)


def first_step():
    return pl.program_id(0) == 0


def last_step():
    return pl.program_id(0) == pl.num_programs(0) - 1


def to_tiles(parts):
    lines = [part[:, at : at + 128] for part in parts for at in range(0, part.shape[1], 128)]
    lines += [jnp.zeros_like(lines[0])] * (-len(lines) % 8)
    return jnp.concatenate(lines, axis=0)


def from_tiles(tiles, count, width):
    tiles = [tiles[at : at + 1] for at in range(count * width // 128)]
    many = width // 128
    return [jnp.concatenate(tiles[at * many : (at + 1) * many], axis=1) for at in range(count)]


def received(sent, count, width):
    return from_tiles(jnp.sum(sent[...], axis=0), count, width)


def keep(coefs, values):
    for at, value in enumerate(values):
        coefs[at] = jnp.broadcast_to(value, coefs.shape[1:])


def note(out, values):
    values = list(values)
    values += [jnp.zeros_like(values[0])] * (out.shape[0] - len(values))
    out[...] = jnp.concatenate(values, axis=0)


def add_sums(sums, parts):
    @pl.when(first_step())
    def _():
        sums[...] = jnp.zeros_like(sums)

    for at, part in enumerate(parts):
        sums[at] += part


def publish(sums, out, extra=()):
    @pl.when(last_step())
    def _():
        parts = [jnp.sum(sums[at], axis=0, keepdims=True) for at in range(sums.shape[0])]
        parts += list(extra)
        out[...] = jnp.broadcast_to(to_tiles(parts)[None], out.shape)


def norm_coefs(column_sum, square, count, scaling, offsets):
    mean = column_sum / count
    reciprocal = lax.rsqrt(square / count - mean * mean + EPSILON)
    factor = scaling * reciprocal
    return mean, reciprocal, factor, offsets - mean * factor


def back_coefs(shift_sum, gain_sum, count, mean, reciprocal, scaling):
    factor = scaling * reciprocal
    slope = factor * reciprocal * gain_sum / count
    return factor, factor * shift_sum / count - slope * mean, slope


def zeros(count, channels):
    return tuple(jnp.zeros((8, channels), F32) for _ in range(count))


def enter_stage(sides, image, cotangent, x_out, u_out, sent, padded, sums):
    at_crop = pl.program_id(0)
    side = sides[at_crop]
    canvas, channels = image.shape[1], image.shape[3]
    inside = columns_inside(side, channels)

    @pl.when(first_step())
    def _():
        padded[...] = jnp.zeros_like(padded)

    def step(at, carry):
        mask = jnp.where(at < side, inside, 0.0)
        start = pl.multiple_of(at * ROW, ROW)
        padded[0, pl.ds(start, canvas), :] = image[0, at].astype(F32)
        padded[1, pl.ds(start, canvas), :] = cotangent[0, at].astype(F32)
        x = padded[0, rows(at), :] * mask
        u = padded[1, rows(at), :] * mask
        x_out[rows(at), :] = x.astype(BF16)
        u_out[rows(at), :] = u.astype(BF16)
        return carry[0] + fold(x), carry[1] + fold(x * x)

    add_sums(sums, lax.fori_loop(0, canvas, step, zeros(2, channels), unroll=14))
    count = jnp.int32(0)
    for at in range(sides.shape[0]):
        count += sides[at] * sides[at]
    publish(sums, sent, [jnp.full((1, 128), count.astype(F32))])


def first_stage(sides, came, scale, offset, x_in, weight, low_out, pre_out, sent, seen, coefs, sums):
    channels = x_in.shape[1]
    canvas = x_in.shape[0] // ROW
    side = sides[pl.program_id(0)]

    @pl.when(first_step())
    def _():
        tiles = channels // 128
        parts = received(came, 2 * tiles + 1, 128)
        column_sum = jnp.concatenate(parts[:tiles], axis=1)
        square = jnp.concatenate(parts[tiles : 2 * tiles], axis=1)
        count = jnp.concatenate([parts[2 * tiles]] * tiles, axis=1)
        mean, reciprocal, factor, constant = norm_coefs(column_sum, square, count, scale[0:1], offset[0:1])
        keep(coefs, [factor, constant])
        note(seen, [count, mean, reciprocal, column_sum, square])

    inside = columns_inside(side, channels)
    factor, constant = twice(coefs[0]), twice(coefs[1])

    def step(at, carry):
        mask = jnp.where(at < side, inside, 0.0)
        low_out[rows(at), :] = (mask * (factor * x_in[rows(at), :].astype(F32) + constant)).astype(BF16)
        return carry

    lax.fori_loop(0, canvas, step, 0, unroll=14)
    pre_out[...] = dot(low_out[...], weight[...])

    def measure(at, carry):
        pre = pre_out[rows(at), :]
        return carry[0] + fold(pre), carry[1] + fold(pre * pre)

    add_sums(sums, lax.fori_loop(0, canvas, measure, zeros(2, channels), unroll=14))
    publish(sums, sent)


def times(spectrum, kernel, half, at, conj):
    real, imag = pl.ds(pl.multiple_of(at * 16, 16), 16), pl.ds(pl.multiple_of(half + at * 16, 16), 16)
    a, b = spectrum[real, :], spectrum[imag, :]
    c, d = kernel[real, :], kernel[imag, :]
    if conj:
        return real, imag, a * c + b * d, b * c - a * d
    return real, imag, a * c - b * d, a * d + b * c


def ahead_once(tables, values):
    return dot(tables[0][...], values)


def back_once(tables, values):
    return dot(tables[0][...], values.astype(BF16))


def ahead(tables, values):
    return dot(tables[0][...], values) + dot(tables[1][...], values)


def back(tables, high, low):
    return dot(tables[0][...], high) + dot(tables[0][...], low) + dot(tables[1][...], high)


def mixer_stage(
    sides, came, seen, scale, offset, pre_in, ahead_t, back_t, large_w, small_w,
    low_out, large_out, small_out, waves_out, sent, noted, coefs, sums, spectrum, high, low,
):
    channels = pre_in.shape[1]
    canvas = pre_in.shape[0] // ROW
    half = spectrum.shape[0] // 2
    side = sides[pl.program_id(0)]

    @pl.when(first_step())
    def _():
        mean, reciprocal, factor, constant = norm_coefs(
            *received(came, 2, channels), seen[0:1], scale[1:2], offset[1:2]
        )
        keep(coefs, [factor, constant])
        note(noted, [mean, reciprocal])

    inside = columns_inside(side, channels)
    factor, constant = twice(coefs[0]), twice(coefs[1])

    def step(at, carry):
        mask = jnp.where(at < side, inside, 0.0)
        low_out[rows(at), :] = gelu(mask * (factor * pre_in[rows(at), :] + constant)).astype(BF16)
        return carry

    lax.fori_loop(0, canvas, step, 0, unroll=14)
    spectrum[...] = ahead(ahead_t, low_out[...])
    waves_out[...] = spectrum[...].astype(BF16)
    parts = ()
    for kernel, out in ((large_w, large_out), (small_w, small_out)):

        def product(at, carry):
            real, imag, new_real, new_imag = times(spectrum, kernel, half, at, False)
            high[real, :], low[real, :] = halves(new_real)
            high[imag, :], low[imag, :] = halves(new_imag)
            return carry

        lax.fori_loop(0, half // 16, product, 0, unroll=4)
        out[...] = back(back_t, high[...], low[...])

        def measure(at, carry):
            conv = jnp.where(at < side, inside, 0.0) * out[rows(at), :]
            out[rows(at), :] = conv
            return carry[0] + fold(conv), carry[1] + fold(conv * conv)

        parts += lax.fori_loop(0, canvas, measure, zeros(2, channels), unroll=14)
    add_sums(sums, parts)
    publish(sums, sent)


def merge_stage(
    sides, came, seen, scale, offset, large_in, small_in, x_in, u_in, weight,
    low_out, proj_out, sent, noted, coefs, sums,
):
    channels = x_in.shape[1]
    canvas = x_in.shape[0] // ROW
    side = sides[pl.program_id(0)]

    @pl.when(first_step())
    def _():
        large_sum, large_square, small_sum, small_square = received(came, 4, channels)
        large = norm_coefs(large_sum, large_square, seen[0:1], scale[2:3], offset[2:3])
        small = norm_coefs(small_sum, small_square, seen[0:1], scale[3:4], offset[3:4])
        keep(coefs, [large[2], small[2], large[3] + small[3]])
        note(noted, [large[0], large[1], small[0], small[1], large[2], small[2], large[3] + small[3]])

    inside = columns_inside(side, channels)
    large, small, constant = twice(coefs[0]), twice(coefs[1]), twice(coefs[2])

    def step(at, carry):
        mask = jnp.where(at < side, inside, 0.0)
        merged = mask * (large * large_in[rows(at), :] + small * small_in[rows(at), :] + constant)
        low_out[rows(at), :] = gelu(merged).astype(BF16)
        return carry

    lax.fori_loop(0, canvas, step, 0, unroll=14)
    proj_out[...] = dot(low_out[...], weight[...])

    def measure(at, carry):
        proj = proj_out[rows(at), :]
        x, u = x_in[rows(at), :].astype(F32), u_in[rows(at), :].astype(F32)
        parts = (proj, proj * proj, proj * x, proj * u)
        return tuple(old + fold(part) for old, part in zip(carry, parts))

    add_sums(sums, lax.fori_loop(0, canvas, measure, zeros(4, channels), unroll=7))
    publish(sums, sent)


def widen_stage(
    sides, core, came, seen, scale, offset, x_in, proj_in, weight,
    low_out, hidden_out, mine, other, noted, coefs, sums, found,
):
    channels = x_in.shape[1]
    canvas = x_in.shape[0] // ROW
    side = sides[pl.program_id(0)]

    @pl.when(first_step())
    def _():
        proj_sum, proj_square, cross, _ = parts = received(came, 4, channels)
        count, x_mean, x_sum, x_square = seen[0:1], seen[1:2], seen[3:4], seen[4:5]
        mean, reciprocal, factor, constant = norm_coefs(
            proj_sum, proj_square, count, scale[4:5], offset[4:5]
        )
        mid_mean = x_mean + factor * mean + constant
        x_var = x_square / count - x_mean * x_mean
        proj_var = proj_square / count - mean * mean
        both = cross / count - x_mean * mean
        mid_var = x_var + factor * factor * proj_var + 2.0 * factor * both
        mid_reciprocal = lax.rsqrt(mid_var + EPSILON)
        mid_factor = scale[5:6] * mid_reciprocal
        keep(coefs, [mid_factor, mid_factor * factor, mid_factor * (constant - mid_mean) + offset[5:6]])
        note(noted, [mean, reciprocal, mid_mean, mid_reciprocal] + parts)

    inside = columns_inside(side, channels)
    from_x, from_proj, constant = twice(coefs[0]), twice(coefs[1]), twice(coefs[2])

    def step(at, carry):
        mask = jnp.where(at < side, inside, 0.0)
        x = x_in[rows(at), :].astype(F32)
        low_out[rows(at), :] = (mask * (from_x * x + from_proj * proj_in[rows(at), :] + constant)).astype(BF16)
        return carry

    lax.fori_loop(0, canvas, step, 0, unroll=14)
    parts = [[], []]
    for at_block in range(hidden_out.shape[1] // channels):
        block = slice(at_block * channels, (at_block + 1) * channels)
        found[...] = dot(low_out[...], weight[:, block])

        def measure(at, carry):
            hidden = found[rows(at), :]
            hidden_out[rows(at), block] = hidden.astype(BF16)
            return carry[0] + fold(hidden), carry[1] + fold(hidden * hidden)

        pair = lax.fori_loop(0, canvas, measure, zeros(2, channels), unroll=14)
        parts[0].append(pair[0])
        parts[1].append(pair[1])
    add_sums(sums, [jnp.concatenate(part, axis=1) for part in parts])
    hand_over(sums, core, mine, other)


def hand_over(sums, core, mine, other):
    @pl.when(last_step())
    def _():
        first, second = (to_tiles([jnp.sum(sums[at], axis=0, keepdims=True)]) for at in range(2))
        mine[...] = jnp.where(core[0] == 0, first, second)
        other[...] = jnp.where(core[0] == 0, second, first)


def taken_over(core, came):
    mine, other = came[0][...], came[1][...]
    wide = mine.size
    first = jnp.where(core[0] == 0, mine, other)
    second = jnp.where(core[0] == 0, other, mine)
    return from_tiles(first, 1, wide)[0], from_tiles(second, 1, wide)[0]


def narrow_stage(
    sides, core, came, seen, wide_scale, wide_offset, hidden_in, u_in, weight,
    low_out, proj_out, sent, noted, coefs, sums,
):
    channels = u_in.shape[1]
    canvas = u_in.shape[0] // ROW
    wide = hidden_in.shape[1]
    side = sides[pl.program_id(0)]

    @pl.when(first_step())
    def _():
        count = jnp.concatenate([seen[0:1]] * (wide // channels), axis=1)
        mean, reciprocal, factor, constant = norm_coefs(
            *taken_over(core, came), count, wide_scale[...], wide_offset[...]
        )
        keep(coefs, [factor, constant])
        note(noted, [mean, reciprocal, factor, constant, count])

    for at_block in range(wide // channels):
        block = slice(at_block * channels, (at_block + 1) * channels)
        factor, constant = twice(coefs[0, :, block]), twice(coefs[1, :, block])

        def step(at, carry):
            hidden = hidden_in[rows(at), block].astype(F32)
            low_out[rows(at), block] = gelu(factor * hidden + constant).astype(BF16)
            return carry

        lax.fori_loop(0, canvas, step, 0, unroll=14)
    proj_out[...] = dot(low_out[...], weight[...])
    inside = columns_inside(side, channels)

    def measure(at, carry):
        proj = jnp.where(at < side, inside, 0.0) * proj_out[rows(at), :]
        proj_out[rows(at), :] = proj
        u = u_in[rows(at), :].astype(F32)
        parts = (proj, proj * proj, proj * u, u)
        return tuple(old + fold(part) for old, part in zip(carry, parts))

    add_sums(sums, lax.fori_loop(0, canvas, measure, zeros(4, channels), unroll=7))
    publish(sums, sent)


def wide_back_stage(
    sides, core, came, seen, wide_seen, scale, offset, proj_in, u_in, hidden_in, weight,
    down_out, grad_out, mine, other, noted, coefs, sums, found,
):
    channels = u_in.shape[1]
    canvas = u_in.shape[0] // ROW
    wide = hidden_in.shape[1]
    side = sides[pl.program_id(0)]

    @pl.when(first_step())
    def _():
        proj_sum, proj_square, cross, u_sum = received(came, 4, channels)
        count = seen[0:1]
        mean, reciprocal, factor, constant = norm_coefs(
            proj_sum, proj_square, count, scale[6:7], offset[6:7]
        )
        gain_sum = reciprocal * (cross - mean * u_sum)
        keep(coefs, back_coefs(u_sum, gain_sum, count, mean, reciprocal, scale[6:7]))
        note(noted, [mean, reciprocal, u_sum, gain_sum, factor, constant])

    inside = columns_inside(side, channels)
    factor, constant, slope = twice(coefs[0]), twice(coefs[1]), twice(coefs[2])

    def step(at, carry):
        mask = jnp.where(at < side, inside, 0.0)
        u = u_in[rows(at), :].astype(F32)
        down_out[rows(at), :] = (mask * (factor * u - constant - slope * proj_in[rows(at), :])).astype(BF16)
        return carry

    lax.fori_loop(0, canvas, step, 0, unroll=14)
    parts = [[], []]
    for at_block in range(wide // channels):
        block = slice(at_block * channels, (at_block + 1) * channels)
        found[...] = dot(down_out[...], weight[:, block])
        wide_factor = jnp.broadcast_to(wide_seen[2:3, block], (ROW, channels))
        wide_constant = jnp.broadcast_to(wide_seen[3:4, block], (ROW, channels))

        def measure(at, carry):
            hidden = hidden_in[rows(at), block].astype(F32)
            grad = found[rows(at), :] * gelu_slope(wide_factor * hidden + wide_constant)
            grad_out[rows(at), block] = grad.astype(BF16)
            return carry[0] + fold(grad), carry[1] + fold(grad * hidden)

        pair = lax.fori_loop(0, canvas, measure, zeros(2, channels), unroll=7)
        parts[0].append(pair[0])
        parts[1].append(pair[1])
    add_sums(sums, [jnp.concatenate(part, axis=1) for part in parts])
    hand_over(sums, core, mine, other)


def narrow_back_stage(
    sides, core, came, wide_seen, wide_scale, grad_in, hidden_in, x_in, proj_in, weight,
    up_out, ffn_out, sent, noted, coefs, sums,
):
    channels = x_in.shape[1]
    canvas = x_in.shape[0] // ROW
    wide = hidden_in.shape[1]
    side = sides[pl.program_id(0)]

    @pl.when(first_step())
    def _():
        mean, reciprocal, count = wide_seen[0:1], wide_seen[1:2], wide_seen[4:5]
        shift_sum, with_hidden = taken_over(core, came)
        gain_sum = reciprocal * (with_hidden - mean * shift_sum)
        keep(coefs, back_coefs(shift_sum, gain_sum, count, mean, reciprocal, wide_scale[...]))
        note(noted, [gain_sum, shift_sum])

    for at_block in range(wide // channels):
        block = slice(at_block * channels, (at_block + 1) * channels)
        factor, constant, slope = (twice(coefs[at, :, block]) for at in range(3))

        def step(at, carry):
            grad = factor * grad_in[rows(at), block].astype(F32) - constant
            grad = grad - slope * hidden_in[rows(at), block].astype(F32)
            up_out[rows(at), block] = grad.astype(BF16)
            return carry

        lax.fori_loop(0, canvas, step, 0, unroll=14)
    ffn_out[...] = dot(up_out[...], weight[...])
    inside = columns_inside(side, channels)

    def measure(at, carry):
        grad = jnp.where(at < side, inside, 0.0) * ffn_out[rows(at), :]
        ffn_out[rows(at), :] = grad
        parts = (grad, grad * x_in[rows(at), :].astype(F32), grad * proj_in[rows(at), :])
        return tuple(old + fold(part) for old, part in zip(carry, parts))

    add_sums(sums, lax.fori_loop(0, canvas, measure, zeros(3, channels), unroll=7))
    publish(sums, sent)


def mid_back_stage(
    sides, came, seen, merge_seen, mid_seen, last_seen, scale, offset,
    x_in, u_in, proj_in, ffn_in, large_in, small_in, weight,
    resid_out, back_out, grad_out, sent, noted, coefs, sums,
):
    channels = x_in.shape[1]
    canvas = x_in.shape[0] // ROW
    side = sides[pl.program_id(0)]

    @pl.when(first_step())
    def _():
        ffn_sum, ffn_x, ffn_proj = received(came, 3, channels)
        count, u_sum = seen[0:1], last_seen[2:3]
        mean, reciprocal, mid_mean, mid_reciprocal = (mid_seen[at : at + 1] for at in range(4))
        proj_sum, proj_square, cross, proj_u = (mid_seen[at : at + 1] for at in range(4, 8))
        proj_factor = scale[4:5] * reciprocal
        proj_constant = offset[4:5] - mean * proj_factor
        ffn_mid = ffn_x + proj_factor * ffn_proj + proj_constant * ffn_sum
        mid_gain = mid_reciprocal * (ffn_mid - mid_mean * ffn_sum)
        factor, constant, slope = back_coefs(ffn_sum, mid_gain, count, mid_mean, mid_reciprocal, scale[5:6])
        mid_proj = cross + proj_factor * proj_square + proj_constant * proj_sum
        resid_sum = u_sum
        resid_proj = proj_u + factor * ffn_proj - constant * proj_sum - slope * mid_proj
        gain = reciprocal * (resid_proj - mean * resid_sum)
        second = back_coefs(resid_sum, gain, count, mean, reciprocal, scale[4:5])
        keep(coefs, [factor, constant + slope * proj_constant, slope, slope * proj_factor, *second])
        note(noted, [mid_gain, ffn_sum, gain, resid_sum])

    inside = columns_inside(side, channels)

    def step(at, carry):
        mask = jnp.where(at < side, inside, 0.0)
        x, u = x_in[rows(at), :].astype(F32), u_in[rows(at), :].astype(F32)
        proj = proj_in[rows(at), :]
        resid = twice(coefs[0]) * ffn_in[rows(at), :] - twice(coefs[1]) - twice(coefs[2]) * x
        resid = u + mask * (resid - twice(coefs[3]) * proj)
        resid_out[rows(at), :] = resid
        down = twice(coefs[4]) * resid - twice(coefs[5]) - twice(coefs[6]) * proj
        back_out[rows(at), :] = (mask * down).astype(BF16)
        return carry

    lax.fori_loop(0, canvas, step, 0, unroll=14)
    grad_out[...] = dot(back_out[...], weight[...])
    large = jnp.broadcast_to(merge_seen[4:5], (ROW, channels))
    small = jnp.broadcast_to(merge_seen[5:6], (ROW, channels))
    constant = jnp.broadcast_to(merge_seen[6:7], (ROW, channels))

    def measure(at, carry):
        large_conv, small_conv = large_in[rows(at), :], small_in[rows(at), :]
        grad = grad_out[rows(at), :] * gelu_slope(large * large_conv + small * small_conv + constant)
        grad_out[rows(at), :] = grad
        parts = (grad, grad * large_conv, grad * small_conv)
        return tuple(old + fold(part) for old, part in zip(carry, parts))

    add_sums(sums, lax.fori_loop(0, canvas, measure, zeros(3, channels), unroll=7))
    publish(sums, sent)


def mixer_back_stage(
    sides, came, seen, merge_seen, first_seen, scale, offset, large_in, small_in, grad_in, pre_in, waves_in,
    ahead_t, back_t, large_w, small_w,
    grad_out, large_sum, small_sum, sent, noted, coefs, sums, large_out, small_out, large_s, small_s, summed,
):
    channels = pre_in.shape[1]
    canvas = pre_in.shape[0] // ROW
    half = large_s.shape[0] // 2
    side = sides[pl.program_id(0)]

    @pl.when(first_step())
    def _():
        shift_sum, with_large, with_small = received(came, 3, channels)
        count = seen[0:1]
        large_mean, large_r, small_mean, small_r = (merge_seen[at : at + 1] for at in range(4))
        large_gain = large_r * (with_large - large_mean * shift_sum)
        small_gain = small_r * (with_small - small_mean * shift_sum)
        keep(
            coefs,
            [
                *back_coefs(shift_sum, large_gain, count, large_mean, large_r, scale[2:3]),
                *back_coefs(shift_sum, small_gain, count, small_mean, small_r, scale[3:4]),
            ],
        )
        note(noted, [large_gain, small_gain, shift_sum])

    inside = columns_inside(side, channels)

    def step(at, carry):
        mask = jnp.where(at < side, inside, 0.0)
        grad = grad_in[rows(at), :]
        large = twice(coefs[0]) * grad - twice(coefs[1]) - twice(coefs[2]) * large_in[rows(at), :]
        small = twice(coefs[3]) * grad - twice(coefs[4]) - twice(coefs[5]) * small_in[rows(at), :]
        large_out[rows(at), :] = (mask * large).astype(BF16)
        small_out[rows(at), :] = (mask * small).astype(BF16)
        return carry

    lax.fori_loop(0, canvas, step, 0, unroll=14)
    large_s[...] = ahead_once(ahead_t, large_out[...])
    small_s[...] = ahead_once(ahead_t, small_out[...])

    def product(at, carry):
        real, imag, one_real, one_imag = times(large_s, large_w, half, at, True)
        _, _, two_real, two_imag = times(small_s, small_w, half, at, True)
        summed[real, :] = (one_real + two_real).astype(BF16)
        summed[imag, :] = (one_imag + two_imag).astype(BF16)
        a, b = waves_in[real, :].astype(F32), waves_in[imag, :].astype(F32)
        for total, spectrum in ((large_sum, large_s), (small_sum, small_s)):
            c, d = spectrum[real, :], spectrum[imag, :]
            total[real, :] += a * c + b * d
            total[imag, :] += b * c - a * d
        return carry

    @pl.when(first_step())
    def _():
        large_sum[...] = jnp.zeros_like(large_sum)
        small_sum[...] = jnp.zeros_like(small_sum)

    lax.fori_loop(0, half // 16, product, 0, unroll=4)
    grad_out[...] = back_once(back_t, summed[...])
    reciprocal = first_seen[1:2]
    factor = scale[1:2] * reciprocal
    constant = jnp.broadcast_to(offset[1:2] - first_seen[0:1] * factor, (ROW, channels))
    factor = jnp.broadcast_to(factor, (ROW, channels))

    def measure(at, carry):
        mask = jnp.where(at < side, inside, 0.0)
        pre = pre_in[rows(at), :]
        grad = mask * grad_out[rows(at), :] * gelu_slope(factor * pre + constant)
        grad_out[rows(at), :] = grad
        return carry[0] + fold(grad), carry[1] + fold(grad * pre)

    add_sums(sums, lax.fori_loop(0, canvas, measure, zeros(2, channels), unroll=7))
    publish(sums, sent)


def first_back_stage(
    sides, came, seen, first_seen, scale, grad_in, pre_in, x_in, weight,
    low_out, grad_out, sent, noted, coefs, sums,
):
    channels = pre_in.shape[1]
    canvas = pre_in.shape[0] // ROW
    side = sides[pl.program_id(0)]

    @pl.when(first_step())
    def _():
        shift_sum, with_pre = received(came, 2, channels)
        mean, reciprocal = first_seen[0:1], first_seen[1:2]
        gain_sum = reciprocal * (with_pre - mean * shift_sum)
        keep(coefs, back_coefs(shift_sum, gain_sum, seen[0:1], mean, reciprocal, scale[1:2]))
        note(noted, [gain_sum, shift_sum])

    inside = columns_inside(side, channels)
    factor, constant, slope = twice(coefs[0]), twice(coefs[1]), twice(coefs[2])

    def step(at, carry):
        mask = jnp.where(at < side, inside, 0.0)
        grad = factor * grad_in[rows(at), :] - constant - slope * pre_in[rows(at), :]
        low_out[rows(at), :] = (mask * grad).astype(BF16)
        return carry

    lax.fori_loop(0, canvas, step, 0, unroll=14)
    grad_out[...] = dot(low_out[...], weight[...])

    def measure(at, carry):
        grad = grad_out[rows(at), :]
        return carry[0] + fold(grad), carry[1] + fold(grad * x_in[rows(at), :].astype(F32))

    add_sums(sums, lax.fori_loop(0, canvas, measure, zeros(2, channels), unroll=14))
    publish(sums, sent)


def leave_stage(sides, came, seen, scale, resid_in, grad_in, x_in, image_out, noted, coefs):
    channels = x_in.shape[1]
    canvas = x_in.shape[0] // ROW
    side = sides[pl.program_id(0)]

    @pl.when(first_step())
    def _():
        shift_sum, with_x = received(came, 2, channels)
        count, mean, reciprocal = (seen[at : at + 1] for at in range(3))
        gain_sum = reciprocal * (with_x - mean * shift_sum)
        keep(coefs, back_coefs(shift_sum, gain_sum, count, mean, reciprocal, scale[0:1]))
        note(noted, [gain_sum, shift_sum])

    inside = columns_inside(side, channels)
    factor, constant, slope = twice(coefs[0]), twice(coefs[1]), twice(coefs[2])

    def step(at, carry):
        mask = jnp.where(at < side, inside, 0.0)
        grad = factor * grad_in[rows(at), :] - constant - slope * x_in[rows(at), :].astype(F32)
        image_out[0, at] = (mask * (resid_in[rows(at), :] + grad))[:canvas]
        return carry

    lax.fori_loop(0, canvas, step, 0, unroll=14)


def block_out_stage(sides, mid_seen, last_seen, scale, offset, x_in, mid_in, last_in, out):
    channels = x_in.shape[1]
    canvas = x_in.shape[0] // ROW
    side = sides[pl.program_id(0)]
    inside = columns_inside(side, channels)
    factor = scale[4:5] * mid_seen[1:2]
    constant = offset[4:5] - mid_seen[0:1] * factor + last_seen[5:6]
    constant = jnp.broadcast_to(constant, (ROW, channels))
    factor = jnp.broadcast_to(factor, (ROW, channels))
    last = jnp.broadcast_to(last_seen[4:5], (ROW, channels))

    def step(at, carry):
        mask = jnp.where(at < side, inside, 0.0)
        added = factor * mid_in[rows(at), :] + last * last_in[rows(at), :] + constant
        out[0, at] = (x_in[rows(at), :].astype(F32) + mask * added)[:canvas].astype(BF16)
        return carry

    lax.fori_loop(0, canvas, step, 0, unroll=14)


def kernel_waves_stage(large, small, large_t, small_t, large_out, small_out, large_rows, small_rows):
    for kernel, table, out, flat in (
        (large, large_t, large_out, large_rows),
        (small, small_t, small_out, small_rows),
    ):
        side = kernel.shape[0]
        row = flat.shape[0] // side
        flat[...] = jnp.zeros_like(flat)
        for at in range(side):
            flat[at * row : at * row + side, :] = kernel[at]
        out[...] = ahead(table, flat[...])


def kernel_grad_stage(
    place, merged, merged_grad, large_sum, small_sum, large_t, small_t, other_out, mine_out, flat, proj_sum
):
    proj_sum[...] = dot_tn(merged[...], merged_grad[...])
    start = 0
    for total, table in ((large_sum, large_t), (small_sum, small_t)):
        size = table[0].shape[0]
        flat[start : start + size, :] = back(table, *halves(total[...]))
        start += size
    if start < flat.shape[0]:
        flat[start:, :] = jnp.zeros((flat.shape[0] - start, flat.shape[1]), F32)
    size, rest = flat.shape[0] // 2, proj_sum.shape[0] // 2
    for out, core in ((mine_out, place[0]), (other_out, 1 - place[0])):
        out[:size, :] = flat[pl.ds(pl.multiple_of(core * size, 8), size), :]
        out[size:, :] = proj_sum[pl.ds(pl.multiple_of(core * rest, 8), rest), :]


def kernel_grad_out_stage(settled, large_out, small_out, proj_out, flat, *, canvas):
    rest = proj_out.shape[0] // 2
    size = settled.shape[0] // 2 - rest
    for core in range(2):
        start = core * (size + rest)
        flat[core * size : (core + 1) * size, :] = settled[start : start + size, :]
        proj_out[core * rest : (core + 1) * rest, :] = settled[start + size : start + size + rest, :]
    start = 0
    for out in (large_out, small_out):
        side = out.shape[0]
        first, count = used_rows(side, canvas)
        out[...] = jnp.zeros_like(out)
        for at in range(first, first + count):
            out[at, first : first + count, :] = flat[start : start + count, :]
            start += count
        start = -(-start // 8) * 8


def weight_grad_stage(place, inputs, gradient, out):
    out[...] = dot_tn(inputs[...], gradient[...])


SMEM = pl.BlockSpec(memory_space=pltpu.SMEM)


def whole(shape):
    return pl.BlockSpec(shape, lambda at: (0,) * len(shape))


VMEM = 36 * 1024 * 1024


def call(kernel, crops, ins, outs, scratch):
    def spec(shape, kind):
        if kind == "smem":
            return SMEM
        if kind == "rows":
            return pl.BlockSpec((shape[0] // crops, shape[1]), lambda at: (at, 0))
        if kind == "map":
            return pl.BlockSpec((1,) + tuple(shape[1:]), lambda at: (at, 0, 0, 0))
        return whole(tuple(shape))

    flat, specs, places = [], [], []
    for value, kind in ins:
        group = value if isinstance(value, tuple) else (value,)
        places.append((len(flat), len(group) if isinstance(value, tuple) else 0))
        for part in group:
            if kind == "rows":
                part = pltpu.with_memory_space_constraint(part, pltpu.HBM)
            flat.append(part)
            specs.append(spec(part.shape, kind))

    def body(*refs):
        given = [refs[at : at + size] if size else refs[at] for at, size in places]
        kernel(*given, *refs[len(flat) :])

    return pl.pallas_call(
        body,
        grid=(crops,),
        in_specs=specs,
        out_specs=[spec(shape, kind) for shape, _, kind in outs],
        out_shape=[
            (pltpu.HBM if kind == "rows" else jax.ShapeDtypeStruct)(shape, dtype) for shape, dtype, kind in outs
        ],
        scratch_shapes=[pltpu.VMEM(shape, dtype) for shape, dtype in scratch],
        compiler_params=pltpu.CompilerParams(
            dimension_semantics=("arbitrary",), vmem_limit_bytes=VMEM
        ),
        cost_estimate=pl.CostEstimate(
            flops=0,
            bytes_accessed=sum(math.prod(part.shape) * part.dtype.itemsize for part in flat)
            + sum(math.prod(shape) * jnp.dtype(dtype).itemsize for shape, dtype, _ in outs),
            transcendentals=0,
        ),
        name=getattr(kernel, "func", kernel).__name__,
    )(*flat)


def weight_grad(inputs, gradient, place=None):
    deep, high = inputs.shape
    wide = gradient.shape[1]
    large = place is None
    if large:
        place = jnp.zeros((1,), jnp.int32)
        inputs = pltpu.with_memory_space_constraint(inputs, pltpu.HBM)
        gradient = pltpu.with_memory_space_constraint(gradient, pltpu.HBM)
    else:
        high = high // 2
    block, across = min(high, 512), min(wide, 512)
    return pl.pallas_call(
        weight_grad_stage,
        grid_spec=pltpu.PrefetchScalarGridSpec(
            num_scalar_prefetch=1,
            grid=(high // block, wide // across),
            in_specs=[
                pl.BlockSpec((deep, block), lambda i, j, place: (0, place[0] * (high // block) + i)),
                pl.BlockSpec((deep, across), lambda i, j, place: (0, j)),
            ],
            out_specs=pl.BlockSpec((block, across), lambda i, j, place: (i, j)),
        ),
        out_shape=pltpu.HBM((high, wide), F32) if large else jax.ShapeDtypeStruct((high, wide), F32),
        compiler_params=pltpu.CompilerParams(
            dimension_semantics=("arbitrary", "arbitrary"), vmem_limit_bytes=VMEM
        ),
        cost_estimate=pl.CostEstimate(
            flops=2 * deep * high * wide,
            bytes_accessed=2 * deep * (high + wide) + 4 * high * wide,
            transcendentals=0,
        ),
        name="weight_grad_stage",
    )(place, inputs, gradient)


def exchange(sent):
    return lax.all_to_all(sent, AXES, 0, 0, tiled=True)


SWAP = [(0, 1), (1, 0)]


def wide_exchange(mine, other, *beside):
    mine = mine + lax.ppermute(other, "core", SWAP)
    chips = lax.axis_size(("node", "chip"))
    copies = jnp.broadcast_to(mine[None], (chips,) + mine.shape)
    mine = jnp.sum(together(lax.all_to_all(copies, ("node", "chip"), 0, 0, tiled=True), *beside), axis=0)
    return mine, lax.ppermute(mine, "core", SWAP)


def sum_and_cut(arrays, place, ways):
    count, wide = arrays[0].shape
    part = count // ways

    def body(place, *refs):
        total = refs[0][...]
        for ref in refs[1 : len(arrays)]:
            total = total + ref[...]
        for at, out in enumerate(refs[len(arrays) :]):

            @pl.when(pl.program_id(0) == at)
            def _():
                out[...] = total

    return pl.pallas_call(
        body,
        grid_spec=pltpu.PrefetchScalarGridSpec(
            num_scalar_prefetch=1,
            grid=(ways,),
            in_specs=[pl.BlockSpec((part, wide), lambda at, place: (place[0] ^ at, 0))] * len(arrays),
            out_specs=[pl.BlockSpec((part, wide), lambda at, place: (0, 0))] * ways,
        ),
        out_shape=[jax.ShapeDtypeStruct((part, wide), F32)] * ways,
        compiler_params=pltpu.CompilerParams(dimension_semantics=("arbitrary",), vmem_limit_bytes=VMEM),
        cost_estimate=pl.CostEstimate(
            flops=0, bytes_accessed=4 * count * wide * (len(arrays) + 1), transcendentals=0
        ),
        name="sum_and_cut",
    )(place, *arrays)


def join(parts, place):
    part, wide = parts[0].shape
    ways = len(parts)

    def body(place, *refs):
        for at, ref in enumerate(refs[:ways]):

            @pl.when(pl.program_id(0) == at)
            def _():
                refs[ways][...] = ref[...]

    return pl.pallas_call(
        body,
        grid_spec=pltpu.PrefetchScalarGridSpec(
            num_scalar_prefetch=1,
            grid=(ways,),
            in_specs=[pl.BlockSpec((part, wide), lambda at, place: (0, 0))] * ways,
            out_specs=pl.BlockSpec((part, wide), lambda at, place: (place[0] ^ at, 0)),
        ),
        out_shape=jax.ShapeDtypeStruct((ways * part, wide), F32),
        compiler_params=pltpu.CompilerParams(dimension_semantics=("arbitrary",), vmem_limit_bytes=VMEM),
        cost_estimate=pl.CostEstimate(flops=0, bytes_accessed=8 * ways * part * wide, transcendentals=0),
        name="join",
    )(place, *parts)


def place_on(axis):
    return lax.axis_index(axis)[None]


def across(parts, axis):
    size = lax.axis_size(axis)
    return [
        lax.ppermute(part, axis, [(at, at ^ k) for at in range(size)]) if k else part
        for k, part in enumerate(parts)
    ]


class Settle:
    def __init__(self, other, mine, steps):
        half = mine.shape[0]
        self.first = mine
        if half % (8 * lax.axis_size(("node", "chip"))):
            first = lax.axis_index("core") == 0
            both = jnp.where(first, jnp.concatenate([mine, other]), jnp.concatenate([other, mine]))
            self.value = lax.psum(both, AXES)
            self.steps = []
        else:
            self.parts = [mine, lax.ppermute(other, "core", SWAP)]
            self.steps = list(steps)

    def chip(self):
        self.cut("chip")

    def node(self):
        self.cut("node")

    def cut(self, axis):
        self.parts = sum_and_cut(self.parts, place_on(axis), lax.axis_size(axis))
        self.mark = self.parts[0]
        self.parts = across(self.parts, axis)

    def piece(self):
        (self.mark,) = sum_and_cut(self.parts, place_on("node") * 0, 1)
        self.parts = across([self.mark] * lax.axis_size("node"), "node")

    def gather(self):
        (self.mark,) = sum_and_cut(self.parts, place_on("node") * 0, 1)
        self.value = lax.all_gather(self.mark, ("core", "chip", "node"), axis=0, tiled=True)

    def to_chip(self):
        self.join("node", "chip")

    def to_core(self):
        self.join("chip", "core")

    def end(self):
        self.value = self.mark = join(self.parts, place_on("core"))

    def join(self, axis, onward):
        self.mark = join(self.parts, place_on(axis))
        self.parts = across([self.mark] * lax.axis_size(onward), onward)

    def step(self, token):
        if not self.steps:
            return token
        self.parts, token = lax.optimization_barrier((self.parts, token))
        getattr(self, self.steps.pop(0))()
        return self.mark


BY_PERMUTES = ("chip", "node", "piece", "to_chip", "to_core", "end")
BY_GATHER = ("chip", "node", "gather")


def settle_weight_grad(inputs, gradient, steps):
    core = place_on("core")
    other = weight_grad(inputs, gradient, 1 - core)
    gradient, other = lax.optimization_barrier((gradient, other))
    mine = weight_grad(inputs, gradient, core)
    return Settle(other, mine, steps)


def turned(token, *weights):
    return [weight.T for weight in lax.optimization_barrier((weights, token))[0]]


def together(value, *tokens):
    return lax.optimization_barrier((value, tokens))[0]


def local(
    image, crop_sides, proj_in, kernel_large, kernel_small, proj_out, proj_up, proj_down,
    norm_gain, norm_shift, wide_gain, wide_shift, cotangent,
):
    crops, canvas, _, channels = image.shape
    wide = proj_up.shape[1]
    devices = lax.axis_size(AXES)
    cells = crops * canvas * ROW
    tables = wave_tables(canvas, kernel_large.shape[0], kernel_small.shape[0])
    half = tables["half"]

    def const(name):
        return tuple(jnp.asarray(part) for part in tables[name])

    ahead_t, back_t = const("ahead"), const("back")
    sides = (crop_sides, "smem")
    scale, offset = (norm_gain, "whole"), (norm_shift, "whole")
    wide_scale, wide_offset = (wide_gain[None], "whole"), (wide_shift[None], "whole")
    full, full_low = ((cells, channels), F32, "rows"), ((cells, channels), BF16, "rows")
    wide_low = ((cells, wide), BF16, "rows")
    wide_half = ((wide // 128, 128), F32, "whole")
    core = (place_on("core"), "smem")
    seen_out, wide_seen_out = ((8, channels), F32, "whole"), ((8, wide), F32, "whole")

    def send(count):
        return ((devices, -(-count // 1024) * 8, 128), F32, "whole")

    def coefs(count, width=channels):
        return ((count, 8, width), F32)

    def run(kernel, ins, outs, scratch):
        return call(kernel, crops, ins, outs, scratch)

    def r(value):
        return (value, "rows")

    def w(value):
        return (value, "whole")

    x, u, sent = run(
        enter_stage,
        [sides, (image, "map"), (cotangent, "map")],
        [full_low, full_low, send(2 * channels + 128)],
        [((2, canvas * ROW, channels), F32), coefs(2)],
    )
    came = exchange(sent)
    spectrum_out = ((2 * half, channels), F32, "whole")
    large_w, small_w = call(
        kernel_waves_stage,
        1,
        [w(kernel_large), w(kernel_small), w(const("large")), w(const("small"))],
        [spectrum_out, spectrum_out],
        [
            ((tables["large"][0].shape[1], channels), BF16),
            ((tables["small"][0].shape[1], channels), BF16),
        ],
    )
    came = together(came, large_w, small_w)
    pre_low, pre, sent, seen = run(
        first_stage,
        [sides, w(came), scale, offset, r(x), w(proj_in)],
        [full_low, full, send(2 * channels), seen_out],
        [coefs(2), coefs(2)],
    )
    spectrum = ((2 * half, channels), F32)
    spectrum_low = ((2 * half, channels), BF16)
    down_t, out_t = turned(sent, proj_down, proj_out)
    came = together(exchange(sent), down_t, out_t)
    mixer_low, large, small, mixer_waves, sent, first_seen = run(
        mixer_stage,
        [sides, w(came), w(seen), scale, offset, r(pre), w(ahead_t), w(back_t), w(large_w), w(small_w)],
        [full_low, full, full, ((crops * 2 * half, channels), BF16, "rows"), send(4 * channels), seen_out],
        [coefs(2), coefs(4), spectrum, spectrum_low, spectrum_low],
    )
    up_t, in_t = turned(sent, proj_up, proj_in)
    came = together(exchange(sent), up_t, in_t)
    merged_low, proj, sent, merge_seen = run(
        merge_stage,
        [sides, w(came), w(seen), scale, offset, r(large), r(small), r(x), r(u), w(proj_out)],
        [full_low, full, send(4 * channels), seen_out],
        [coefs(3), coefs(4)],
    )
    ffn_low, hidden, mine, other, mid_seen = run(
        widen_stage,
        [sides, core, w(exchange(sent)), w(seen), scale, offset, r(x), r(proj), w(proj_up)],
        [full_low, wide_low, wide_half, wide_half, seen_out],
        [coefs(3), coefs(2, wide), ((canvas * ROW, channels), F32)],
    )
    hidden_low, last, sent, wide_seen = run(
        narrow_stage,
        [sides, core, w(wide_exchange(mine, other)), w(seen), wide_scale, wide_offset, r(hidden), r(u), w(proj_down)],
        [wide_low, full, send(4 * channels), wide_seen_out],
        [coefs(2, wide), coefs(4)],
    )
    down_low, hidden_grad, mine, other, last_seen = run(
        wide_back_stage,
        [
            sides, core, w(exchange(sent)), w(seen), w(wide_seen), scale, offset,
            r(last), r(u), r(hidden), w(down_t),
        ],
        [full_low, wide_low, wide_half, wide_half, seen_out],
        [coefs(3), coefs(2, wide), ((canvas * ROW, channels), F32)],
    )
    grad_down = weight_grad(hidden_low, down_low)
    came = wide_exchange(mine, other, grad_down)
    up_low, ffn_grad, sent, wide_noted = run(
        narrow_back_stage,
        [sides, core, w(came), w(wide_seen), wide_scale, r(hidden_grad), r(hidden), r(x), r(proj), w(up_t)],
        [wide_low, full, send(3 * channels), wide_seen_out],
        [coefs(3, wide), coefs(3)],
    )
    came = exchange(sent)
    grad_up = weight_grad(ffn_low, up_low)
    came = together(came, grad_up)
    grad_down, grad_up = lax.psum((grad_down, grad_up), AXES)
    resid_grad, back_low, merged_grad, sent, mid_noted = run(
        mid_back_stage,
        [
            sides, w(came), w(seen), w(merge_seen), w(mid_seen), w(last_seen), scale, offset,
            r(x), r(u), r(proj), r(ffn_grad), r(large), r(small), w(out_t),
        ],
        [full, full_low, full, send(3 * channels), seen_out],
        [coefs(7), coefs(3)],
    )
    came = exchange(sent)
    mixer_grad, large_sum, small_sum, sent, mixer_noted = run(
        mixer_back_stage,
        [
            sides, w(came), w(seen), w(merge_seen), w(first_seen), scale, offset,
            r(large), r(small), r(merged_grad), r(pre), r(mixer_waves), w(ahead_t), w(back_t), w(large_w), w(small_w),
        ],
        [full, spectrum_out, spectrum_out, send(2 * channels), seen_out],
        [
            coefs(6), coefs(2), ((canvas * ROW, channels), BF16), ((canvas * ROW, channels), BF16),
            spectrum, spectrum, spectrum_low,
        ],
    )
    came = exchange(sent)
    taps_t = (const("large_back"), const("small_back"))
    tap_rows = sum(table[0].shape[0] for table in taps_t)
    tap_rows = -(-tap_rows // (8 * devices)) * 8 * devices
    half_taps = (((tap_rows + channels) // 2, channels), F32, "whole")
    other, mine = call(
        kernel_grad_stage,
        1,
        [core, w(merged_low), w(back_low), w(large_sum), w(small_sum), w(taps_t[0]), w(taps_t[1])],
        [half_taps, half_taps],
        [((tap_rows, channels), F32), ((channels, channels), F32)],
    )
    came = together(came, other, mine)
    settle_taps = Settle(other, mine, BY_PERMUTES)
    pre_round, first_grad, sent, first_noted = run(
        first_back_stage,
        [sides, w(came), w(seen), w(first_seen), scale, r(mixer_grad), r(pre), r(x), w(in_t)],
        [full_low, full, send(2 * channels), seen_out],
        [coefs(3), coefs(2)],
    )
    settle_in = settle_weight_grad(pre_low, pre_round, BY_PERMUTES)
    came = exchange(together(sent, settle_in.first))
    token = settle_in.step(settle_taps.step(settle_in.first))
    (block_out,) = run(
        block_out_stage,
        [sides, w(mid_seen), w(last_seen), scale, offset, r(x), r(proj), r(together(last, token))],
        [(image.shape, BF16, "map")],
        [],
    )
    token = settle_in.step(settle_taps.step(block_out))
    came = together(came, token)
    grad_image, enter_noted = run(
        leave_stage,
        [sides, w(came), w(seen), scale, r(resid_grad), r(first_grad), r(x)],
        [(image.shape, F32, "map"), seen_out],
        [coefs(3)],
    )
    token = grad_image
    while settle_in.steps or settle_taps.steps:
        token = settle_in.step(settle_taps.step(token))
    grad_in = settle_in.value
    grad_large, grad_small, grad_out = call(
        functools.partial(kernel_grad_out_stage, canvas=canvas),
        1,
        [w(settle_taps.value)],
        [(kernel_large.shape, F32, "whole"), (kernel_small.shape, F32, "whole"), (proj_out.shape, F32, "whole")],
        [((tap_rows, channels), F32)],
    )
    gain_grads = jnp.stack(
        [enter_noted[0], first_noted[0], mixer_noted[0], mixer_noted[1], mid_noted[2], mid_noted[0], last_seen[3]]
    )
    shift_grads = jnp.stack(
        [enter_noted[1], first_noted[1], mixer_noted[2], mixer_noted[2], mid_noted[3], mid_noted[1], last_seen[2]]
    )
    return (
        block_out, grad_image, grad_in, grad_large, grad_small, grad_out, grad_up, grad_down,
        gain_grads, shift_grads, wide_noted[0], wide_noted[1],
    )


def solution(mesh):
    nodes, devices = mesh.devices.shape
    chips = jax.sharding.Mesh(mesh.devices.reshape(nodes, devices // 2, 2), AXES)
    maps = P(AXES, None, None, None)
    return jax.shard_map(
        local,
        mesh=chips,
        in_specs=(maps, P(AXES)) + (P(),) * 10 + (maps,),
        out_specs=(maps, maps) + (P(),) * 10,
        check_vma=False,
    )
```

```python
import functools
import math

import jax
import jax.numpy as jnp
import ml_dtypes
import numpy as np
from jax import lax
from jax.experimental import pallas as pl
from jax.experimental.pallas import tpu as pltpu
from jax.sharding import PartitionSpec as P

EPSILON = 1e-05
ROOT = 0.7978845608028654
CUBIC = 0.044715
AXES = ("node", "chip", "core")
ROW = 16
F32 = jnp.float32
BF16 = jnp.bfloat16


def split(table):
    high = table.astype(ml_dtypes.bfloat16)
    low = (table - high.astype(np.float64)).astype(ml_dtypes.bfloat16)
    return high, low


@functools.lru_cache(maxsize=None)
def wave_tables(canvas, side_large, side_small):
    period = 2 * canvas - 1
    pairs = [(0, v) for v in range(canvas)]
    pairs += [(u, v) for u in range(1, canvas) for v in range(period)]
    waves = np.array(pairs)
    half = -(-len(pairs) // 16) * 16

    def table(places_h, places_w, keep, sign):
        grid = np.stack(np.meshgrid(places_h, places_w, indexing="ij"), -1).reshape(-1, 2)
        angle = 2 * np.pi * ((waves @ grid.T) % period) / period
        out = np.zeros((2 * half, grid.shape[0]))
        out[: len(pairs)] = np.cos(angle) * keep
        out[half : half + len(pairs)] = sign * np.sin(angle) * keep
        return out

    share = np.zeros((2 * half, 1))
    share[: len(pairs)] = 2.0 / period**2
    share[half : half + len(pairs)] = 2.0 / period**2
    share[0] = 1.0 / period**2

    inside = (np.arange(ROW) < canvas).astype(np.float64)
    cells = table(np.arange(canvas), np.arange(ROW), np.tile(inside, canvas), -1.0)

    def taps(side, row):
        middle = (side - 1) // 2
        offsets_h = np.arange(side) - middle
        offsets_w = np.arange(row) - middle
        keep = (np.abs(offsets_h) < canvas)[:, None] & (np.abs(offsets_w) < canvas)[None, :]
        keep = keep & (np.arange(row) < side)[None, :]
        return table(offsets_h, offsets_w, keep.reshape(-1).astype(np.float64), 1.0)

    def taps_back(side):
        first, count = used_rows(side, canvas)
        every = taps(side, side).reshape(2 * half, side, side)
        used = every[:, first : first + count, first : first + count].reshape(2 * half, -1)
        return np.pad(used, ((0, 0), (0, -used.shape[1] % 8)))

    def tap_row(side):
        return -(-side // 16) * 16

    large = taps(side_large, tap_row(side_large))
    small = taps(side_small, tap_row(side_small))
    turn = np.ones((2 * half, 1))
    turn[half:] = -1.0
    return dict(
        half=half,
        ahead=split(cells),
        back=split((cells * share).T),
        large=split(large),
        small=split(small),
        large_back=split((taps_back(side_large) * turn * share).T),
        small_back=split((taps_back(side_small) * turn * share).T),
    )


def used_rows(side, canvas):
    first = max(0, (side - 1) // 2 - (canvas - 1))
    return first, side - 2 * first


def dot(left, right):
    return jnp.dot(left, right, preferred_element_type=F32)


def dot_nt(left, right):
    return lax.dot_general(left, right, (((1,), (1,)), ((), ())), preferred_element_type=F32)


def dot_tn(left, right):
    return lax.dot_general(left, right, (((0,), (0,)), ((), ())), preferred_element_type=F32)


def halves(values):
    high = values.astype(BF16)
    return high, (values - high.astype(F32)).astype(BF16)


def gelu(values):
    inner = values * (ROOT + (ROOT * CUBIC) * (values * values))
    return values * (0.5 + 0.5 * jnp.tanh(inner))


def gelu_and_slope(values):
    square = values * values
    bend = jnp.tanh(values * (ROOT + (ROOT * CUBIC) * square))
    slope = ROOT + (3.0 * ROOT * CUBIC) * square
    half = 0.5 + 0.5 * bend
    return values * half, half * (1.0 + values * slope * (1.0 - bend))


def gelu_slope(values):
    square = values * values
    bend = jnp.tanh(values * (ROOT + (ROOT * CUBIC) * square))
    slope = ROOT + (3.0 * ROOT * CUBIC) * square
    return 0.5 + 0.5 * bend + values * slope * (0.5 - 0.5 * bend * bend)


def rows(at):
    return pl.ds(pl.multiple_of(at * ROW, ROW), ROW)


def fold(values):
    return values[:8] + values[8:]


def twice(values):
    return jnp.concatenate([values, values], axis=0)


def columns_inside(side, channels):
    places = lax.broadcasted_iota(jnp.int32, (ROW, 128), 0)
    inside = (places < side).astype(F32)
    return jnp.concatenate([inside] * (channels // 128), axis=1)


def first_step():
    return pl.program_id(0) == 0


def last_step():
    return pl.program_id(0) == pl.num_programs(0) - 1


def to_tiles(parts):
    lines = [part[:, at : at + 128] for part in parts for at in range(0, part.shape[1], 128)]
    lines += [jnp.zeros_like(lines[0])] * (-len(lines) % 8)
    return jnp.concatenate(lines, axis=0)


def from_tiles(tiles, count, width):
    tiles = [tiles[at : at + 1] for at in range(count * width // 128)]
    many = width // 128
    return [jnp.concatenate(tiles[at * many : (at + 1) * many], axis=1) for at in range(count)]


def received(sent, count, width):
    return from_tiles(jnp.sum(sent[...], axis=0), count, width)


def keep(coefs, values):
    for at, value in enumerate(values):
        coefs[at] = jnp.broadcast_to(value, coefs.shape[1:])


def note(out, values):
    values = list(values)
    values += [jnp.zeros_like(values[0])] * (out.shape[0] - len(values))
    out[...] = jnp.concatenate(values, axis=0)


def add_sums(sums, parts):
    @pl.when(first_step())
    def _():
        sums[...] = jnp.zeros_like(sums)

    for at, part in enumerate(parts):
        sums[at] += part


def publish(sums, out, extra=()):
    @pl.when(last_step())
    def _():
        parts = [jnp.sum(sums[at], axis=0, keepdims=True) for at in range(sums.shape[0])]
        parts += list(extra)
        out[...] = jnp.broadcast_to(to_tiles(parts)[None], out.shape)


def norm_coefs(column_sum, square, count, scaling, offsets):
    mean = column_sum / count
    reciprocal = lax.rsqrt(square / count - mean * mean + EPSILON)
    factor = scaling * reciprocal
    return mean, reciprocal, factor, offsets - mean * factor


def back_coefs(shift_sum, gain_sum, count, mean, reciprocal, scaling):
    factor = scaling * reciprocal
    slope = factor * reciprocal * gain_sum / count
    return factor, factor * shift_sum / count - slope * mean, slope


def zeros(count, channels):
    return tuple(jnp.zeros((8, channels), F32) for _ in range(count))


def enter_stage(sides, image, cotangent, x_out, u_out, sent, padded, sums):
    at_crop = pl.program_id(0)
    side = sides[at_crop]
    canvas, channels = image.shape[1], image.shape[3]
    inside = columns_inside(side, channels)

    @pl.when(first_step())
    def _():
        padded[...] = jnp.zeros_like(padded)

    def step(at, carry):
        mask = jnp.where(at < side, inside, 0.0)
        start = pl.multiple_of(at * ROW, ROW)
        padded[0, pl.ds(start, canvas), :] = image[0, at].astype(F32)
        padded[1, pl.ds(start, canvas), :] = cotangent[0, at].astype(F32)
        x = padded[0, rows(at), :] * mask
        u = padded[1, rows(at), :] * mask
        x_out[rows(at), :] = x.astype(BF16)
        u_out[rows(at), :] = u.astype(BF16)
        return carry[0] + fold(x), carry[1] + fold(x * x)

    add_sums(sums, lax.fori_loop(0, canvas, step, zeros(2, channels), unroll=14))
    count = jnp.int32(0)
    for at in range(sides.shape[0]):
        count += sides[at] * sides[at]
    publish(sums, sent, [jnp.full((1, 128), count.astype(F32))])


def first_stage(sides, came, scale, offset, x_in, weight, low_out, pre_out, sent, seen, coefs, sums):
    channels = x_in.shape[1]
    canvas = x_in.shape[0] // ROW
    side = sides[pl.program_id(0)]

    @pl.when(first_step())
    def _():
        tiles = channels // 128
        parts = received(came, 2 * tiles + 1, 128)
        column_sum = jnp.concatenate(parts[:tiles], axis=1)
        square = jnp.concatenate(parts[tiles : 2 * tiles], axis=1)
        count = jnp.concatenate([parts[2 * tiles]] * tiles, axis=1)
        mean, reciprocal, factor, constant = norm_coefs(column_sum, square, count, scale[0:1], offset[0:1])
        keep(coefs, [factor, constant])
        note(seen, [count, mean, reciprocal, column_sum, square])

    inside = columns_inside(side, channels)
    factor, constant = twice(coefs[0]), twice(coefs[1])

    def step(at, carry):
        mask = jnp.where(at < side, inside, 0.0)
        low_out[rows(at), :] = (mask * (factor * x_in[rows(at), :].astype(F32) + constant)).astype(BF16)
        return carry

    lax.fori_loop(0, canvas, step, 0, unroll=14)
    pre_out[...] = dot(low_out[...], weight[...])

    def measure(at, carry):
        pre = pre_out[rows(at), :]
        return carry[0] + fold(pre), carry[1] + fold(pre * pre)

    add_sums(sums, lax.fori_loop(0, canvas, measure, zeros(2, channels), unroll=14))
    publish(sums, sent)


def times(spectrum, kernel, half, at, conj):
    real, imag = pl.ds(pl.multiple_of(at * 16, 16), 16), pl.ds(pl.multiple_of(half + at * 16, 16), 16)
    a, b = spectrum[real, :], spectrum[imag, :]
    c, d = kernel[real, :], kernel[imag, :]
    if conj:
        return real, imag, a * c + b * d, b * c - a * d
    return real, imag, a * c - b * d, a * d + b * c


def ahead_once(tables, values):
    return dot(tables[0][...], values)


def back_once(tables, values):
    return dot(tables[0][...], values.astype(BF16))


def ahead(tables, values):
    return dot(tables[0][...], values) + dot(tables[1][...], values)


def back(tables, high, low):
    return dot(tables[0][...], high) + dot(tables[0][...], low) + dot(tables[1][...], high)


def mixer_stage(
    sides, came, seen, scale, offset, pre_in, ahead_t, back_t, large_w, small_w,
    low_out, large_out, small_out, waves_out, sent, noted, coefs, sums, spectrum, high,
):
    channels = pre_in.shape[1]
    canvas = pre_in.shape[0] // ROW
    half = spectrum.shape[0] // 2
    side = sides[pl.program_id(0)]

    @pl.when(first_step())
    def _():
        mean, reciprocal, factor, constant = norm_coefs(
            *received(came, 2, channels), seen[0:1], scale[1:2], offset[1:2]
        )
        keep(coefs, [factor, constant])
        note(noted, [mean, reciprocal])

    inside = columns_inside(side, channels)
    factor, constant = twice(coefs[0]), twice(coefs[1])

    def step(at, carry):
        mask = jnp.where(at < side, inside, 0.0)
        low_out[rows(at), :] = gelu(mask * (factor * pre_in[rows(at), :] + constant)).astype(BF16)
        return carry

    lax.fori_loop(0, canvas, step, 0, unroll=14)
    spectrum[...] = ahead(ahead_t, low_out[...])
    waves_out[...] = spectrum[...].astype(BF16)
    parts = ()
    for kernel, out in ((large_w, large_out), (small_w, small_out)):

        def product(at, carry):
            real, imag, new_real, new_imag = times(spectrum, kernel, half, at, False)
            high[real, :] = new_real.astype(BF16)
            high[imag, :] = new_imag.astype(BF16)
            return carry

        lax.fori_loop(0, half // 16, product, 0, unroll=4)
        out[...] = ahead(back_t, high[...])

        def measure(at, carry):
            conv = jnp.where(at < side, inside, 0.0) * out[rows(at), :]
            out[rows(at), :] = conv
            return carry[0] + fold(conv), carry[1] + fold(conv * conv)

        parts += lax.fori_loop(0, canvas, measure, zeros(2, channels), unroll=14)
    add_sums(sums, parts)
    publish(sums, sent)


def merge_stage(
    sides, came, seen, scale, offset, large_in, small_in, x_in, u_in, weight,
    low_out, proj_out, sent, noted, coefs, sums,
):
    channels = x_in.shape[1]
    canvas = x_in.shape[0] // ROW
    side = sides[pl.program_id(0)]

    @pl.when(first_step())
    def _():
        large_sum, large_square, small_sum, small_square = received(came, 4, channels)
        large = norm_coefs(large_sum, large_square, seen[0:1], scale[2:3], offset[2:3])
        small = norm_coefs(small_sum, small_square, seen[0:1], scale[3:4], offset[3:4])
        keep(coefs, [large[2], small[2], large[3] + small[3]])
        note(noted, [large[0], large[1], small[0], small[1], large[2], small[2], large[3] + small[3]])

    inside = columns_inside(side, channels)
    large, small, constant = twice(coefs[0]), twice(coefs[1]), twice(coefs[2])

    def step(at, carry):
        mask = jnp.where(at < side, inside, 0.0)
        merged = mask * (large * large_in[rows(at), :] + small * small_in[rows(at), :] + constant)
        low_out[rows(at), :] = gelu(merged).astype(BF16)
        return carry

    lax.fori_loop(0, canvas, step, 0, unroll=14)
    proj_out[...] = dot(low_out[...], weight[...])

    def measure(at, carry):
        proj = proj_out[rows(at), :]
        x, u = x_in[rows(at), :].astype(F32), u_in[rows(at), :].astype(F32)
        parts = (proj, proj * proj, proj * x, proj * u)
        return tuple(old + fold(part) for old, part in zip(carry, parts))

    add_sums(sums, lax.fori_loop(0, canvas, measure, zeros(4, channels), unroll=7))
    publish(sums, sent)


def widen_stage(
    sides, core, came, seen, scale, offset, x_in, proj_in, weight,
    low_out, hidden_out, mine, other, noted, coefs, sums, found,
):
    channels = x_in.shape[1]
    canvas = x_in.shape[0] // ROW
    side = sides[pl.program_id(0)]

    @pl.when(first_step())
    def _():
        proj_sum, proj_square, cross, _ = parts = received(came, 4, channels)
        count, x_mean, x_sum, x_square = seen[0:1], seen[1:2], seen[3:4], seen[4:5]
        mean, reciprocal, factor, constant = norm_coefs(
            proj_sum, proj_square, count, scale[4:5], offset[4:5]
        )
        mid_mean = x_mean + factor * mean + constant
        x_var = x_square / count - x_mean * x_mean
        proj_var = proj_square / count - mean * mean
        both = cross / count - x_mean * mean
        mid_var = x_var + factor * factor * proj_var + 2.0 * factor * both
        mid_reciprocal = lax.rsqrt(mid_var + EPSILON)
        mid_factor = scale[5:6] * mid_reciprocal
        keep(coefs, [mid_factor, mid_factor * factor, mid_factor * (constant - mid_mean) + offset[5:6]])
        note(noted, [mean, reciprocal, mid_mean, mid_reciprocal] + parts)

    inside = columns_inside(side, channels)
    from_x, from_proj, constant = twice(coefs[0]), twice(coefs[1]), twice(coefs[2])

    def step(at, carry):
        mask = jnp.where(at < side, inside, 0.0)
        x = x_in[rows(at), :].astype(F32)
        low_out[rows(at), :] = (mask * (from_x * x + from_proj * proj_in[rows(at), :] + constant)).astype(BF16)
        return carry

    lax.fori_loop(0, canvas, step, 0, unroll=14)
    parts = [[], []]
    for at_block in range(hidden_out.shape[1] // channels):
        block = slice(at_block * channels, (at_block + 1) * channels)
        found[...] = dot(low_out[...], weight[:, block])

        def measure(at, carry):
            hidden = found[rows(at), :]
            hidden_out[rows(at), block] = hidden.astype(BF16)
            return carry[0] + fold(hidden), carry[1] + fold(hidden * hidden)

        pair = lax.fori_loop(0, canvas, measure, zeros(2, channels), unroll=14)
        parts[0].append(pair[0])
        parts[1].append(pair[1])
    add_sums(sums, [jnp.concatenate(part, axis=1) for part in parts])
    hand_over(sums, core, mine, other)


def hand_over(sums, core, mine, other):
    @pl.when(last_step())
    def _():
        first, second = (to_tiles([jnp.sum(sums[at], axis=0, keepdims=True)]) for at in range(2))
        mine[...] = jnp.where(core[0] == 0, first, second)
        other[...] = jnp.where(core[0] == 0, second, first)


def taken_over(core, came):
    mine, other = came[0][...], came[1][...]
    wide = mine.size
    first = jnp.where(core[0] == 0, mine, other)
    second = jnp.where(core[0] == 0, other, mine)
    return from_tiles(first, 1, wide)[0], from_tiles(second, 1, wide)[0]


def narrow_stage(
    sides, core, came, seen, wide_scale, wide_offset, hidden_in, u_in, weight,
    low_out, slope_out, proj_out, sent, noted, coefs, sums,
):
    channels = u_in.shape[1]
    canvas = u_in.shape[0] // ROW
    wide = hidden_in.shape[1]
    side = sides[pl.program_id(0)]

    @pl.when(first_step())
    def _():
        count = jnp.concatenate([seen[0:1]] * (wide // channels), axis=1)
        mean, reciprocal, factor, constant = norm_coefs(
            *taken_over(core, came), count, wide_scale[...], wide_offset[...]
        )
        keep(coefs, [factor, constant])
        note(noted, [mean, reciprocal, factor, constant, count])

    for at_block in range(wide // channels):
        block = slice(at_block * channels, (at_block + 1) * channels)
        factor, constant = twice(coefs[0, :, block]), twice(coefs[1, :, block])

        def step(at, carry):
            hidden = hidden_in[rows(at), block].astype(F32)
            value, slope = gelu_and_slope(factor * hidden + constant)
            low_out[rows(at), block] = value.astype(BF16)
            slope_out[rows(at), block] = slope.astype(BF16)
            return carry

        lax.fori_loop(0, canvas, step, 0, unroll=14)
    proj_out[...] = dot(low_out[...], weight[...])
    inside = columns_inside(side, channels)

    def measure(at, carry):
        proj = jnp.where(at < side, inside, 0.0) * proj_out[rows(at), :]
        proj_out[rows(at), :] = proj
        u = u_in[rows(at), :].astype(F32)
        parts = (proj, proj * proj, proj * u, u)
        return tuple(old + fold(part) for old, part in zip(carry, parts))

    add_sums(sums, lax.fori_loop(0, canvas, measure, zeros(4, channels), unroll=7))
    publish(sums, sent)


def wide_back_stage(
    sides, core, came, seen, scale, offset, proj_in, u_in, hidden_in, slope_in, weight,
    down_out, grad_out, mine, other, noted, coefs, sums, found,
):
    channels = u_in.shape[1]
    canvas = u_in.shape[0] // ROW
    wide = hidden_in.shape[1]
    side = sides[pl.program_id(0)]

    @pl.when(first_step())
    def _():
        proj_sum, proj_square, cross, u_sum = received(came, 4, channels)
        count = seen[0:1]
        mean, reciprocal, factor, constant = norm_coefs(
            proj_sum, proj_square, count, scale[6:7], offset[6:7]
        )
        gain_sum = reciprocal * (cross - mean * u_sum)
        keep(coefs, back_coefs(u_sum, gain_sum, count, mean, reciprocal, scale[6:7]))
        note(noted, [mean, reciprocal, u_sum, gain_sum, factor, constant])

    inside = columns_inside(side, channels)
    factor, constant, slope = twice(coefs[0]), twice(coefs[1]), twice(coefs[2])

    def step(at, carry):
        mask = jnp.where(at < side, inside, 0.0)
        u = u_in[rows(at), :].astype(F32)
        down_out[rows(at), :] = (mask * (factor * u - constant - slope * proj_in[rows(at), :])).astype(BF16)
        return carry

    lax.fori_loop(0, canvas, step, 0, unroll=14)
    parts = [[], []]
    for at_block in range(wide // channels):
        block = slice(at_block * channels, (at_block + 1) * channels)
        found[...] = dot(down_out[...], weight[:, block])

        def measure(at, carry):
            hidden = hidden_in[rows(at), block].astype(F32)
            grad = found[rows(at), :] * slope_in[rows(at), block].astype(F32)
            grad_out[rows(at), block] = grad.astype(BF16)
            return carry[0] + fold(grad), carry[1] + fold(grad * hidden)

        pair = lax.fori_loop(0, canvas, measure, zeros(2, channels), unroll=7)
        parts[0].append(pair[0])
        parts[1].append(pair[1])
    add_sums(sums, [jnp.concatenate(part, axis=1) for part in parts])
    hand_over(sums, core, mine, other)


def narrow_back_stage(
    sides, core, came, wide_seen, wide_scale, grad_in, hidden_in, x_in, proj_in, weight,
    up_out, ffn_out, sent, noted, coefs, sums,
):
    channels = x_in.shape[1]
    canvas = x_in.shape[0] // ROW
    wide = hidden_in.shape[1]
    side = sides[pl.program_id(0)]

    @pl.when(first_step())
    def _():
        mean, reciprocal, count = wide_seen[0:1], wide_seen[1:2], wide_seen[4:5]
        shift_sum, with_hidden = taken_over(core, came)
        gain_sum = reciprocal * (with_hidden - mean * shift_sum)
        keep(coefs, back_coefs(shift_sum, gain_sum, count, mean, reciprocal, wide_scale[...]))
        note(noted, [gain_sum, shift_sum])

    for at_block in range(wide // channels):
        block = slice(at_block * channels, (at_block + 1) * channels)
        factor, constant, slope = (twice(coefs[at, :, block]) for at in range(3))

        def step(at, carry):
            grad = factor * grad_in[rows(at), block].astype(F32) - constant
            grad = grad - slope * hidden_in[rows(at), block].astype(F32)
            up_out[rows(at), block] = grad.astype(BF16)
            return carry

        lax.fori_loop(0, canvas, step, 0, unroll=14)
    ffn_out[...] = dot(up_out[...], weight[...])
    inside = columns_inside(side, channels)

    def measure(at, carry):
        grad = jnp.where(at < side, inside, 0.0) * ffn_out[rows(at), :]
        ffn_out[rows(at), :] = grad
        parts = (grad, grad * x_in[rows(at), :].astype(F32), grad * proj_in[rows(at), :])
        return tuple(old + fold(part) for old, part in zip(carry, parts))

    add_sums(sums, lax.fori_loop(0, canvas, measure, zeros(3, channels), unroll=7))
    publish(sums, sent)


def mid_back_stage(
    sides, came, seen, merge_seen, mid_seen, last_seen, scale, offset,
    x_in, u_in, proj_in, ffn_in, large_in, small_in, weight,
    resid_out, back_out, grad_out, sent, noted, coefs, sums,
):
    channels = x_in.shape[1]
    canvas = x_in.shape[0] // ROW
    side = sides[pl.program_id(0)]

    @pl.when(first_step())
    def _():
        ffn_sum, ffn_x, ffn_proj = received(came, 3, channels)
        count, u_sum = seen[0:1], last_seen[2:3]
        mean, reciprocal, mid_mean, mid_reciprocal = (mid_seen[at : at + 1] for at in range(4))
        proj_sum, proj_square, cross, proj_u = (mid_seen[at : at + 1] for at in range(4, 8))
        proj_factor = scale[4:5] * reciprocal
        proj_constant = offset[4:5] - mean * proj_factor
        ffn_mid = ffn_x + proj_factor * ffn_proj + proj_constant * ffn_sum
        mid_gain = mid_reciprocal * (ffn_mid - mid_mean * ffn_sum)
        factor, constant, slope = back_coefs(ffn_sum, mid_gain, count, mid_mean, mid_reciprocal, scale[5:6])
        mid_proj = cross + proj_factor * proj_square + proj_constant * proj_sum
        resid_sum = u_sum
        resid_proj = proj_u + factor * ffn_proj - constant * proj_sum - slope * mid_proj
        gain = reciprocal * (resid_proj - mean * resid_sum)
        second = back_coefs(resid_sum, gain, count, mean, reciprocal, scale[4:5])
        keep(coefs, [factor, constant + slope * proj_constant, slope, slope * proj_factor, *second])
        note(noted, [mid_gain, ffn_sum, gain, resid_sum])

    inside = columns_inside(side, channels)

    def step(at, carry):
        mask = jnp.where(at < side, inside, 0.0)
        x, u = x_in[rows(at), :].astype(F32), u_in[rows(at), :].astype(F32)
        proj = proj_in[rows(at), :]
        resid = twice(coefs[0]) * ffn_in[rows(at), :] - twice(coefs[1]) - twice(coefs[2]) * x
        resid = u + mask * (resid - twice(coefs[3]) * proj)
        resid_out[rows(at), :] = resid
        down = twice(coefs[4]) * resid - twice(coefs[5]) - twice(coefs[6]) * proj
        back_out[rows(at), :] = (mask * down).astype(BF16)
        return carry

    lax.fori_loop(0, canvas, step, 0, unroll=14)
    grad_out[...] = dot(back_out[...], weight[...])
    large = jnp.broadcast_to(merge_seen[4:5], (ROW, channels))
    small = jnp.broadcast_to(merge_seen[5:6], (ROW, channels))
    constant = jnp.broadcast_to(merge_seen[6:7], (ROW, channels))

    def measure(at, carry):
        large_conv, small_conv = large_in[rows(at), :], small_in[rows(at), :]
        grad = grad_out[rows(at), :] * gelu_slope(large * large_conv + small * small_conv + constant)
        grad_out[rows(at), :] = grad
        parts = (grad, grad * large_conv, grad * small_conv)
        return tuple(old + fold(part) for old, part in zip(carry, parts))

    add_sums(sums, lax.fori_loop(0, canvas, measure, zeros(3, channels), unroll=7))
    publish(sums, sent)


def mixer_back_stage(
    sides, came, seen, merge_seen, first_seen, scale, offset, large_in, small_in, grad_in, pre_in, waves_in,
    ahead_t, back_t, large_w, small_w,
    grad_out, large_sum, small_sum, sent, noted, coefs, sums, large_out, small_out, large_s, small_s, summed,
):
    channels = pre_in.shape[1]
    canvas = pre_in.shape[0] // ROW
    half = large_s.shape[0] // 2
    side = sides[pl.program_id(0)]

    @pl.when(first_step())
    def _():
        shift_sum, with_large, with_small = received(came, 3, channels)
        count = seen[0:1]
        large_mean, large_r, small_mean, small_r = (merge_seen[at : at + 1] for at in range(4))
        large_gain = large_r * (with_large - large_mean * shift_sum)
        small_gain = small_r * (with_small - small_mean * shift_sum)
        keep(
            coefs,
            [
                *back_coefs(shift_sum, large_gain, count, large_mean, large_r, scale[2:3]),
                *back_coefs(shift_sum, small_gain, count, small_mean, small_r, scale[3:4]),
            ],
        )
        note(noted, [large_gain, small_gain, shift_sum])

    inside = columns_inside(side, channels)

    def step(at, carry):
        mask = jnp.where(at < side, inside, 0.0)
        grad = grad_in[rows(at), :]
        large = twice(coefs[0]) * grad - twice(coefs[1]) - twice(coefs[2]) * large_in[rows(at), :]
        small = twice(coefs[3]) * grad - twice(coefs[4]) - twice(coefs[5]) * small_in[rows(at), :]
        large_out[rows(at), :] = (mask * large).astype(BF16)
        small_out[rows(at), :] = (mask * small).astype(BF16)
        return carry

    lax.fori_loop(0, canvas, step, 0, unroll=14)
    large_s[...] = ahead_once(ahead_t, large_out[...])
    small_s[...] = ahead_once(ahead_t, small_out[...])

    def product(at, carry):
        real, imag, one_real, one_imag = times(large_s, large_w, half, at, True)
        _, _, two_real, two_imag = times(small_s, small_w, half, at, True)
        summed[real, :] = (one_real + two_real).astype(BF16)
        summed[imag, :] = (one_imag + two_imag).astype(BF16)
        a, b = waves_in[real, :].astype(F32), waves_in[imag, :].astype(F32)
        for total, spectrum in ((large_sum, large_s), (small_sum, small_s)):
            c, d = spectrum[real, :], spectrum[imag, :]
            total[real, :] += a * c + b * d
            total[imag, :] += b * c - a * d
        return carry

    @pl.when(first_step())
    def _():
        large_sum[...] = jnp.zeros_like(large_sum)
        small_sum[...] = jnp.zeros_like(small_sum)

    lax.fori_loop(0, half // 16, product, 0, unroll=4)
    grad_out[...] = back_once(back_t, summed[...])
    reciprocal = first_seen[1:2]
    factor = scale[1:2] * reciprocal
    constant = jnp.broadcast_to(offset[1:2] - first_seen[0:1] * factor, (ROW, channels))
    factor = jnp.broadcast_to(factor, (ROW, channels))

    def measure(at, carry):
        mask = jnp.where(at < side, inside, 0.0)
        pre = pre_in[rows(at), :]
        grad = mask * grad_out[rows(at), :] * gelu_slope(factor * pre + constant)
        grad_out[rows(at), :] = grad
        return carry[0] + fold(grad), carry[1] + fold(grad * pre)

    add_sums(sums, lax.fori_loop(0, canvas, measure, zeros(2, channels), unroll=7))
    publish(sums, sent)


def first_back_stage(
    sides, came, seen, first_seen, scale, grad_in, pre_in, x_in, weight,
    low_out, grad_out, sent, noted, coefs, sums,
):
    channels = pre_in.shape[1]
    canvas = pre_in.shape[0] // ROW
    side = sides[pl.program_id(0)]

    @pl.when(first_step())
    def _():
        shift_sum, with_pre = received(came, 2, channels)
        mean, reciprocal = first_seen[0:1], first_seen[1:2]
        gain_sum = reciprocal * (with_pre - mean * shift_sum)
        keep(coefs, back_coefs(shift_sum, gain_sum, seen[0:1], mean, reciprocal, scale[1:2]))
        note(noted, [gain_sum, shift_sum])

    inside = columns_inside(side, channels)
    factor, constant, slope = twice(coefs[0]), twice(coefs[1]), twice(coefs[2])

    def step(at, carry):
        mask = jnp.where(at < side, inside, 0.0)
        grad = factor * grad_in[rows(at), :] - constant - slope * pre_in[rows(at), :]
        low_out[rows(at), :] = (mask * grad).astype(BF16)
        return carry

    lax.fori_loop(0, canvas, step, 0, unroll=14)
    grad_out[...] = dot(low_out[...], weight[...])

    def measure(at, carry):
        grad = grad_out[rows(at), :]
        return carry[0] + fold(grad), carry[1] + fold(grad * x_in[rows(at), :].astype(F32))

    add_sums(sums, lax.fori_loop(0, canvas, measure, zeros(2, channels), unroll=14))
    publish(sums, sent)


def leave_stage(sides, came, seen, scale, resid_in, grad_in, x_in, image_out, noted, coefs):
    channels = x_in.shape[1]
    canvas = x_in.shape[0] // ROW
    side = sides[pl.program_id(0)]

    @pl.when(first_step())
    def _():
        shift_sum, with_x = received(came, 2, channels)
        count, mean, reciprocal = (seen[at : at + 1] for at in range(3))
        gain_sum = reciprocal * (with_x - mean * shift_sum)
        keep(coefs, back_coefs(shift_sum, gain_sum, count, mean, reciprocal, scale[0:1]))
        note(noted, [gain_sum, shift_sum])

    inside = columns_inside(side, channels)
    factor, constant, slope = twice(coefs[0]), twice(coefs[1]), twice(coefs[2])

    def step(at, carry):
        mask = jnp.where(at < side, inside, 0.0)
        grad = factor * grad_in[rows(at), :] - constant - slope * x_in[rows(at), :].astype(F32)
        image_out[0, at] = (mask * (resid_in[rows(at), :] + grad))[:canvas]
        return carry

    lax.fori_loop(0, canvas, step, 0, unroll=14)


def block_out_stage(sides, mid_seen, last_seen, scale, offset, x_in, mid_in, last_in, out):
    channels = x_in.shape[1]
    canvas = x_in.shape[0] // ROW
    side = sides[pl.program_id(0)]
    inside = columns_inside(side, channels)
    factor = scale[4:5] * mid_seen[1:2]
    constant = offset[4:5] - mid_seen[0:1] * factor + last_seen[5:6]
    constant = jnp.broadcast_to(constant, (ROW, channels))
    factor = jnp.broadcast_to(factor, (ROW, channels))
    last = jnp.broadcast_to(last_seen[4:5], (ROW, channels))

    def step(at, carry):
        mask = jnp.where(at < side, inside, 0.0)
        added = factor * mid_in[rows(at), :] + last * last_in[rows(at), :] + constant
        out[0, at] = (x_in[rows(at), :].astype(F32) + mask * added)[:canvas].astype(BF16)
        return carry

    lax.fori_loop(0, canvas, step, 0, unroll=14)


def kernel_waves_stage(large, small, large_t, small_t, large_out, small_out, large_rows, small_rows):
    for kernel, table, out, flat in (
        (large, large_t, large_out, large_rows),
        (small, small_t, small_out, small_rows),
    ):
        side = kernel.shape[0]
        row = flat.shape[0] // side
        flat[...] = jnp.zeros_like(flat)
        for at in range(side):
            flat[at * row : at * row + side, :] = kernel[at]
        out[...] = ahead(table, flat[...])


def kernel_grad_stage(
    place, merged, merged_grad, large_sum, small_sum, large_t, small_t, other_out, mine_out, flat, proj_sum
):
    proj_sum[...] = dot_tn(merged[...], merged_grad[...])
    start = 0
    for total, table in ((large_sum, large_t), (small_sum, small_t)):
        size = table[0].shape[0]
        flat[start : start + size, :] = back(table, *halves(total[...]))
        start += size
    if start < flat.shape[0]:
        flat[start:, :] = jnp.zeros((flat.shape[0] - start, flat.shape[1]), F32)
    size, rest = flat.shape[0] // 2, proj_sum.shape[0] // 2
    for out, core in ((mine_out, place[0]), (other_out, 1 - place[0])):
        out[:size, :] = flat[pl.ds(pl.multiple_of(core * size, 8), size), :]
        out[size:, :] = proj_sum[pl.ds(pl.multiple_of(core * rest, 8), rest), :]


def kernel_grad_out_stage(settled, large_out, small_out, proj_out, flat, *, canvas):
    rest = proj_out.shape[0] // 2
    size = settled.shape[0] // 2 - rest
    for core in range(2):
        start = core * (size + rest)
        flat[core * size : (core + 1) * size, :] = settled[start : start + size, :]
        proj_out[core * rest : (core + 1) * rest, :] = settled[start + size : start + size + rest, :]
    start = 0
    for out in (large_out, small_out):
        side = out.shape[0]
        first, count = used_rows(side, canvas)
        out[...] = jnp.zeros_like(out)
        for at in range(first, first + count):
            out[at, first : first + count, :] = flat[start : start + count, :]
            start += count
        start = -(-start // 8) * 8


def weight_grad_stage(place, inputs, gradient, out):
    out[...] = dot_tn(inputs[...], gradient[...])


SMEM = pl.BlockSpec(memory_space=pltpu.SMEM)


def whole(shape):
    return pl.BlockSpec(shape, lambda at: (0,) * len(shape))


VMEM = 36 * 1024 * 1024


def call(kernel, crops, ins, outs, scratch):
    def spec(shape, kind):
        if kind == "smem":
            return SMEM
        if kind == "rows":
            return pl.BlockSpec((shape[0] // crops, shape[1]), lambda at: (at, 0))
        if kind == "map":
            return pl.BlockSpec((1,) + tuple(shape[1:]), lambda at: (at, 0, 0, 0))
        return whole(tuple(shape))

    flat, specs, places = [], [], []
    for value, kind in ins:
        group = value if isinstance(value, tuple) else (value,)
        places.append((len(flat), len(group) if isinstance(value, tuple) else 0))
        for part in group:
            if kind in ("rows", "apart"):
                part = pltpu.with_memory_space_constraint(part, pltpu.HBM)
            flat.append(part)
            specs.append(spec(part.shape, kind))

    def body(*refs):
        given = [refs[at : at + size] if size else refs[at] for at, size in places]
        kernel(*given, *refs[len(flat) :])

    return pl.pallas_call(
        body,
        grid=(crops,),
        in_specs=specs,
        out_specs=[spec(shape, kind) for shape, _, kind in outs],
        out_shape=[
            (pltpu.HBM if kind == "rows" else jax.ShapeDtypeStruct)(shape, dtype) for shape, dtype, kind in outs
        ],
        scratch_shapes=[pltpu.VMEM(shape, dtype) for shape, dtype in scratch],
        compiler_params=pltpu.CompilerParams(
            dimension_semantics=("arbitrary",), vmem_limit_bytes=VMEM
        ),
        cost_estimate=pl.CostEstimate(
            flops=0,
            bytes_accessed=sum(math.prod(part.shape) * part.dtype.itemsize for part in flat)
            + sum(math.prod(shape) * jnp.dtype(dtype).itemsize for shape, dtype, _ in outs),
            transcendentals=0,
        ),
        name=getattr(kernel, "func", kernel).__name__,
    )(*flat)


def weight_grad(inputs, gradient, place=None):
    deep, high = inputs.shape
    wide = gradient.shape[1]
    large = place is None
    if large:
        place = jnp.zeros((1,), jnp.int32)
        inputs = pltpu.with_memory_space_constraint(inputs, pltpu.HBM)
        gradient = pltpu.with_memory_space_constraint(gradient, pltpu.HBM)
    else:
        high = high // 2
    block, across = min(high, 512), min(wide, 512)
    return pl.pallas_call(
        weight_grad_stage,
        grid_spec=pltpu.PrefetchScalarGridSpec(
            num_scalar_prefetch=1,
            grid=(high // block, wide // across),
            in_specs=[
                pl.BlockSpec((deep, block), lambda i, j, place: (0, place[0] * (high // block) + i)),
                pl.BlockSpec((deep, across), lambda i, j, place: (0, j)),
            ],
            out_specs=pl.BlockSpec((block, across), lambda i, j, place: (i, j)),
        ),
        out_shape=pltpu.HBM((high, wide), F32) if large else jax.ShapeDtypeStruct((high, wide), F32),
        compiler_params=pltpu.CompilerParams(
            dimension_semantics=("arbitrary", "arbitrary"), vmem_limit_bytes=VMEM
        ),
        cost_estimate=pl.CostEstimate(
            flops=2 * deep * high * wide,
            bytes_accessed=2 * deep * (high + wide) + 4 * high * wide,
            transcendentals=0,
        ),
        name="weight_grad_stage",
    )(place, inputs, gradient)


def exchange(sent):
    return lax.all_to_all(sent, AXES, 0, 0, tiled=True)


SWAP = [(0, 1), (1, 0)]


def wide_exchange(mine, other, *beside):
    mine = mine + lax.ppermute(other, "core", SWAP)
    chips = lax.axis_size(("node", "chip"))
    copies = jnp.broadcast_to(mine[None], (chips,) + mine.shape)
    mine = jnp.sum(together(lax.all_to_all(copies, ("node", "chip"), 0, 0, tiled=True), *beside), axis=0)
    return mine, lax.ppermute(mine, "core", SWAP)


def sum_and_cut(arrays, place, ways):
    count, wide = arrays[0].shape
    part = count // ways

    def body(place, *refs):
        total = refs[0][...]
        for ref in refs[1 : len(arrays)]:
            total = total + ref[...]
        for at, out in enumerate(refs[len(arrays) :]):

            @pl.when(pl.program_id(0) == at)
            def _():
                out[...] = total

    return pl.pallas_call(
        body,
        grid_spec=pltpu.PrefetchScalarGridSpec(
            num_scalar_prefetch=1,
            grid=(ways,),
            in_specs=[pl.BlockSpec((part, wide), lambda at, place: (place[0] ^ at, 0))] * len(arrays),
            out_specs=[pl.BlockSpec((part, wide), lambda at, place: (0, 0))] * ways,
        ),
        out_shape=[jax.ShapeDtypeStruct((part, wide), F32)] * ways,
        compiler_params=pltpu.CompilerParams(dimension_semantics=("arbitrary",), vmem_limit_bytes=VMEM),
        cost_estimate=pl.CostEstimate(
            flops=0, bytes_accessed=4 * count * wide * (len(arrays) + 1), transcendentals=0
        ),
        name="sum_and_cut",
    )(place, *arrays)


def join(parts, place):
    part, wide = parts[0].shape
    ways = len(parts)

    def body(place, *refs):
        for at, ref in enumerate(refs[:ways]):

            @pl.when(pl.program_id(0) == at)
            def _():
                refs[ways][...] = ref[...]

    return pl.pallas_call(
        body,
        grid_spec=pltpu.PrefetchScalarGridSpec(
            num_scalar_prefetch=1,
            grid=(ways,),
            in_specs=[pl.BlockSpec((part, wide), lambda at, place: (0, 0))] * ways,
            out_specs=pl.BlockSpec((part, wide), lambda at, place: (place[0] ^ at, 0)),
        ),
        out_shape=jax.ShapeDtypeStruct((ways * part, wide), F32),
        compiler_params=pltpu.CompilerParams(dimension_semantics=("arbitrary",), vmem_limit_bytes=VMEM),
        cost_estimate=pl.CostEstimate(flops=0, bytes_accessed=8 * ways * part * wide, transcendentals=0),
        name="join",
    )(place, *parts)


def place_on(axis):
    return lax.axis_index(axis)[None]


def across(parts, axis):
    size = lax.axis_size(axis)
    return [
        lax.ppermute(part, axis, [(at, at ^ k) for at in range(size)]) if k else part
        for k, part in enumerate(parts)
    ]


class Settle:
    def __init__(self, other, mine, steps):
        half = mine.shape[0]
        self.first = mine
        if half % (8 * lax.axis_size(("node", "chip"))):
            first = lax.axis_index("core") == 0
            both = jnp.where(first, jnp.concatenate([mine, other]), jnp.concatenate([other, mine]))
            self.value = lax.psum(both, AXES)
            self.steps = []
        else:
            self.parts = [mine, lax.ppermute(other, "core", SWAP)]
            self.steps = list(steps)

    def chip(self):
        self.cut("chip")

    def node(self):
        self.cut("node")

    def cut(self, axis):
        self.parts = sum_and_cut(self.parts, place_on(axis), lax.axis_size(axis))
        self.mark = self.parts[0]
        self.parts = across(self.parts, axis)

    def piece(self):
        (self.mark,) = sum_and_cut(self.parts, place_on("node") * 0, 1)
        self.parts = across([self.mark] * lax.axis_size("node"), "node")

    def gather(self):
        (self.mark,) = sum_and_cut(self.parts, place_on("node") * 0, 1)
        self.value = lax.all_gather(self.mark, ("core", "chip", "node"), axis=0, tiled=True)

    def to_chip(self):
        self.join("node", "chip")

    def to_core(self):
        self.join("chip", "core")

    def end(self):
        self.value = self.mark = join(self.parts, place_on("core"))

    def join(self, axis, onward):
        self.mark = join(self.parts, place_on(axis))
        self.parts = across([self.mark] * lax.axis_size(onward), onward)

    def step(self, token):
        if not self.steps:
            return token
        self.parts, token = lax.optimization_barrier((self.parts, token))
        getattr(self, self.steps.pop(0))()
        return self.mark


BY_PERMUTES = ("chip", "node", "piece", "to_chip", "to_core", "end")
BY_GATHER = ("chip", "node", "gather")


def settle_weight_grad(inputs, gradient, steps):
    core = place_on("core")
    other = weight_grad(inputs, gradient, 1 - core)
    gradient, other = lax.optimization_barrier((gradient, other))
    mine = weight_grad(inputs, gradient, core)
    return Settle(other, mine, steps)


def turned(token, *weights):
    return [weight.T for weight in lax.optimization_barrier((weights, token))[0]]


def together(value, *tokens):
    return lax.optimization_barrier((value, tokens))[0]


def local(
    image, crop_sides, proj_in, kernel_large, kernel_small, proj_out, proj_up, proj_down,
    norm_gain, norm_shift, wide_gain, wide_shift, cotangent,
):
    crops, canvas, _, channels = image.shape
    wide = proj_up.shape[1]
    devices = lax.axis_size(AXES)
    cells = crops * canvas * ROW
    tables = wave_tables(canvas, kernel_large.shape[0], kernel_small.shape[0])
    half = tables["half"]

    def const(name):
        return tuple(jnp.asarray(part) for part in tables[name])

    ahead_t, back_t = const("ahead"), const("back")
    sides = (crop_sides, "smem")
    scale, offset = (norm_gain, "apart"), (norm_shift, "apart")
    wide_scale, wide_offset = (wide_gain[None], "apart"), (wide_shift[None], "apart")
    full, full_low = ((cells, channels), F32, "rows"), ((cells, channels), BF16, "rows")
    wide_low = ((cells, wide), BF16, "rows")
    wide_half = ((wide // 128, 128), F32, "whole")
    core = (place_on("core"), "smem")
    seen_out, wide_seen_out = ((8, channels), F32, "whole"), ((8, wide), F32, "whole")

    def send(count):
        return ((devices, -(-count // 1024) * 8, 128), F32, "whole")

    def coefs(count, width=channels):
        return ((count, 8, width), F32)

    def run(kernel, ins, outs, scratch):
        return call(kernel, crops, ins, outs, scratch)

    def r(value):
        return (value, "rows")

    def w(value):
        return (value, "whole")

    def apart(value):
        return (value, "apart")

    x, u, sent = run(
        enter_stage,
        [sides, (image, "map"), (cotangent, "map")],
        [full_low, full_low, send(2 * channels + 128)],
        [((2, canvas * ROW, channels), F32), coefs(2)],
    )
    came = exchange(sent)
    spectrum_out = ((2 * half, channels), F32, "whole")
    large_w, small_w = call(
        kernel_waves_stage,
        1,
        [apart(kernel_large), apart(kernel_small), apart(const("large")), apart(const("small"))],
        [spectrum_out, spectrum_out],
        [
            ((tables["large"][0].shape[1], channels), BF16),
            ((tables["small"][0].shape[1], channels), BF16),
        ],
    )
    came = together(came, large_w, small_w)
    pre_low, pre, sent, seen = run(
        first_stage,
        [sides, w(came), scale, offset, r(x), apart(proj_in)],
        [full_low, full, send(2 * channels), seen_out],
        [coefs(2), coefs(2)],
    )
    spectrum = ((2 * half, channels), F32)
    spectrum_low = ((2 * half, channels), BF16)
    down_t, out_t = turned(sent, proj_down, proj_out)
    came = together(exchange(sent), down_t, out_t)
    mixer_low, large, small, mixer_waves, sent, first_seen = run(
        mixer_stage,
        [sides, w(came), w(seen), scale, offset, r(pre), apart(ahead_t), apart(back_t), apart(large_w), apart(small_w)],
        [full_low, full, full, ((crops * 2 * half, channels), BF16, "rows"), send(4 * channels), seen_out],
        [coefs(2), coefs(4), spectrum, spectrum_low],
    )
    up_t, in_t = turned(sent, proj_up, proj_in)
    came = together(exchange(sent), up_t, in_t)
    merged_low, proj, sent, merge_seen = run(
        merge_stage,
        [sides, w(came), w(seen), scale, offset, r(large), r(small), r(x), r(u), apart(proj_out)],
        [full_low, full, send(4 * channels), seen_out],
        [coefs(3), coefs(4)],
    )
    ffn_low, hidden, mine, other, mid_seen = run(
        widen_stage,
        [sides, core, w(exchange(sent)), w(seen), scale, offset, r(x), r(proj), apart(proj_up)],
        [full_low, wide_low, wide_half, wide_half, seen_out],
        [coefs(3), coefs(2, wide), ((canvas * ROW, channels), F32)],
    )
    hidden_low, hidden_slope, last, sent, wide_seen = run(
        narrow_stage,
        [sides, core, w(wide_exchange(mine, other)), w(seen), wide_scale, wide_offset, r(hidden), r(u), apart(proj_down)],
        [wide_low, wide_low, full, send(4 * channels), wide_seen_out],
        [coefs(2, wide), coefs(4)],
    )
    down_low, hidden_grad, mine, other, last_seen = run(
        wide_back_stage,
        [
            sides, core, w(exchange(sent)), w(seen), scale, offset,
            r(last), r(u), r(hidden), r(hidden_slope), apart(down_t),
        ],
        [full_low, wide_low, wide_half, wide_half, seen_out],
        [coefs(3), coefs(2, wide), ((canvas * ROW, channels), F32)],
    )
    grad_down = weight_grad(hidden_low, down_low)
    came = wide_exchange(mine, other, grad_down)
    up_low, ffn_grad, sent, wide_noted = run(
        narrow_back_stage,
        [sides, core, w(came), w(wide_seen), wide_scale, r(hidden_grad), r(hidden), r(x), r(proj), apart(up_t)],
        [wide_low, full, send(3 * channels), wide_seen_out],
        [coefs(3, wide), coefs(3)],
    )
    came = exchange(sent)
    grad_up = weight_grad(ffn_low, up_low)
    came = together(came, grad_up)
    grad_down, grad_up = lax.psum((grad_down, grad_up), AXES)
    resid_grad, back_low, merged_grad, sent, mid_noted = run(
        mid_back_stage,
        [
            sides, w(came), w(seen), w(merge_seen), w(mid_seen), w(last_seen), scale, offset,
            r(x), r(u), r(proj), r(ffn_grad), r(large), r(small), apart(out_t),
        ],
        [full, full_low, full, send(3 * channels), seen_out],
        [coefs(7), coefs(3)],
    )
    came = exchange(sent)
    mixer_grad, large_sum, small_sum, sent, mixer_noted = run(
        mixer_back_stage,
        [
            sides, w(came), w(seen), w(merge_seen), w(first_seen), scale, offset,
            r(large), r(small), r(merged_grad), r(pre), r(mixer_waves), apart(ahead_t), apart(back_t), apart(large_w), apart(small_w),
        ],
        [full, spectrum_out, spectrum_out, send(2 * channels), seen_out],
        [
            coefs(6), coefs(2), ((canvas * ROW, channels), BF16), ((canvas * ROW, channels), BF16),
            spectrum, spectrum, spectrum_low,
        ],
    )
    came = exchange(sent)
    taps_t = (const("large_back"), const("small_back"))
    tap_rows = sum(table[0].shape[0] for table in taps_t)
    tap_rows = -(-tap_rows // (8 * devices)) * 8 * devices
    half_taps = (((tap_rows + channels) // 2, channels), F32, "whole")
    other, mine = call(
        kernel_grad_stage,
        1,
        [core, w(merged_low), w(back_low), w(large_sum), w(small_sum), apart(taps_t[0]), apart(taps_t[1])],
        [half_taps, half_taps],
        [((tap_rows, channels), F32), ((channels, channels), F32)],
    )
    came = together(came, other, mine)
    settle_taps = Settle(other, mine, BY_PERMUTES)
    pre_round, first_grad, sent, first_noted = run(
        first_back_stage,
        [sides, w(came), w(seen), w(first_seen), scale, r(mixer_grad), r(pre), r(x), apart(in_t)],
        [full_low, full, send(2 * channels), seen_out],
        [coefs(3), coefs(2)],
    )
    settle_in = settle_weight_grad(pre_low, pre_round, BY_PERMUTES)
    came = exchange(together(sent, settle_in.first))
    token = settle_in.step(settle_taps.step(settle_in.first))
    (block_out,) = run(
        block_out_stage,
        [sides, w(mid_seen), w(last_seen), scale, offset, r(x), r(proj), r(together(last, token))],
        [(image.shape, BF16, "map")],
        [],
    )
    token = settle_in.step(settle_taps.step(block_out))
    came = together(came, token)
    grad_image, enter_noted = run(
        leave_stage,
        [sides, w(came), w(seen), scale, r(resid_grad), r(first_grad), r(x)],
        [(image.shape, F32, "map"), seen_out],
        [coefs(3)],
    )
    token = grad_image
    while settle_in.steps or settle_taps.steps:
        token = settle_in.step(settle_taps.step(token))
    grad_in = settle_in.value
    grad_large, grad_small, grad_out = call(
        functools.partial(kernel_grad_out_stage, canvas=canvas),
        1,
        [w(settle_taps.value)],
        [(kernel_large.shape, F32, "whole"), (kernel_small.shape, F32, "whole"), (proj_out.shape, F32, "whole")],
        [((tap_rows, channels), F32)],
    )
    gain_grads = jnp.stack(
        [enter_noted[0], first_noted[0], mixer_noted[0], mixer_noted[1], mid_noted[2], mid_noted[0], last_seen[3]]
    )
    shift_grads = jnp.stack(
        [enter_noted[1], first_noted[1], mixer_noted[2], mixer_noted[2], mid_noted[3], mid_noted[1], last_seen[2]]
    )
    return (
        block_out, grad_image, grad_in, grad_large, grad_small, grad_out, grad_up, grad_down,
        gain_grads, shift_grads, wide_noted[0], wide_noted[1],
    )


def solution(mesh):
    nodes, devices = mesh.devices.shape
    chips = jax.sharding.Mesh(mesh.devices.reshape(nodes, devices // 2, 2), AXES)
    maps = P(AXES, None, None, None)
    return jax.shard_map(
        local,
        mesh=chips,
        in_specs=(maps, P(AXES)) + (P(),) * 10 + (maps,),
        out_specs=(maps, maps) + (P(),) * 10,
        check_vma=False,
    )
```

```python
import functools
import math

import jax
import jax.numpy as jnp
import ml_dtypes
import numpy as np
from jax import lax
from jax.experimental import pallas as pl
from jax.experimental.pallas import tpu as pltpu
from jax.sharding import PartitionSpec as P

EPSILON = 1e-05
ROOT = 0.7978845608028654
CUBIC = 0.044715
AXES = ("node", "chip", "core")
ROW = 16
F32 = jnp.float32
BF16 = jnp.bfloat16


def split(table):
    high = table.astype(ml_dtypes.bfloat16)
    low = (table - high.astype(np.float64)).astype(ml_dtypes.bfloat16)
    return high, low


@functools.lru_cache(maxsize=None)
def wave_tables(canvas, side_large, side_small):
    period = 2 * canvas - 1
    pairs = [(0, v) for v in range(canvas)]
    pairs += [(u, v) for u in range(1, canvas) for v in range(period)]
    waves = np.array(pairs)
    half = -(-len(pairs) // 16) * 16

    def table(places_h, places_w, keep, sign):
        grid = np.stack(np.meshgrid(places_h, places_w, indexing="ij"), -1).reshape(-1, 2)
        angle = 2 * np.pi * ((waves @ grid.T) % period) / period
        out = np.zeros((2 * half, grid.shape[0]))
        out[: len(pairs)] = np.cos(angle) * keep
        out[half : half + len(pairs)] = sign * np.sin(angle) * keep
        return out

    share = np.zeros((2 * half, 1))
    share[: len(pairs)] = 2.0 / period**2
    share[half : half + len(pairs)] = 2.0 / period**2
    share[0] = 1.0 / period**2

    inside = (np.arange(ROW) < canvas).astype(np.float64)
    cells = table(np.arange(canvas), np.arange(ROW), np.tile(inside, canvas), -1.0)

    def taps(side, row):
        middle = (side - 1) // 2
        offsets_h = np.arange(side) - middle
        offsets_w = np.arange(row) - middle
        keep = (np.abs(offsets_h) < canvas)[:, None] & (np.abs(offsets_w) < canvas)[None, :]
        keep = keep & (np.arange(row) < side)[None, :]
        return table(offsets_h, offsets_w, keep.reshape(-1).astype(np.float64), 1.0)

    def taps_back(side):
        first, count = used_rows(side, canvas)
        every = taps(side, side).reshape(2 * half, side, side)
        used = every[:, first : first + count, first : first + count].reshape(2 * half, -1)
        return np.pad(used, ((0, 0), (0, -used.shape[1] % 8)))

    def tap_row(side):
        return -(-side // 16) * 16

    large = taps(side_large, tap_row(side_large))
    small = taps(side_small, tap_row(side_small))
    turn = np.ones((2 * half, 1))
    turn[half:] = -1.0
    return dict(
        half=half,
        ahead=split(cells),
        back=split((cells * share).T),
        large=split(large),
        small=split(small),
        large_back=split((taps_back(side_large) * turn * share).T),
        small_back=split((taps_back(side_small) * turn * share).T),
    )


def used_rows(side, canvas):
    first = max(0, (side - 1) // 2 - (canvas - 1))
    return first, side - 2 * first


def dot(left, right):
    return jnp.dot(left, right, preferred_element_type=F32)


def dot_nt(left, right):
    return lax.dot_general(left, right, (((1,), (1,)), ((), ())), preferred_element_type=F32)


def dot_tn(left, right):
    return lax.dot_general(left, right, (((0,), (0,)), ((), ())), preferred_element_type=F32)


def halves(values):
    high = values.astype(BF16)
    return high, (values - high.astype(F32)).astype(BF16)


def gelu(values):
    inner = values * (ROOT + (ROOT * CUBIC) * (values * values))
    return values * (0.5 + 0.5 * jnp.tanh(inner))


def gelu_and_slope(values):
    square = values * values
    bend = jnp.tanh(values * (ROOT + (ROOT * CUBIC) * square))
    slope = ROOT + (3.0 * ROOT * CUBIC) * square
    half = 0.5 + 0.5 * bend
    return values * half, half * (1.0 + values * slope * (1.0 - bend))


def gelu_slope(values):
    square = values * values
    bend = jnp.tanh(values * (ROOT + (ROOT * CUBIC) * square))
    slope = ROOT + (3.0 * ROOT * CUBIC) * square
    return 0.5 + 0.5 * bend + values * slope * (0.5 - 0.5 * bend * bend)


def rows(at):
    return pl.ds(pl.multiple_of(at * ROW, ROW), ROW)


def fold(values):
    return values[:8] + values[8:]


def twice(values):
    return jnp.concatenate([values, values], axis=0)


def columns_inside(side, channels):
    places = lax.broadcasted_iota(jnp.int32, (ROW, 128), 0)
    inside = (places < side).astype(F32)
    return jnp.concatenate([inside] * (channels // 128), axis=1)


def first_step():
    return pl.program_id(0) == 0


def last_step():
    return pl.program_id(0) == pl.num_programs(0) - 1


def to_tiles(parts):
    lines = [part[:, at : at + 128] for part in parts for at in range(0, part.shape[1], 128)]
    lines += [jnp.zeros_like(lines[0])] * (-len(lines) % 8)
    return jnp.concatenate(lines, axis=0)


def from_tiles(tiles, count, width):
    tiles = [tiles[at : at + 1] for at in range(count * width // 128)]
    many = width // 128
    return [jnp.concatenate(tiles[at * many : (at + 1) * many], axis=1) for at in range(count)]


def received(sent, count, width):
    return from_tiles(jnp.sum(sent[...], axis=0), count, width)


def keep(coefs, values):
    for at, value in enumerate(values):
        coefs[at] = jnp.broadcast_to(value, coefs.shape[1:])


def note(out, values):
    values = list(values)
    values += [jnp.zeros_like(values[0])] * (out.shape[0] - len(values))
    out[...] = jnp.concatenate(values, axis=0)


def add_sums(sums, parts):
    @pl.when(first_step())
    def _():
        sums[...] = jnp.zeros_like(sums)

    for at, part in enumerate(parts):
        sums[at] += part


def publish(sums, out, extra=()):
    @pl.when(last_step())
    def _():
        parts = [jnp.sum(sums[at], axis=0, keepdims=True) for at in range(sums.shape[0])]
        parts += list(extra)
        out[...] = jnp.broadcast_to(to_tiles(parts)[None], out.shape)


def norm_coefs(column_sum, square, count, scaling, offsets):
    mean = column_sum / count
    reciprocal = lax.rsqrt(square / count - mean * mean + EPSILON)
    factor = scaling * reciprocal
    return mean, reciprocal, factor, offsets - mean * factor


def back_coefs(shift_sum, gain_sum, count, mean, reciprocal, scaling):
    factor = scaling * reciprocal
    slope = factor * reciprocal * gain_sum / count
    return factor, factor * shift_sum / count - slope * mean, slope


def zeros(count, channels):
    return tuple(jnp.zeros((8, channels), F32) for _ in range(count))


def enter_stage(sides, image, cotangent, x_out, u_out, sent, padded, sums):
    at_crop = pl.program_id(0)
    side = sides[at_crop]
    canvas, channels = image.shape[1], image.shape[3]
    inside = columns_inside(side, channels)

    @pl.when(first_step())
    def _():
        padded[...] = jnp.zeros_like(padded)

    def step(at, carry):
        mask = jnp.where(at < side, inside, 0.0)
        start = pl.multiple_of(at * ROW, ROW)
        padded[0, pl.ds(start, canvas), :] = image[0, at].astype(F32)
        padded[1, pl.ds(start, canvas), :] = cotangent[0, at].astype(F32)
        x = padded[0, rows(at), :] * mask
        u = padded[1, rows(at), :] * mask
        x_out[rows(at), :] = x.astype(BF16)
        u_out[rows(at), :] = u.astype(BF16)
        return carry[0] + fold(x), carry[1] + fold(x * x)

    add_sums(sums, lax.fori_loop(0, canvas, step, zeros(2, channels), unroll=14))
    count = jnp.int32(0)
    for at in range(sides.shape[0]):
        count += sides[at] * sides[at]
    publish(sums, sent, [jnp.full((1, 128), count.astype(F32))])


def first_stage(sides, came, scale, offset, x_in, weight, low_out, pre_out, sent, seen, coefs, sums):
    channels = x_in.shape[1]
    canvas = x_in.shape[0] // ROW
    side = sides[pl.program_id(0)]

    @pl.when(first_step())
    def _():
        tiles = channels // 128
        parts = received(came, 2 * tiles + 1, 128)
        column_sum = jnp.concatenate(parts[:tiles], axis=1)
        square = jnp.concatenate(parts[tiles : 2 * tiles], axis=1)
        count = jnp.concatenate([parts[2 * tiles]] * tiles, axis=1)
        mean, reciprocal, factor, constant = norm_coefs(column_sum, square, count, scale[0:1], offset[0:1])
        keep(coefs, [factor, constant])
        note(seen, [count, mean, reciprocal, column_sum, square])

    inside = columns_inside(side, channels)
    factor, constant = twice(coefs[0]), twice(coefs[1])

    def step(at, carry):
        mask = jnp.where(at < side, inside, 0.0)
        low_out[rows(at), :] = (mask * (factor * x_in[rows(at), :].astype(F32) + constant)).astype(BF16)
        return carry

    lax.fori_loop(0, canvas, step, 0, unroll=14)
    pre_out[...] = dot(low_out[...], weight[...])

    def measure(at, carry):
        pre = pre_out[rows(at), :]
        return carry[0] + fold(pre), carry[1] + fold(pre * pre)

    add_sums(sums, lax.fori_loop(0, canvas, measure, zeros(2, channels), unroll=14))
    publish(sums, sent)


def times(spectrum, kernel, half, at, conj):
    real, imag = pl.ds(pl.multiple_of(at * 16, 16), 16), pl.ds(pl.multiple_of(half + at * 16, 16), 16)
    a, b = spectrum[real, :], spectrum[imag, :]
    c, d = kernel[real, :], kernel[imag, :]
    if conj:
        return real, imag, a * c + b * d, b * c - a * d
    return real, imag, a * c - b * d, a * d + b * c


def ahead_once(tables, values):
    return dot(tables[0][...], values)


def back_once(tables, values):
    return dot(tables[0][...], values.astype(BF16))


def ahead(tables, values):
    return dot(tables[0][...], values) + dot(tables[1][...], values)


def back(tables, high, low):
    return dot(tables[0][...], high) + dot(tables[0][...], low) + dot(tables[1][...], high)


def mixer_stage(
    sides, came, seen, scale, offset, pre_in, ahead_t, back_t, large_w, small_w,
    low_out, large_out, small_out, waves_out, sent, noted, coefs, sums, spectrum, high,
):
    channels = pre_in.shape[1]
    canvas = pre_in.shape[0] // ROW
    half = spectrum.shape[0] // 2
    side = sides[pl.program_id(0)]

    @pl.when(first_step())
    def _():
        mean, reciprocal, factor, constant = norm_coefs(
            *received(came, 2, channels), seen[0:1], scale[1:2], offset[1:2]
        )
        keep(coefs, [factor, constant])
        note(noted, [mean, reciprocal])

    inside = columns_inside(side, channels)
    factor, constant = twice(coefs[0]), twice(coefs[1])

    def step(at, carry):
        mask = jnp.where(at < side, inside, 0.0)
        low_out[rows(at), :] = gelu(mask * (factor * pre_in[rows(at), :] + constant)).astype(BF16)
        return carry

    lax.fori_loop(0, canvas, step, 0, unroll=14)
    spectrum[...] = ahead(ahead_t, low_out[...])
    waves_out[...] = spectrum[...].astype(BF16)
    parts = ()
    for kernel, out in ((large_w, large_out), (small_w, small_out)):

        def product(at, carry):
            real, imag, new_real, new_imag = times(spectrum, kernel, half, at, False)
            high[real, :] = new_real.astype(BF16)
            high[imag, :] = new_imag.astype(BF16)
            return carry

        lax.fori_loop(0, half // 16, product, 0, unroll=23)
        out[...] = ahead(back_t, high[...])

        def measure(at, carry):
            conv = jnp.where(at < side, inside, 0.0) * out[rows(at), :]
            out[rows(at), :] = conv
            return carry[0] + fold(conv), carry[1] + fold(conv * conv)

        parts += lax.fori_loop(0, canvas, measure, zeros(2, channels), unroll=14)
    add_sums(sums, parts)
    publish(sums, sent)


def merge_stage(
    sides, came, seen, scale, offset, large_in, small_in, x_in, u_in, weight,
    low_out, proj_out, sent, noted, coefs, sums,
):
    channels = x_in.shape[1]
    canvas = x_in.shape[0] // ROW
    side = sides[pl.program_id(0)]

    @pl.when(first_step())
    def _():
        large_sum, large_square, small_sum, small_square = received(came, 4, channels)
        large = norm_coefs(large_sum, large_square, seen[0:1], scale[2:3], offset[2:3])
        small = norm_coefs(small_sum, small_square, seen[0:1], scale[3:4], offset[3:4])
        keep(coefs, [large[2], small[2], large[3] + small[3]])
        note(noted, [large[0], large[1], small[0], small[1], large[2], small[2], large[3] + small[3]])

    inside = columns_inside(side, channels)
    large, small, constant = twice(coefs[0]), twice(coefs[1]), twice(coefs[2])

    def step(at, carry):
        mask = jnp.where(at < side, inside, 0.0)
        merged = mask * (large * large_in[rows(at), :] + small * small_in[rows(at), :] + constant)
        low_out[rows(at), :] = gelu(merged).astype(BF16)
        return carry

    lax.fori_loop(0, canvas, step, 0, unroll=14)
    proj_out[...] = dot(low_out[...], weight[...])

    def measure(at, carry):
        proj = proj_out[rows(at), :]
        x, u = x_in[rows(at), :].astype(F32), u_in[rows(at), :].astype(F32)
        parts = (proj, proj * proj, proj * x, proj * u)
        return tuple(old + fold(part) for old, part in zip(carry, parts))

    add_sums(sums, lax.fori_loop(0, canvas, measure, zeros(4, channels), unroll=14))
    publish(sums, sent)


def widen_stage(
    sides, core, came, seen, scale, offset, x_in, proj_in, weight,
    low_out, hidden_out, mine, other, noted, coefs, sums, found,
):
    channels = x_in.shape[1]
    canvas = x_in.shape[0] // ROW
    side = sides[pl.program_id(0)]

    @pl.when(first_step())
    def _():
        proj_sum, proj_square, cross, _ = parts = received(came, 4, channels)
        count, x_mean, x_sum, x_square = seen[0:1], seen[1:2], seen[3:4], seen[4:5]
        mean, reciprocal, factor, constant = norm_coefs(
            proj_sum, proj_square, count, scale[4:5], offset[4:5]
        )
        mid_mean = x_mean + factor * mean + constant
        x_var = x_square / count - x_mean * x_mean
        proj_var = proj_square / count - mean * mean
        both = cross / count - x_mean * mean
        mid_var = x_var + factor * factor * proj_var + 2.0 * factor * both
        mid_reciprocal = lax.rsqrt(mid_var + EPSILON)
        mid_factor = scale[5:6] * mid_reciprocal
        keep(coefs, [mid_factor, mid_factor * factor, mid_factor * (constant - mid_mean) + offset[5:6]])
        note(noted, [mean, reciprocal, mid_mean, mid_reciprocal] + parts)

    inside = columns_inside(side, channels)
    from_x, from_proj, constant = twice(coefs[0]), twice(coefs[1]), twice(coefs[2])

    def step(at, carry):
        mask = jnp.where(at < side, inside, 0.0)
        x = x_in[rows(at), :].astype(F32)
        low_out[rows(at), :] = (mask * (from_x * x + from_proj * proj_in[rows(at), :] + constant)).astype(BF16)
        return carry

    lax.fori_loop(0, canvas, step, 0, unroll=14)
    parts = [[], []]
    for at_block in range(hidden_out.shape[1] // channels):
        block = slice(at_block * channels, (at_block + 1) * channels)
        found[...] = dot(low_out[...], weight[:, block])

        def measure(at, carry):
            hidden = found[rows(at), :]
            hidden_out[rows(at), block] = hidden.astype(BF16)
            return carry[0] + fold(hidden), carry[1] + fold(hidden * hidden)

        pair = lax.fori_loop(0, canvas, measure, zeros(2, channels), unroll=14)
        parts[0].append(pair[0])
        parts[1].append(pair[1])
    add_sums(sums, [jnp.concatenate(part, axis=1) for part in parts])
    hand_over(sums, core, mine, other)


def hand_over(sums, core, mine, other):
    @pl.when(last_step())
    def _():
        first, second = (to_tiles([jnp.sum(sums[at], axis=0, keepdims=True)]) for at in range(2))
        mine[...] = jnp.where(core[0] == 0, first, second)
        other[...] = jnp.where(core[0] == 0, second, first)


def taken_over(core, came):
    mine, other = came[0][...], came[1][...]
    wide = mine.size
    first = jnp.where(core[0] == 0, mine, other)
    second = jnp.where(core[0] == 0, other, mine)
    return from_tiles(first, 1, wide)[0], from_tiles(second, 1, wide)[0]


def narrow_stage(
    sides, core, came, seen, wide_scale, wide_offset, hidden_in, u_in, weight,
    low_out, slope_out, proj_out, sent, noted, coefs, sums,
):
    channels = u_in.shape[1]
    canvas = u_in.shape[0] // ROW
    wide = hidden_in.shape[1]
    side = sides[pl.program_id(0)]

    @pl.when(first_step())
    def _():
        count = jnp.concatenate([seen[0:1]] * (wide // channels), axis=1)
        mean, reciprocal, factor, constant = norm_coefs(
            *taken_over(core, came), count, wide_scale[...], wide_offset[...]
        )
        keep(coefs, [factor, constant])
        note(noted, [mean, reciprocal, factor, constant, count])

    for at_block in range(wide // channels):
        block = slice(at_block * channels, (at_block + 1) * channels)
        factor, constant = twice(coefs[0, :, block]), twice(coefs[1, :, block])

        def step(at, carry):
            hidden = hidden_in[rows(at), block].astype(F32)
            value, slope = gelu_and_slope(factor * hidden + constant)
            low_out[rows(at), block] = value.astype(BF16)
            slope_out[rows(at), block] = slope.astype(BF16)
            return carry

        lax.fori_loop(0, canvas, step, 0, unroll=14)
    proj_out[...] = dot(low_out[...], weight[...])
    inside = columns_inside(side, channels)

    def measure(at, carry):
        proj = jnp.where(at < side, inside, 0.0) * proj_out[rows(at), :]
        proj_out[rows(at), :] = proj
        u = u_in[rows(at), :].astype(F32)
        parts = (proj, proj * proj, proj * u, u)
        return tuple(old + fold(part) for old, part in zip(carry, parts))

    add_sums(sums, lax.fori_loop(0, canvas, measure, zeros(4, channels), unroll=14))
    publish(sums, sent)


def wide_back_stage(
    sides, core, came, seen, scale, offset, proj_in, u_in, hidden_in, slope_in, weight,
    down_out, grad_out, mine, other, noted, coefs, sums, found,
):
    channels = u_in.shape[1]
    canvas = u_in.shape[0] // ROW
    wide = hidden_in.shape[1]
    side = sides[pl.program_id(0)]

    @pl.when(first_step())
    def _():
        proj_sum, proj_square, cross, u_sum = received(came, 4, channels)
        count = seen[0:1]
        mean, reciprocal, factor, constant = norm_coefs(
            proj_sum, proj_square, count, scale[6:7], offset[6:7]
        )
        gain_sum = reciprocal * (cross - mean * u_sum)
        keep(coefs, back_coefs(u_sum, gain_sum, count, mean, reciprocal, scale[6:7]))
        note(noted, [mean, reciprocal, u_sum, gain_sum, factor, constant])

    inside = columns_inside(side, channels)
    factor, constant, slope = twice(coefs[0]), twice(coefs[1]), twice(coefs[2])

    def step(at, carry):
        mask = jnp.where(at < side, inside, 0.0)
        u = u_in[rows(at), :].astype(F32)
        down_out[rows(at), :] = (mask * (factor * u - constant - slope * proj_in[rows(at), :])).astype(BF16)
        return carry

    lax.fori_loop(0, canvas, step, 0, unroll=14)
    parts = [[], []]
    for at_block in range(wide // channels):
        block = slice(at_block * channels, (at_block + 1) * channels)
        found[...] = dot(down_out[...], weight[:, block])

        def measure(at, carry):
            hidden = hidden_in[rows(at), block].astype(F32)
            grad = found[rows(at), :] * slope_in[rows(at), block].astype(F32)
            grad_out[rows(at), block] = grad.astype(BF16)
            return carry[0] + fold(grad), carry[1] + fold(grad * hidden)

        pair = lax.fori_loop(0, canvas, measure, zeros(2, channels), unroll=14)
        parts[0].append(pair[0])
        parts[1].append(pair[1])
    add_sums(sums, [jnp.concatenate(part, axis=1) for part in parts])
    hand_over(sums, core, mine, other)


def narrow_back_stage(
    sides, core, came, wide_seen, wide_scale, grad_in, hidden_in, x_in, proj_in, weight,
    up_out, ffn_out, sent, noted, coefs, sums,
):
    channels = x_in.shape[1]
    canvas = x_in.shape[0] // ROW
    wide = hidden_in.shape[1]
    side = sides[pl.program_id(0)]

    @pl.when(first_step())
    def _():
        mean, reciprocal, count = wide_seen[0:1], wide_seen[1:2], wide_seen[4:5]
        shift_sum, with_hidden = taken_over(core, came)
        gain_sum = reciprocal * (with_hidden - mean * shift_sum)
        keep(coefs, back_coefs(shift_sum, gain_sum, count, mean, reciprocal, wide_scale[...]))
        note(noted, [gain_sum, shift_sum])

    for at_block in range(wide // channels):
        block = slice(at_block * channels, (at_block + 1) * channels)
        factor, constant, slope = (twice(coefs[at, :, block]) for at in range(3))

        def step(at, carry):
            grad = factor * grad_in[rows(at), block].astype(F32) - constant
            grad = grad - slope * hidden_in[rows(at), block].astype(F32)
            up_out[rows(at), block] = grad.astype(BF16)
            return carry

        lax.fori_loop(0, canvas, step, 0, unroll=14)
    ffn_out[...] = dot(up_out[...], weight[...])
    inside = columns_inside(side, channels)

    def measure(at, carry):
        grad = jnp.where(at < side, inside, 0.0) * ffn_out[rows(at), :]
        ffn_out[rows(at), :] = grad
        parts = (grad, grad * x_in[rows(at), :].astype(F32), grad * proj_in[rows(at), :])
        return tuple(old + fold(part) for old, part in zip(carry, parts))

    add_sums(sums, lax.fori_loop(0, canvas, measure, zeros(3, channels), unroll=14))
    publish(sums, sent)


def mid_back_stage(
    sides, came, seen, merge_seen, mid_seen, last_seen, scale, offset,
    x_in, u_in, proj_in, ffn_in, large_in, small_in, weight,
    resid_out, back_out, grad_out, sent, noted, coefs, sums,
):
    channels = x_in.shape[1]
    canvas = x_in.shape[0] // ROW
    side = sides[pl.program_id(0)]

    @pl.when(first_step())
    def _():
        ffn_sum, ffn_x, ffn_proj = received(came, 3, channels)
        count, u_sum = seen[0:1], last_seen[2:3]
        mean, reciprocal, mid_mean, mid_reciprocal = (mid_seen[at : at + 1] for at in range(4))
        proj_sum, proj_square, cross, proj_u = (mid_seen[at : at + 1] for at in range(4, 8))
        proj_factor = scale[4:5] * reciprocal
        proj_constant = offset[4:5] - mean * proj_factor
        ffn_mid = ffn_x + proj_factor * ffn_proj + proj_constant * ffn_sum
        mid_gain = mid_reciprocal * (ffn_mid - mid_mean * ffn_sum)
        factor, constant, slope = back_coefs(ffn_sum, mid_gain, count, mid_mean, mid_reciprocal, scale[5:6])
        mid_proj = cross + proj_factor * proj_square + proj_constant * proj_sum
        resid_sum = u_sum
        resid_proj = proj_u + factor * ffn_proj - constant * proj_sum - slope * mid_proj
        gain = reciprocal * (resid_proj - mean * resid_sum)
        second = back_coefs(resid_sum, gain, count, mean, reciprocal, scale[4:5])
        keep(coefs, [factor, constant + slope * proj_constant, slope, slope * proj_factor, *second])
        note(noted, [mid_gain, ffn_sum, gain, resid_sum])

    inside = columns_inside(side, channels)

    def step(at, carry):
        mask = jnp.where(at < side, inside, 0.0)
        x, u = x_in[rows(at), :].astype(F32), u_in[rows(at), :].astype(F32)
        proj = proj_in[rows(at), :]
        resid = twice(coefs[0]) * ffn_in[rows(at), :] - twice(coefs[1]) - twice(coefs[2]) * x
        resid = u + mask * (resid - twice(coefs[3]) * proj)
        resid_out[rows(at), :] = resid
        down = twice(coefs[4]) * resid - twice(coefs[5]) - twice(coefs[6]) * proj
        back_out[rows(at), :] = (mask * down).astype(BF16)
        return carry

    lax.fori_loop(0, canvas, step, 0, unroll=14)
    grad_out[...] = dot(back_out[...], weight[...])
    large = jnp.broadcast_to(merge_seen[4:5], (ROW, channels))
    small = jnp.broadcast_to(merge_seen[5:6], (ROW, channels))
    constant = jnp.broadcast_to(merge_seen[6:7], (ROW, channels))

    def measure(at, carry):
        large_conv, small_conv = large_in[rows(at), :], small_in[rows(at), :]
        grad = grad_out[rows(at), :] * gelu_slope(large * large_conv + small * small_conv + constant)
        grad_out[rows(at), :] = grad
        parts = (grad, grad * large_conv, grad * small_conv)
        return tuple(old + fold(part) for old, part in zip(carry, parts))

    add_sums(sums, lax.fori_loop(0, canvas, measure, zeros(3, channels), unroll=14))
    publish(sums, sent)


def mixer_back_stage(
    sides, came, seen, merge_seen, first_seen, scale, offset, large_in, small_in, grad_in, pre_in, waves_in,
    ahead_t, back_t, large_w, small_w,
    grad_out, large_sum, small_sum, sent, noted, coefs, sums, large_out, small_out, large_s, small_s, summed,
):
    channels = pre_in.shape[1]
    canvas = pre_in.shape[0] // ROW
    half = large_s.shape[0] // 2
    side = sides[pl.program_id(0)]

    @pl.when(first_step())
    def _():
        shift_sum, with_large, with_small = received(came, 3, channels)
        count = seen[0:1]
        large_mean, large_r, small_mean, small_r = (merge_seen[at : at + 1] for at in range(4))
        large_gain = large_r * (with_large - large_mean * shift_sum)
        small_gain = small_r * (with_small - small_mean * shift_sum)
        keep(
            coefs,
            [
                *back_coefs(shift_sum, large_gain, count, large_mean, large_r, scale[2:3]),
                *back_coefs(shift_sum, small_gain, count, small_mean, small_r, scale[3:4]),
            ],
        )
        note(noted, [large_gain, small_gain, shift_sum])

    inside = columns_inside(side, channels)

    def step(at, carry):
        mask = jnp.where(at < side, inside, 0.0)
        grad = grad_in[rows(at), :]
        large = twice(coefs[0]) * grad - twice(coefs[1]) - twice(coefs[2]) * large_in[rows(at), :]
        small = twice(coefs[3]) * grad - twice(coefs[4]) - twice(coefs[5]) * small_in[rows(at), :]
        large_out[rows(at), :] = (mask * large).astype(BF16)
        small_out[rows(at), :] = (mask * small).astype(BF16)
        return carry

    lax.fori_loop(0, canvas, step, 0, unroll=14)
    large_s[...] = ahead_once(ahead_t, large_out[...])
    small_s[...] = ahead_once(ahead_t, small_out[...])

    def product(at, carry):
        real, imag, one_real, one_imag = times(large_s, large_w, half, at, True)
        _, _, two_real, two_imag = times(small_s, small_w, half, at, True)
        summed[real, :] = (one_real + two_real).astype(BF16)
        summed[imag, :] = (one_imag + two_imag).astype(BF16)
        a, b = waves_in[real, :].astype(F32), waves_in[imag, :].astype(F32)
        for total, spectrum in ((large_sum, large_s), (small_sum, small_s)):
            c, d = spectrum[real, :], spectrum[imag, :]
            total[real, :] += a * c + b * d
            total[imag, :] += b * c - a * d
        return carry

    @pl.when(first_step())
    def _():
        large_sum[...] = jnp.zeros_like(large_sum)
        small_sum[...] = jnp.zeros_like(small_sum)

    lax.fori_loop(0, half // 16, product, 0, unroll=23)
    grad_out[...] = back_once(back_t, summed[...])
    reciprocal = first_seen[1:2]
    factor = scale[1:2] * reciprocal
    constant = jnp.broadcast_to(offset[1:2] - first_seen[0:1] * factor, (ROW, channels))
    factor = jnp.broadcast_to(factor, (ROW, channels))

    def measure(at, carry):
        mask = jnp.where(at < side, inside, 0.0)
        pre = pre_in[rows(at), :]
        grad = mask * grad_out[rows(at), :] * gelu_slope(factor * pre + constant)
        grad_out[rows(at), :] = grad
        return carry[0] + fold(grad), carry[1] + fold(grad * pre)

    add_sums(sums, lax.fori_loop(0, canvas, measure, zeros(2, channels), unroll=14))
    publish(sums, sent)


def first_back_stage(
    sides, came, seen, first_seen, scale, grad_in, pre_in, x_in, weight,
    low_out, grad_out, sent, noted, coefs, sums,
):
    channels = pre_in.shape[1]
    canvas = pre_in.shape[0] // ROW
    side = sides[pl.program_id(0)]

    @pl.when(first_step())
    def _():
        shift_sum, with_pre = received(came, 2, channels)
        mean, reciprocal = first_seen[0:1], first_seen[1:2]
        gain_sum = reciprocal * (with_pre - mean * shift_sum)
        keep(coefs, back_coefs(shift_sum, gain_sum, seen[0:1], mean, reciprocal, scale[1:2]))
        note(noted, [gain_sum, shift_sum])

    inside = columns_inside(side, channels)
    factor, constant, slope = twice(coefs[0]), twice(coefs[1]), twice(coefs[2])

    def step(at, carry):
        mask = jnp.where(at < side, inside, 0.0)
        grad = factor * grad_in[rows(at), :] - constant - slope * pre_in[rows(at), :]
        low_out[rows(at), :] = (mask * grad).astype(BF16)
        return carry

    lax.fori_loop(0, canvas, step, 0, unroll=14)
    grad_out[...] = dot(low_out[...], weight[...])

    def measure(at, carry):
        grad = grad_out[rows(at), :]
        return carry[0] + fold(grad), carry[1] + fold(grad * x_in[rows(at), :].astype(F32))

    add_sums(sums, lax.fori_loop(0, canvas, measure, zeros(2, channels), unroll=14))
    publish(sums, sent)


def leave_stage(sides, came, seen, scale, resid_in, grad_in, x_in, image_out, noted, coefs):
    channels = x_in.shape[1]
    canvas = x_in.shape[0] // ROW
    side = sides[pl.program_id(0)]

    @pl.when(first_step())
    def _():
        shift_sum, with_x = received(came, 2, channels)
        count, mean, reciprocal = (seen[at : at + 1] for at in range(3))
        gain_sum = reciprocal * (with_x - mean * shift_sum)
        keep(coefs, back_coefs(shift_sum, gain_sum, count, mean, reciprocal, scale[0:1]))
        note(noted, [gain_sum, shift_sum])

    inside = columns_inside(side, channels)
    factor, constant, slope = twice(coefs[0]), twice(coefs[1]), twice(coefs[2])

    def step(at, carry):
        mask = jnp.where(at < side, inside, 0.0)
        grad = factor * grad_in[rows(at), :] - constant - slope * x_in[rows(at), :].astype(F32)
        image_out[0, at] = (mask * (resid_in[rows(at), :] + grad))[:canvas]
        return carry

    lax.fori_loop(0, canvas, step, 0, unroll=14)


def block_out_stage(sides, mid_seen, last_seen, scale, offset, x_in, mid_in, last_in, out):
    channels = x_in.shape[1]
    canvas = x_in.shape[0] // ROW
    side = sides[pl.program_id(0)]
    inside = columns_inside(side, channels)
    factor = scale[4:5] * mid_seen[1:2]
    constant = offset[4:5] - mid_seen[0:1] * factor + last_seen[5:6]
    constant = jnp.broadcast_to(constant, (ROW, channels))
    factor = jnp.broadcast_to(factor, (ROW, channels))
    last = jnp.broadcast_to(last_seen[4:5], (ROW, channels))

    def step(at, carry):
        mask = jnp.where(at < side, inside, 0.0)
        added = factor * mid_in[rows(at), :] + last * last_in[rows(at), :] + constant
        out[0, at] = (x_in[rows(at), :].astype(F32) + mask * added)[:canvas].astype(BF16)
        return carry

    lax.fori_loop(0, canvas, step, 0, unroll=14)


def kernel_waves_stage(large, small, large_t, small_t, large_out, small_out, large_rows, small_rows):
    for kernel, table, out, flat in (
        (large, large_t, large_out, large_rows),
        (small, small_t, small_out, small_rows),
    ):
        side = kernel.shape[0]
        row = flat.shape[0] // side
        flat[...] = jnp.zeros_like(flat)
        for at in range(side):
            flat[at * row : at * row + side, :] = kernel[at]
        out[...] = ahead(table, flat[...])


def kernel_grad_stage(
    place, merged, merged_grad, large_sum, small_sum, large_t, small_t, other_out, mine_out, flat, proj_sum
):
    proj_sum[...] = dot_tn(merged[...], merged_grad[...])
    start = 0
    for total, table in ((large_sum, large_t), (small_sum, small_t)):
        size = table[0].shape[0]
        flat[start : start + size, :] = back(table, *halves(total[...]))
        start += size
    if start < flat.shape[0]:
        flat[start:, :] = jnp.zeros((flat.shape[0] - start, flat.shape[1]), F32)
    size, rest = flat.shape[0] // 2, proj_sum.shape[0] // 2
    for out, core in ((mine_out, place[0]), (other_out, 1 - place[0])):
        out[:size, :] = flat[pl.ds(pl.multiple_of(core * size, 8), size), :]
        out[size:, :] = proj_sum[pl.ds(pl.multiple_of(core * rest, 8), rest), :]


def kernel_grad_out_stage(settled, large_out, small_out, proj_out, flat, *, canvas):
    rest = proj_out.shape[0] // 2
    size = settled.shape[0] // 2 - rest
    for core in range(2):
        start = core * (size + rest)
        flat[core * size : (core + 1) * size, :] = settled[start : start + size, :]
        proj_out[core * rest : (core + 1) * rest, :] = settled[start + size : start + size + rest, :]
    start = 0
    for out in (large_out, small_out):
        side = out.shape[0]
        first, count = used_rows(side, canvas)
        out[...] = jnp.zeros_like(out)
        for at in range(first, first + count):
            out[at, first : first + count, :] = flat[start : start + count, :]
            start += count
        start = -(-start // 8) * 8


def weight_grad_stage(place, inputs, gradient, out):
    out[...] = dot_tn(inputs[...], gradient[...])


SMEM = pl.BlockSpec(memory_space=pltpu.SMEM)


def whole(shape):
    return pl.BlockSpec(shape, lambda at: (0,) * len(shape))


VMEM = 36 * 1024 * 1024


def call(kernel, crops, ins, outs, scratch):
    def spec(shape, kind):
        if kind == "smem":
            return SMEM
        if kind == "rows":
            return pl.BlockSpec((shape[0] // crops, shape[1]), lambda at: (at, 0))
        if kind == "map":
            return pl.BlockSpec((1,) + tuple(shape[1:]), lambda at: (at, 0, 0, 0))
        return whole(tuple(shape))

    flat, specs, places = [], [], []
    for value, kind in ins:
        group = value if isinstance(value, tuple) else (value,)
        places.append((len(flat), len(group) if isinstance(value, tuple) else 0))
        for part in group:
            if kind in ("rows", "apart"):
                part = pltpu.with_memory_space_constraint(part, pltpu.HBM)
            flat.append(part)
            specs.append(spec(part.shape, kind))

    def body(*refs):
        given = [refs[at : at + size] if size else refs[at] for at, size in places]
        kernel(*given, *refs[len(flat) :])

    return pl.pallas_call(
        body,
        grid=(crops,),
        in_specs=specs,
        out_specs=[spec(shape, kind) for shape, _, kind in outs],
        out_shape=[
            (pltpu.HBM if kind == "rows" else jax.ShapeDtypeStruct)(shape, dtype) for shape, dtype, kind in outs
        ],
        scratch_shapes=[pltpu.VMEM(shape, dtype) for shape, dtype in scratch],
        compiler_params=pltpu.CompilerParams(
            dimension_semantics=("arbitrary",), vmem_limit_bytes=VMEM
        ),
        cost_estimate=pl.CostEstimate(
            flops=0,
            bytes_accessed=sum(math.prod(part.shape) * part.dtype.itemsize for part in flat)
            + sum(math.prod(shape) * jnp.dtype(dtype).itemsize for shape, dtype, _ in outs),
            transcendentals=0,
        ),
        name=getattr(kernel, "func", kernel).__name__,
    )(*flat)


def weight_grad(inputs, gradient, place=None):
    deep, high = inputs.shape
    wide = gradient.shape[1]
    large = place is None
    if large:
        place = jnp.zeros((1,), jnp.int32)
        inputs = pltpu.with_memory_space_constraint(inputs, pltpu.HBM)
        gradient = pltpu.with_memory_space_constraint(gradient, pltpu.HBM)
    else:
        high = high // 2
    block, across = min(high, 512), min(wide, 512)
    return pl.pallas_call(
        weight_grad_stage,
        grid_spec=pltpu.PrefetchScalarGridSpec(
            num_scalar_prefetch=1,
            grid=(high // block, wide // across),
            in_specs=[
                pl.BlockSpec((deep, block), lambda i, j, place: (0, place[0] * (high // block) + i)),
                pl.BlockSpec((deep, across), lambda i, j, place: (0, j)),
            ],
            out_specs=pl.BlockSpec((block, across), lambda i, j, place: (i, j)),
        ),
        out_shape=pltpu.HBM((high, wide), F32) if large else jax.ShapeDtypeStruct((high, wide), F32),
        compiler_params=pltpu.CompilerParams(
            dimension_semantics=("arbitrary", "arbitrary"), vmem_limit_bytes=VMEM
        ),
        cost_estimate=pl.CostEstimate(
            flops=2 * deep * high * wide,
            bytes_accessed=2 * deep * (high + wide) + 4 * high * wide,
            transcendentals=0,
        ),
        name="weight_grad_stage",
    )(place, inputs, gradient)


def exchange(sent):
    return lax.all_to_all(sent, AXES, 0, 0, tiled=True)


SWAP = [(0, 1), (1, 0)]


def wide_exchange(mine, other, *beside):
    mine = mine + lax.ppermute(other, "core", SWAP)
    chips = lax.axis_size(("node", "chip"))
    copies = jnp.broadcast_to(mine[None], (chips,) + mine.shape)
    mine = jnp.sum(together(lax.all_to_all(copies, ("node", "chip"), 0, 0, tiled=True), *beside), axis=0)
    return mine, lax.ppermute(mine, "core", SWAP)


def sum_and_cut(arrays, place, ways):
    count, wide = arrays[0].shape
    part = count // ways

    def body(place, *refs):
        total = refs[0][...]
        for ref in refs[1 : len(arrays)]:
            total = total + ref[...]
        for at, out in enumerate(refs[len(arrays) :]):

            @pl.when(pl.program_id(0) == at)
            def _():
                out[...] = total

    return pl.pallas_call(
        body,
        grid_spec=pltpu.PrefetchScalarGridSpec(
            num_scalar_prefetch=1,
            grid=(ways,),
            in_specs=[pl.BlockSpec((part, wide), lambda at, place: (place[0] ^ at, 0))] * len(arrays),
            out_specs=[pl.BlockSpec((part, wide), lambda at, place: (0, 0))] * ways,
        ),
        out_shape=[jax.ShapeDtypeStruct((part, wide), F32)] * ways,
        compiler_params=pltpu.CompilerParams(dimension_semantics=("arbitrary",), vmem_limit_bytes=VMEM),
        cost_estimate=pl.CostEstimate(
            flops=0, bytes_accessed=4 * count * wide * (len(arrays) + 1), transcendentals=0
        ),
        name="sum_and_cut",
    )(place, *arrays)


def join(parts, place):
    part, wide = parts[0].shape
    ways = len(parts)

    def body(place, *refs):
        for at, ref in enumerate(refs[:ways]):

            @pl.when(pl.program_id(0) == at)
            def _():
                refs[ways][...] = ref[...]

    return pl.pallas_call(
        body,
        grid_spec=pltpu.PrefetchScalarGridSpec(
            num_scalar_prefetch=1,
            grid=(ways,),
            in_specs=[pl.BlockSpec((part, wide), lambda at, place: (0, 0))] * ways,
            out_specs=pl.BlockSpec((part, wide), lambda at, place: (place[0] ^ at, 0)),
        ),
        out_shape=jax.ShapeDtypeStruct((ways * part, wide), F32),
        compiler_params=pltpu.CompilerParams(dimension_semantics=("arbitrary",), vmem_limit_bytes=VMEM),
        cost_estimate=pl.CostEstimate(flops=0, bytes_accessed=8 * ways * part * wide, transcendentals=0),
        name="join",
    )(place, *parts)


def place_on(axis):
    return lax.axis_index(axis)[None]


def across(parts, axis):
    size = lax.axis_size(axis)
    return [
        lax.ppermute(part, axis, [(at, at ^ k) for at in range(size)]) if k else part
        for k, part in enumerate(parts)
    ]


class Settle:
    def __init__(self, other, mine, steps):
        half = mine.shape[0]
        self.first = mine
        if half % (8 * lax.axis_size(("node", "chip"))):
            first = lax.axis_index("core") == 0
            both = jnp.where(first, jnp.concatenate([mine, other]), jnp.concatenate([other, mine]))
            self.value = lax.psum(both, AXES)
            self.steps = []
        else:
            self.parts = [mine, lax.ppermute(other, "core", SWAP)]
            self.steps = list(steps)

    def chip(self):
        self.cut("chip")

    def node(self):
        self.cut("node")

    def cut(self, axis):
        self.parts = sum_and_cut(self.parts, place_on(axis), lax.axis_size(axis))
        self.mark = self.parts[0]
        self.parts = across(self.parts, axis)

    def piece(self):
        (self.mark,) = sum_and_cut(self.parts, place_on("node") * 0, 1)
        self.parts = across([self.mark] * lax.axis_size("node"), "node")

    def gather(self):
        (self.mark,) = sum_and_cut(self.parts, place_on("node") * 0, 1)
        self.value = lax.all_gather(self.mark, ("core", "chip", "node"), axis=0, tiled=True)

    def to_chip(self):
        self.join("node", "chip")

    def to_core(self):
        self.join("chip", "core")

    def end(self):
        self.value = self.mark = join(self.parts, place_on("core"))

    def join(self, axis, onward):
        self.mark = join(self.parts, place_on(axis))
        self.parts = across([self.mark] * lax.axis_size(onward), onward)

    def step(self, token):
        if not self.steps:
            return token
        self.parts, token = lax.optimization_barrier((self.parts, token))
        getattr(self, self.steps.pop(0))()
        return self.mark


BY_PERMUTES = ("chip", "node", "piece", "to_chip", "to_core", "end")
BY_GATHER = ("chip", "node", "gather")


def settle_weight_grad(inputs, gradient, steps):
    core = place_on("core")
    other = weight_grad(inputs, gradient, 1 - core)
    gradient, other = lax.optimization_barrier((gradient, other))
    mine = weight_grad(inputs, gradient, core)
    return Settle(other, mine, steps)


def turned(token, *weights):
    return [weight.T for weight in lax.optimization_barrier((weights, token))[0]]


def together(value, *tokens):
    return lax.optimization_barrier((value, tokens))[0]


def local(
    image, crop_sides, proj_in, kernel_large, kernel_small, proj_out, proj_up, proj_down,
    norm_gain, norm_shift, wide_gain, wide_shift, cotangent,
):
    crops, canvas, _, channels = image.shape
    wide = proj_up.shape[1]
    devices = lax.axis_size(AXES)
    cells = crops * canvas * ROW
    tables = wave_tables(canvas, kernel_large.shape[0], kernel_small.shape[0])
    half = tables["half"]

    def const(name):
        return tuple(jnp.asarray(part) for part in tables[name])

    ahead_t, back_t = const("ahead"), const("back")
    sides = (crop_sides, "smem")
    scale, offset = (norm_gain, "apart"), (norm_shift, "apart")
    wide_scale, wide_offset = (wide_gain[None], "apart"), (wide_shift[None], "apart")
    full, full_low = ((cells, channels), F32, "rows"), ((cells, channels), BF16, "rows")
    wide_low = ((cells, wide), BF16, "rows")
    wide_half = ((wide // 128, 128), F32, "whole")
    core = (place_on("core"), "smem")
    seen_out, wide_seen_out = ((8, channels), F32, "whole"), ((8, wide), F32, "whole")

    def send(count):
        return ((devices, -(-count // 1024) * 8, 128), F32, "whole")

    def coefs(count, width=channels):
        return ((count, 8, width), F32)

    def run(kernel, ins, outs, scratch):
        return call(kernel, crops, ins, outs, scratch)

    def r(value):
        return (value, "rows")

    def w(value):
        return (value, "whole")

    def apart(value):
        return (value, "apart")

    x, u, sent = run(
        enter_stage,
        [sides, (image, "map"), (cotangent, "map")],
        [full_low, full_low, send(2 * channels + 128)],
        [((2, canvas * ROW, channels), F32), coefs(2)],
    )
    came = exchange(sent)
    spectrum_out = ((2 * half, channels), F32, "whole")
    large_w, small_w = call(
        kernel_waves_stage,
        1,
        [apart(kernel_large), apart(kernel_small), apart(const("large")), apart(const("small"))],
        [spectrum_out, spectrum_out],
        [
            ((tables["large"][0].shape[1], channels), BF16),
            ((tables["small"][0].shape[1], channels), BF16),
        ],
    )
    came = together(came, large_w, small_w)
    pre_low, pre, sent, seen = run(
        first_stage,
        [sides, w(came), scale, offset, r(x), apart(proj_in)],
        [full_low, full, send(2 * channels), seen_out],
        [coefs(2), coefs(2)],
    )
    spectrum = ((2 * half, channels), F32)
    spectrum_low = ((2 * half, channels), BF16)
    down_t, out_t = turned(sent, proj_down, proj_out)
    came = together(exchange(sent), down_t, out_t)
    mixer_low, large, small, mixer_waves, sent, first_seen = run(
        mixer_stage,
        [sides, w(came), w(seen), scale, offset, r(pre), apart(ahead_t), apart(back_t), apart(large_w), apart(small_w)],
        [full_low, full, full, ((crops * 2 * half, channels), BF16, "rows"), send(4 * channels), seen_out],
        [coefs(2), coefs(4), spectrum, spectrum_low],
    )
    up_t, in_t = turned(sent, proj_up, proj_in)
    came = together(exchange(sent), up_t, in_t)
    merged_low, proj, sent, merge_seen = run(
        merge_stage,
        [sides, w(came), w(seen), scale, offset, r(large), r(small), r(x), r(u), apart(proj_out)],
        [full_low, full, send(4 * channels), seen_out],
        [coefs(3), coefs(4)],
    )
    ffn_low, hidden, mine, other, mid_seen = run(
        widen_stage,
        [sides, core, w(exchange(sent)), w(seen), scale, offset, r(x), r(proj), apart(proj_up)],
        [full_low, wide_low, wide_half, wide_half, seen_out],
        [coefs(3), coefs(2, wide), ((canvas * ROW, channels), F32)],
    )
    hidden_low, hidden_slope, last, sent, wide_seen = run(
        narrow_stage,
        [sides, core, w(wide_exchange(mine, other)), w(seen), wide_scale, wide_offset, r(hidden), r(u), apart(proj_down)],
        [wide_low, wide_low, full, send(4 * channels), wide_seen_out],
        [coefs(2, wide), coefs(4)],
    )
    down_low, hidden_grad, mine, other, last_seen = run(
        wide_back_stage,
        [
            sides, core, w(exchange(sent)), w(seen), scale, offset,
            r(last), r(u), r(hidden), r(hidden_slope), apart(down_t),
        ],
        [full_low, wide_low, wide_half, wide_half, seen_out],
        [coefs(3), coefs(2, wide), ((canvas * ROW, channels), F32)],
    )
    grad_down = weight_grad(hidden_low, down_low)
    came = wide_exchange(mine, other, grad_down)
    up_low, ffn_grad, sent, wide_noted = run(
        narrow_back_stage,
        [sides, core, w(came), w(wide_seen), wide_scale, r(hidden_grad), r(hidden), r(x), r(proj), apart(up_t)],
        [wide_low, full, send(3 * channels), wide_seen_out],
        [coefs(3, wide), coefs(3)],
    )
    came = exchange(sent)
    grad_up = weight_grad(ffn_low, up_low)
    came = together(came, grad_up)
    grad_down, grad_up = lax.psum((grad_down, grad_up), AXES)
    resid_grad, back_low, merged_grad, sent, mid_noted = run(
        mid_back_stage,
        [
            sides, w(came), w(seen), w(merge_seen), w(mid_seen), w(last_seen), scale, offset,
            r(x), r(u), r(proj), r(ffn_grad), r(large), r(small), apart(out_t),
        ],
        [full, full_low, full, send(3 * channels), seen_out],
        [coefs(7), coefs(3)],
    )
    came = exchange(sent)
    mixer_grad, large_sum, small_sum, sent, mixer_noted = run(
        mixer_back_stage,
        [
            sides, w(came), w(seen), w(merge_seen), w(first_seen), scale, offset,
            r(large), r(small), r(merged_grad), r(pre), r(mixer_waves), apart(ahead_t), apart(back_t), apart(large_w), apart(small_w),
        ],
        [full, spectrum_out, spectrum_out, send(2 * channels), seen_out],
        [
            coefs(6), coefs(2), ((canvas * ROW, channels), BF16), ((canvas * ROW, channels), BF16),
            spectrum, spectrum, spectrum_low,
        ],
    )
    came = exchange(sent)
    taps_t = (const("large_back"), const("small_back"))
    tap_rows = sum(table[0].shape[0] for table in taps_t)
    tap_rows = -(-tap_rows // (8 * devices)) * 8 * devices
    half_taps = (((tap_rows + channels) // 2, channels), F32, "whole")
    other, mine = call(
        kernel_grad_stage,
        1,
        [core, w(merged_low), w(back_low), w(large_sum), w(small_sum), apart(taps_t[0]), apart(taps_t[1])],
        [half_taps, half_taps],
        [((tap_rows, channels), F32), ((channels, channels), F32)],
    )
    came = together(came, other, mine)
    settle_taps = Settle(other, mine, BY_PERMUTES)
    pre_round, first_grad, sent, first_noted = run(
        first_back_stage,
        [sides, w(came), w(seen), w(first_seen), scale, r(mixer_grad), r(pre), r(x), apart(in_t)],
        [full_low, full, send(2 * channels), seen_out],
        [coefs(3), coefs(2)],
    )
    settle_in = settle_weight_grad(pre_low, pre_round, BY_PERMUTES)
    came = exchange(together(sent, settle_in.first))
    token = settle_in.step(settle_taps.step(settle_in.first))
    (block_out,) = run(
        block_out_stage,
        [sides, w(mid_seen), w(last_seen), scale, offset, r(x), r(proj), r(together(last, token))],
        [(image.shape, BF16, "map")],
        [],
    )
    token = settle_in.step(settle_taps.step(block_out))
    came = together(came, token)
    grad_image, enter_noted = run(
        leave_stage,
        [sides, w(came), w(seen), scale, r(resid_grad), r(first_grad), r(x)],
        [(image.shape, F32, "map"), seen_out],
        [coefs(3)],
    )
    token = grad_image
    while settle_in.steps or settle_taps.steps:
        token = settle_in.step(settle_taps.step(token))
    grad_in = settle_in.value
    grad_large, grad_small, grad_out = call(
        functools.partial(kernel_grad_out_stage, canvas=canvas),
        1,
        [w(settle_taps.value)],
        [(kernel_large.shape, F32, "whole"), (kernel_small.shape, F32, "whole"), (proj_out.shape, F32, "whole")],
        [((tap_rows, channels), F32)],
    )
    gain_grads = jnp.stack(
        [enter_noted[0], first_noted[0], mixer_noted[0], mixer_noted[1], mid_noted[2], mid_noted[0], last_seen[3]]
    )
    shift_grads = jnp.stack(
        [enter_noted[1], first_noted[1], mixer_noted[2], mixer_noted[2], mid_noted[3], mid_noted[1], last_seen[2]]
    )
    return (
        block_out, grad_image, grad_in, grad_large, grad_small, grad_out, grad_up, grad_down,
        gain_grads, shift_grads, wide_noted[0], wide_noted[1],
    )


def solution(mesh):
    nodes, devices = mesh.devices.shape
    chips = jax.sharding.Mesh(mesh.devices.reshape(nodes, devices // 2, 2), AXES)
    maps = P(AXES, None, None, None)
    return jax.shard_map(
        local,
        mesh=chips,
        in_specs=(maps, P(AXES)) + (P(),) * 10 + (maps,),
        out_specs=(maps, maps) + (P(),) * 10,
        check_vma=False,
    )
```
